32 devices in a mesh: dp: 8 (over z, x), tp: 4 (over y, core).
Axes of the slice: x: 2, y: 2, z: 4, core: 2. Of those that a mesh axis runs over, the one named last changes fastest.
Arguments:
- layer_input: bfloat16 [8, 2048, 768], P('dp', 'tp'), may hold values from -6 to 6
- norm_gain: float32 [3, 768], replicated, may hold values from 0.5 to 1.5
- norm_bias: float32 [3, 768], replicated, may hold values from -3 to 3
- self_input_weight: bfloat16 [768, 3, 768], P(None, None, 'tp'), may hold values from -0.21875 to 0.21875
- self_input_bias: float32 [3, 768], P(None, 'tp'), may hold values from -2 to 2
- self_output_weight: bfloat16 [768, 768], P('tp'), may hold values from -0.875 to 0.875
- out_bias: float32 [3, 768], replicated, may hold values from -2 to 2
- cross_query_weight: bfloat16 [768, 768], P(None, 'tp'), may hold values from -0.21875 to 0.21875
- b_cross_q: float32 [768], P('tp'), may hold values from -2 to 2
- w_cross_kv: bfloat16 [768, 2, 768], P(None, None, 'tp'), may hold values from -0.21875 to 0.21875
- b_cross_v: float32 [768], P('tp'), may hold values from -2 to 2
- cross_output_weight: bfloat16 [768, 768], P('tp'), may hold values from -0.875 to 0.875
- expand_weight_1: bfloat16 [768, 3072], P(None, 'tp'), may hold values from -0.21875 to 0.21875
- expand_bias_1: float32 [3072], P('tp'), may hold values from -3 to 3
- contract_weight_2: bfloat16 [3072, 768], P('tp'), may hold values from -0.109375 to 0.109375
- neighbours: bfloat16 [8, 64, 128, 768], P('dp', 'tp'), may hold values from -6 to 6
- segment_ids: int32 [8, 2048], P('dp'), may hold values from 0 to 4, as said below
- span_map: int32 [8, 64], P('dp'), may hold values from 0 to 63, each once within a row
- cotangent: float32 [8, 2048, 768], P('dp', 'tp'), may hold values from -6 to 6
Outputs:
- layer_output: float32 [8, 2048, 768], P('dp', 'tp')
- grad_input: float32 [8, 2048, 768], P('dp', 'tp')
- grad_neighbours: float32 [8, 64, 128, 768], P('dp', 'tp')
- grad_norm_gain: float32 [3, 768], replicated
- grad_norm_bias: float32 [3, 768], replicated
- grad_w_qkv: float32 [768, 3, 768], P(None, None, 'tp')
- grad_b_qkv: float32 [3, 768], P(None, 'tp')
- grad_w_attn_out: float32 [768, 768], P('tp')
- grad_out_bias: float32 [3, 768], replicated
- grad_w_cross_q: float32 [768, 768], P(None, 'tp')
- grad_b_cross_q: float32 [768], P('tp')
- grad_w_cross_kv: float32 [768, 2, 768], P(None, None, 'tp')
- grad_b_cross_v: float32 [768], P('tp')
- grad_w_cross_out: float32 [768, 768], P('tp')
- expand_weight_gradient_1: float32 [768, 3072], P(None, 'tp')
- grad_b_fc1: float32 [3072], P('tp')
- contract_weight_gradient_2: float32 [3072, 768], P('tp')
The draws below stay inside these ranges and needn't reach their ends.
Inputs may be any that keep to these rules, and one draw needn't show every extreme that they name: `segment_ids`: ids never fall along a row, start at 0 in every row and rise by one at each new document; every row holds five documents. `span_map`: each row is a permutation of 0 to 63.
All inputs are finite; a program needn't handle non-finite values.
Results may differ from the reference program's by a relative error of at most 0.029.
Values may be sent and summed in bfloat16 or wider, within the bound.
No kernel may reach another device: no remote copies, remote signals or barrier semaphores. Data moves between devices by JAX's collectives and lax.ppermute only.
A program may use at most 256 MiB of HBM per device.

```python
import math
import jax
import jax.numpy as jnp
from jax import lax

D = 768
HEADS = 12
HEAD_DIM = 64
FF = 3072
LEN = 2048
SPAN = 64
NEIGH = 2
NLEN = 128
QBLOCK = 512
ROWS = 8
POOL = 64


def draw_segment_ids(key, part):
    key = jax.random.fold_in(key, 7)
    key_first, key_last, key_head, key_tail = jax.random.split(key, 4)
    first_pos = jax.random.randint(key_first, (ROWS, 1), 2, LEN // 4)
    last_pos = jax.random.randint(key_last, (ROWS, 1), 3 * LEN // 4, LEN - 2)
    head_cut = jax.random.randint(key_head, (ROWS, 1), 1, first_pos)
    tail_cut = jax.random.randint(key_tail, (ROWS, 1), last_pos + 2, LEN)
    positions = jnp.arange(LEN, dtype=jnp.int32)[None, :]
    new_doc = (positions == head_cut) | (positions == first_pos) | (positions == last_pos + 1) | (positions == tail_cut)
    return jnp.cumsum(new_doc.astype(jnp.int32), axis=1).astype(jnp.int32)


def shard_levels(rng, extent, cuts, low, top_value):
    factor_of, own = 1.0, jax.random.fold_in(rng, 6)
    for position, parts in cuts:
        draws = jnp.exp(jax.random.uniform(jax.random.fold_in(own, position), (parts,), jnp.float32, low / len(cuts), top_value / len(cuts)))
        factor_of = factor_of * jnp.repeat(draws, extent[position] // parts).reshape([-1 if axis == position else 1 for axis in range(len(extent))])
    return factor_of


def gaussian(key, shape, spread, reach, shards=(), held_as=jnp.bfloat16):
    array = jax.random.normal(key, shape, jnp.float32) * spread
    if len(shards) > 0:
        array = shard_levels(key, shape, shards, -0.22, 0.18) * array
    return jnp.clip(array, min=-reach, max=reach).astype(held_as)


def setup_inputs(seed: int = 0) -> dict:
    key_list = jax.random.split(jax.random.key(seed), 20)
    return {
        "layer_input": gaussian(key_list[0], (ROWS, LEN, D), 1.0, 6.0, ((0, 8), (1, 4))),
        "norm_gain": jnp.clip(1.0 + 0.1 * jax.random.normal(key_list[1], (3, D), jnp.float32), 0.5, 1.5),
        "norm_bias": gaussian(key_list[2], (3, D), 0.5, 3.0, (), jnp.float32),
        "self_input_weight": gaussian(key_list[3], (D, 3, D), D ** -0.5, 0.21875, ((2, 4),)),
        "self_input_bias": gaussian(key_list[4], (3, D), 0.3, 2.0, ((1, 4),), jnp.float32),
        "self_output_weight": gaussian(key_list[5], (D, D), (D // 16) ** -0.5, 0.875, ((0, 4),)),
        "out_bias": gaussian(key_list[6], (3, D), 0.3, 2.0, (), jnp.float32),
        "cross_query_weight": gaussian(key_list[7], (D, D), D ** -0.5, 0.21875, ((1, 4),)),
        "b_cross_q": gaussian(key_list[8], (D,), 0.3, 2.0, ((0, 4),), jnp.float32),
        "w_cross_kv": gaussian(key_list[9], (D, 2, D), D ** -0.5, 0.21875, ((2, 4),)),
        "b_cross_v": gaussian(key_list[10], (D,), 0.3, 2.0, ((0, 4),), jnp.float32),
        "cross_output_weight": gaussian(key_list[11], (D, D), (D // 16) ** -0.5, 0.875, ((0, 4),)),
        "expand_weight_1": gaussian(key_list[12], (D, FF), D ** -0.5, 0.21875, ((1, 4),)),
        "expand_bias_1": gaussian(key_list[13], (FF,), 0.5, 3.0, ((0, 4),), jnp.float32),
        "contract_weight_2": gaussian(key_list[14], (FF, D), FF ** -0.5, 0.109375, ((0, 4),)),
        "neighbours": gaussian(key_list[15], (ROWS, POOL, NLEN, D), 1.0, 6.0, ((0, 8), (1, 4))),
        "segment_ids": draw_segment_ids(jax.random.fold_in(key_list[19], 71), 0),
        "span_map": jax.vmap(lambda own: jax.random.permutation(own, POOL))(jax.random.split(key_list[17], ROWS)).reshape((ROWS, POOL)).astype(jnp.int32),
        "cotangent": gaussian(key_list[18], (ROWS, LEN, D), 1.0, 6.0, ((0, 8), (1, 4)), jnp.float32),
    }


PRECISE = lax.Precision.HIGHEST
NEGATIVE = -1e+30
NORM_EPS = 1e-05

@jax.custom_vjp
def low(v):
    return lax.optimization_barrier(v.astype(jnp.bfloat16)).astype(jnp.float32)

@jax.custom_vjp
def low_back(v):
    return v

def low_keep(v):
    return (low(v), None)

def low_pass(kept, grad):
    return (grad,)

def back_keep(v):
    return (v, None)

def back_low(kept, grad):
    return (low(grad),)
low.defvjp(low_keep, low_pass)
low_back.defvjp(back_keep, back_low)

def layer_norm(values, norm_scale, norm_shift):
    centre = values - lax.optimization_barrier(jnp.mean(values, -1, keepdims=True))
    variance = lax.optimization_barrier(jnp.mean(centre * centre, -1, keepdims=True))
    return centre * lax.rsqrt(variance + NORM_EPS) * norm_scale + norm_shift

def rotary_tables(full_length, head_width):
    halfway = head_width // 2
    frequency = 10000.0 ** (-jnp.arange(halfway, dtype=jnp.float32) / halfway)
    angles = jnp.arange(full_length, dtype=jnp.float32)[:, None] * frequency[None, :]
    cosine = jnp.concatenate([jnp.cos(angles), jnp.cos(angles)], -1)[:, None, :]
    sine_table = jnp.concatenate([jnp.sin(angles), jnp.sin(angles)], -1)[:, None, :]
    return (cosine, sine_table)

def rotate(values, cosine, sine_table):
    halfway = values.shape[-1] // 2
    turned = jnp.concatenate([-values[..., halfway:], values[..., :halfway]], -1)
    return values * cosine + turned * sine_table

def forward(param_set, inputs, memory, segments, pick_rows):
    norm_gain, norm_bias, self_input_weight, self_input_bias, self_output_weight, out_bias, cross_query_weight, b_cross_q, w_cross_kv, b_cross_v, cross_output_weight, expand_weight_1, expand_bias_1, contract_weight_2 = param_set
    full_length = inputs.shape[0]
    span_count = full_length // SPAN
    cosine, sine_table = rotary_tables(full_length, HEAD_DIM)
    scale_q = 1.0 / math.sqrt(HEAD_DIM)
    normalized_first = low(layer_norm(inputs, norm_gain[0], norm_bias[0]))
    project = low_back(jnp.einsum('ld,dte->lte', normalized_first, self_input_weight, precision=PRECISE) + self_input_bias)
    shaped = project.reshape(full_length, 3, HEADS, HEAD_DIM)
    query = low(rotate(shaped[:, 0], cosine, sine_table) * scale_q)
    keys_all = low(rotate(shaped[:, 1], cosine, sine_table))
    values_all = low(shaped[:, 2])

    def block_attend(row_start):
        query_block = lax.dynamic_slice_in_dim(query, row_start, QBLOCK, 0)
        scores = jnp.einsum('bhe,khe->hbk', query_block, keys_all, precision=PRECISE)
        row_ids = row_start + lax.iota(jnp.int32, QBLOCK)
        columns = lax.iota(jnp.int32, full_length)
        row_segment = lax.dynamic_slice_in_dim(segments, row_start, QBLOCK, 0)
        allowed = (columns[None, :] <= row_ids[:, None]) & (row_segment[:, None] == segments[None, :])
        scores = low_back(jnp.where(allowed[None], scores, NEGATIVE))
        maxima = lax.optimization_barrier(jnp.max(scores, -1, keepdims=True))
        shifted = jnp.exp(scores - maxima)
        attn_prob = shifted / lax.optimization_barrier(jnp.sum(shifted, -1, keepdims=True))
        return jnp.einsum('hbk,khe->bhe', low(attn_prob), values_all, precision=PRECISE)
    block_starts = jnp.arange(full_length // QBLOCK, dtype=jnp.int32) * QBLOCK
    mixed_heads = lax.map(jax.checkpoint(block_attend), block_starts).reshape(full_length, D)
    attended = low(low_back(mixed_heads))
    after_self = inputs + low_back(jnp.dot(attended, self_output_weight, precision=PRECISE)) + out_bias[0]
    normalized_second = low(layer_norm(after_self, norm_gain[1], norm_bias[1]))
    cross_query = low(low_back(jnp.dot(normalized_second, cross_query_weight, precision=PRECISE) + b_cross_q) * scale_q)
    cross_query = cross_query.reshape(span_count, SPAN, HEADS, HEAD_DIM)
    kv_bias = jnp.stack([jnp.zeros_like(b_cross_v), b_cross_v])
    memory_kv = low(low_back(jnp.einsum('pnd,dte->pnte', memory, w_cross_kv, precision=PRECISE) + kv_bias))
    chosen = memory_kv[pick_rows].reshape(span_count, NEIGH * NLEN, 2, HEADS, HEAD_DIM)
    cross_scores = low_back(jnp.einsum('cqhe,ckhe->chqk', cross_query, chosen[:, :, 0], precision=PRECISE))
    cross_max = lax.optimization_barrier(jnp.max(cross_scores, -1, keepdims=True))
    cross_exp = jnp.exp(cross_scores - cross_max)
    cross_prob = cross_exp / lax.optimization_barrier(jnp.sum(cross_exp, -1, keepdims=True))
    cross_mixed = jnp.einsum('chqk,ckhe->cqhe', low(cross_prob), chosen[:, :, 1], precision=PRECISE)
    cross_vals = low(low_back(cross_mixed.reshape(full_length, D)))
    after_cross = after_self + low_back(jnp.dot(cross_vals, cross_output_weight, precision=PRECISE)) + out_bias[1]
    normalized_middle = low(layer_norm(after_cross, norm_gain[2], norm_bias[2]))
    before_gelu = low_back(jnp.dot(normalized_middle, expand_weight_1, precision=PRECISE) + expand_bias_1)
    hidden = low(jax.nn.gelu(before_gelu))
    return after_cross + low_back(jnp.dot(hidden, contract_weight_2, precision=PRECISE)) + out_bias[2]

def reference(layer_input, norm_gain, norm_bias, self_input_weight, self_input_bias, self_output_weight, out_bias, cross_query_weight, b_cross_q, w_cross_kv, b_cross_v, cross_output_weight, expand_weight_1, expand_bias_1, contract_weight_2, neighbours, segment_ids, span_map, cotangent):
    param_set = (norm_gain.astype(jnp.float32), norm_bias.astype(jnp.float32), self_input_weight.astype(jnp.float32), self_input_bias.astype(jnp.float32), self_output_weight.astype(jnp.float32), out_bias.astype(jnp.float32), cross_query_weight.astype(jnp.float32), b_cross_q.astype(jnp.float32), w_cross_kv.astype(jnp.float32), b_cross_v.astype(jnp.float32), cross_output_weight.astype(jnp.float32), expand_weight_1.astype(jnp.float32), expand_bias_1.astype(jnp.float32), contract_weight_2.astype(jnp.float32))

    def one_sequence(totals, seq_items):
        inputs, memory, segments, pick_rows, seq_cot = seq_items

        def apply_layer(param_list, input_vals, memory_vals):
            return forward(param_list, input_vals, memory_vals, segments, pick_rows)
        outputs, pull_back = jax.vjp(apply_layer, param_set, inputs.astype(jnp.float32), memory.astype(jnp.float32))
        grad_params, grad_inputs, grad_memory = pull_back(seq_cot.astype(jnp.float32))
        totals = jax.tree.map(lambda running, adding: running + adding, totals, grad_params)
        return (totals, (outputs, grad_inputs, grad_memory))
    start_totals = jax.tree.map(jnp.zeros_like, param_set)
    totals, (layer_output, grad_input, grad_neighbours) = lax.scan(one_sequence, start_totals, (layer_input, neighbours, segment_ids, span_map, cotangent))
    return (layer_output, grad_input, grad_neighbours, totals[0], totals[1], totals[2], totals[3], totals[4], totals[5], totals[6], totals[7], totals[8], totals[9], totals[10], totals[11], totals[12], totals[13])
```

```python
import functools
import math

import jax
import jax.numpy as jnp
from jax import lax
from jax.experimental import pallas as pl
from jax.experimental.pallas import tpu as pltpu
from jax.sharding import PartitionSpec as P

HEAD_DIM = 64
SPAN = 64
LANES = 128
QUERY_ROWS = 256
NEGATIVE = -1e30
NORM_EPS = 1e-05
BF = jnp.bfloat16
F32 = jnp.float32
VMEM_BYTES = 56 * 1024 * 1024

DOCS = 5
MASK_LANE = HEAD_DIM
LSE_LANE = HEAD_DIM + DOCS


def nn(a, b):
    return lax.dot_general(a, b, (((1,), (0,)), ((), ())), preferred_element_type=F32)


def nt(a, b):
    return lax.dot_general(a, b, (((1,), (1,)), ((), ())), preferred_element_type=F32)


def tn(a, b):
    return lax.dot_general(a, b, (((0,), (0,)), ((), ())), preferred_element_type=F32)


def call(body, name, grid, in_specs, out_specs, out_shape, args, scratch=(), prefetch=0, flops=0):
    moved = sum(a.size * a.dtype.itemsize for a in args)
    moved += sum(math.prod(o.shape) * jnp.dtype(o.dtype).itemsize for o in jax.tree.leaves(out_shape))
    return pl.pallas_call(
        body,
        out_shape=out_shape,
        grid_spec=pltpu.PrefetchScalarGridSpec(
            num_scalar_prefetch=prefetch,
            grid=grid,
            in_specs=in_specs,
            out_specs=out_specs,
            scratch_shapes=list(scratch),
        ),
        compiler_params=pltpu.CompilerParams(
            vmem_limit_bytes=VMEM_BYTES, dimension_semantics=("arbitrary",) * len(grid)
        ),
        cost_estimate=pl.CostEstimate(flops=int(flops), bytes_accessed=int(moved), transcendentals=0),
        name=name,
    )(*args)


def whole(array):
    zeros = (0,) * array.ndim
    return pl.BlockSpec(array.shape, lambda *_: zeros)


def rows_of(tile, width):
    return pl.BlockSpec((tile, width), lambda i, *_: (i, 0))


def shape_of(shape, dtype):
    return jax.ShapeDtypeStruct(shape, dtype)


def standardize(values):
    centre = values - jnp.mean(values, -1, keepdims=True)
    inverse = lax.rsqrt(jnp.mean(centre * centre, -1, keepdims=True) + NORM_EPS)
    return centre * inverse, inverse


def norm_pull(grad, normed, inverse, gain):
    scaled = grad * gain
    return inverse * (
        scaled
        - jnp.mean(scaled, -1, keepdims=True)
        - normed * jnp.mean(scaled * normed, -1, keepdims=True)
    )


def column_sum(values):
    return jnp.sum(values, 0, keepdims=True)


def add_rows(out_ref, rows):
    @pl.when(pl.program_id(0) == 0)
    def _():
        out_ref[...] = jnp.zeros_like(out_ref)

    for index, row in enumerate(rows):
        out_ref[index : index + 1, :] += row


def spread(values, partners):
    core, chip, _ = partners
    across = lax.ppermute(values, "tp", chip)
    beside = lax.ppermute(values, "tp", core)
    return [values, beside, across, lax.ppermute(across, "tp", core)]


def collect(parts, partners):
    core, chip, _ = partners
    far = lax.ppermute(parts[3], "tp", core)
    near = lax.ppermute(parts[1], "tp", core)
    sent = (parts[2].astype(F32) + far.astype(F32)).astype(BF)
    across = lax.ppermute(sent, "tp", chip)
    return (parts[0].astype(F32) + near.astype(F32)).astype(BF), across


def exchange(parts, partners):
    return [parts[0]] + [lax.ppermute(parts[r], "tp", partners[r - 1]) for r in (1, 2, 3)]


def qkv_body(t_ref, x_ref, gain_ref, shift_ref, w_ref, b_ref, cos_ref, sa_ref, sb_ref, a_ref, out_ref):
    heads = out_ref.shape[1]
    normed, _ = standardize(x_ref[...].astype(F32))
    a = (normed * gain_ref[0:1, :] + shift_ref[0:1, :]).astype(BF)
    a_ref[...] = a
    proj = nn(a, w_ref[...]) + b_ref[...]
    cos, sa, sb = cos_ref[...], sa_ref[...], sb_ref[...]
    for j in range(3 * heads):
        part = proj[:, j * LANES : (j + 1) * LANES]
        if j < 2 * heads:
            part = part * cos + pltpu.roll(part, 96, 1) * sa + pltpu.roll(part, 32, 1) * sb
        if j < heads:
            part = part * (1.0 / math.sqrt(HEAD_DIM))
        out_ref[j // heads, j % heads] = part.astype(BF)


def project_rows(rel, t, x, gain, shift, w, b, tables, heads):
    rows, width = x.shape
    tile = min(256, rows)
    steps = rows // tile
    table = pl.BlockSpec((tile, LANES), lambda i, t_ref: ((t_ref[0] ^ rel) * steps + i, 0))
    return call(
        qkv_body,
        f"qkv_{rel}",
        (steps,),
        [rows_of(tile, width), whole(gain), whole(shift), whole(w), whole(b), table, table, table],
        [rows_of(tile, width), pl.BlockSpec((3, heads, tile, LANES), lambda i, t_ref: (0, 0, i, 0))],
        [shape_of((rows, width), BF), shape_of((3, heads, rows, LANES), BF)],
        (t, x, gain, shift, w, b, *tables),
        prefetch=1,
        flops=2 * rows * width * w.shape[1],
    )


def causal_corner(scores):
    keys = lax.broadcasted_iota(jnp.int32, scores.shape, 0)
    queries = lax.broadcasted_iota(jnp.int32, scores.shape, 1)
    return jnp.where(keys <= queries, scores, NEGATIVE)


def attend_body(t_ref, c0, c1, c2, c3, qx_ref, kx_ref, vx_ref, qe_ref, ke_ref, ve_ref, ot_ref, lse_ref, vt_ref):
    t = t_ref[0]
    rows = c0.shape[2]
    for rel, chunk in enumerate((c0, c1, c2, c3)):
        place = pl.ds(pl.multiple_of((t ^ rel) * rows, rows), rows)
        qe_ref[0, place, :] = chunk[0, 0] + qx_ref[place, :]
        ke_ref[0, place, :] = chunk[1, 0] + kx_ref[place, :]
        values = chunk[2, 0] + vx_ref[...]
        ve_ref[0, place, :] = values
        vt_ref[:, place] = values.astype(F32).T.astype(BF)
    step = QUERY_ROWS
    for low in range(0, qe_ref.shape[1], step):
        high = low + step
        query = qe_ref[0, low:high, :]
        corner = causal_corner(nt(ke_ref[0, low:high, :], query))
        top = jnp.max(corner, 0, keepdims=True)
        if low:
            earlier = nt(ke_ref[0, :low, :], query)
            top = jnp.maximum(top, jnp.max(earlier, 0, keepdims=True))
        mixed = nn(vt_ref[:, low:high], jnp.exp(corner - top).astype(BF))
        if low:
            mixed = mixed + nn(vt_ref[:, :low], jnp.exp(earlier - top).astype(BF))
        total = mixed[HEAD_DIM : HEAD_DIM + 1, :]
        lse_ref[0, :, low:high] = top + jnp.log(total)
        begin = low % rows
        ot_ref[t ^ (low // rows), :, begin : begin + step] = (mixed[:HEAD_DIM] / total).astype(BF)


def attend(t, chunks, qx, kx, vx):
    _, heads, rows, _ = chunks[0].shape
    length = qx.shape[0]
    chunk = pl.BlockSpec((3, 1, rows, LANES), lambda h, t_ref: (0, h, 0, 0))
    plane = pl.BlockSpec((1, length, LANES), lambda h, t_ref: (h, 0, 0))
    padded = shape_of((heads, length, LANES), BF)
    return call(
        attend_body,
        "attend",
        (heads,),
        [chunk] * 4 + [whole(qx), whole(kx), whole(vx)],
        [
            plane,
            plane,
            plane,
            pl.BlockSpec((4, HEAD_DIM, rows), lambda h, t_ref: (0, h, 0)),
            pl.BlockSpec((1, 1, length), lambda h, t_ref: (h, 0, 0)),
        ],
        [padded, padded, padded, shape_of((4, heads * HEAD_DIM, rows), BF), shape_of((heads, 1, length), F32)],
        (t, *chunks, qx, kx, vx),
        scratch=[pltpu.VMEM((LANES, length), BF)],
        prefetch=1,
        flops=heads * length * length * 512,
    )


def three_parts(values):
    first = values.astype(BF).astype(F32)
    second = (values - first).astype(BF).astype(F32)
    return first, second, values - first - second


def attend_back_body(
    t_ref, qe_ref, ke_ref, ve_ref, d0, d1, d2, d3, ot_ref, lse_ref, cos_ref, sa_ref, sb_ref, out_ref,
    qt_ref, kt_ref, dt_ref, dk_ref, dv_ref,
):
    t = t_ref[0]
    rows = d0.shape[1]
    step = QUERY_ROWS
    length = qe_ref.shape[1]
    for rel, chunk in enumerate((d0, d1, d2, d3)):
        place = pl.ds(pl.multiple_of((t ^ rel) * rows, rows), rows)
        grad = chunk[...].astype(F32)
        delta = three_parts(jnp.sum(grad * ot_ref[rel].astype(F32), 0, keepdims=True))
        padded = jnp.concatenate([grad, jnp.zeros_like(grad)], 0)
        row = lax.broadcasted_iota(jnp.int32, padded.shape, 0)
        for index in range(3):
            padded = jnp.where(row == HEAD_DIM + index, -delta[index], padded)
        dt_ref[:, place] = padded.astype(BF)
    for low in range(0, length, rows):
        high = low + rows
        kt_ref[:, low:high] = ke_ref[0, low:high, :].astype(F32).T.astype(BF)
        turned = qe_ref[0, low:high, :].astype(F32).T
        row = lax.broadcasted_iota(jnp.int32, turned.shape, 0)
        pieces = three_parts(lse_ref[0, :, low:high])
        for index in range(3):
            turned = jnp.where(row == LSE_LANE + index, -pieces[index], turned)
        qt_ref[:, low:high] = turned.astype(BF)
    dk_ref[...] = jnp.zeros_like(dk_ref)
    dv_ref[...] = jnp.zeros_like(dv_ref)

    def unrotate(grad, place):
        return (
            grad * cos_ref[place, :]
            - pltpu.roll(grad, 96, 1) * sa_ref[place, :]
            - pltpu.roll(grad, 32, 1) * sb_ref[place, :]
        )

    for low in range(0, length, step):
        high = low + step
        query, query_t, grad_t = qe_ref[0, low:high, :], qt_ref[:, low:high], dt_ref[:, low:high]
        dq_t = None
        for begin, end in ((0, low), (low, high)):
            if begin == end:
                continue
            scores = nn(ke_ref[0, begin:end, :], query_t)
            if begin == low:
                scores = causal_corner(scores)
            prob = jnp.exp(scores)
            grad_scores = (prob * nn(ve_ref[0, begin:end, :], grad_t)).astype(BF)
            dv_ref[begin:end, :] += nt(prob.astype(BF), grad_t)
            dk_ref[begin:end, :] += nn(grad_scores, query)
            part = nn(kt_ref[:, begin:end], grad_scores)
            dq_t = part if dq_t is None else dq_t + part
        start = low % rows
        grad_query = unrotate(dq_t.T, slice(low, high)) * (1.0 / math.sqrt(HEAD_DIM))
        out_ref[t ^ (low // rows), 0, 0, start : start + step, :] = grad_query.astype(BF)
    for low in range(0, length, rows):
        place = slice(low, low + rows)
        rel = t ^ (low // rows)
        out_ref[rel, 1, 0] = unrotate(dk_ref[place, :], place).astype(BF)
        lane = lax.broadcasted_iota(jnp.int32, (rows, LANES), 1)
        out_ref[rel, 2, 0] = jnp.where(lane < HEAD_DIM, dv_ref[place, :], 0.0).astype(BF)


def attend_back(t, qe, ke, ve, grads, ot, lse, tables):
    heads, length, _ = qe.shape
    rows = grads[0].shape[1]
    plane = pl.BlockSpec((1, length, LANES), lambda h, t_ref: (h, 0, 0))
    grad = pl.BlockSpec((HEAD_DIM, rows), lambda h, t_ref: (h, 0))
    return call(
        attend_back_body,
        "attend_back",
        (heads,),
        [plane] * 3
        + [grad] * 4
        + [
            pl.BlockSpec((4, HEAD_DIM, rows), lambda h, t_ref: (0, h, 0)),
            pl.BlockSpec((1, 1, length), lambda h, t_ref: (h, 0, 0)),
        ]
        + [whole(table) for table in tables],
        pl.BlockSpec((4, 3, 1, rows, LANES), lambda h, t_ref: (0, 0, h, 0, 0)),
        shape_of((4, 3, heads, rows, LANES), BF),
        (t, qe, ke, ve, *grads, ot, lse, *tables),
        scratch=[pltpu.VMEM((LANES, length), BF)] * 3 + [pltpu.VMEM((length, LANES), F32)] * 2,
        prefetch=1,
        flops=heads * length * length * 1280,
    )


def input_back_body(x_ref, dp_ref, w_ref, out_ref, small_ref):
    heads = dp_ref.shape[2]
    grads = jnp.concatenate([dp_ref[0, j // heads, j % heads] for j in range(3 * heads)], 1)
    grad = nt(grads, w_ref[...])
    normed, _ = standardize(x_ref[...].astype(F32))
    out_ref[...] = grad.astype(BF)
    add_rows(small_ref, [column_sum(grad * normed), column_sum(grad)])


def input_back(rel, x, dp, w):
    rows, width = x.shape
    heads = dp.shape[2]
    tile = min(256, rows)
    return call(
        input_back_body,
        f"input_back_{rel}",
        (rows // tile,),
        [
            rows_of(tile, width),
            pl.BlockSpec((1, 3, heads, tile, LANES), lambda i: (rel, 0, 0, i, 0)),
            whole(w),
        ],
        [rows_of(tile, width), pl.BlockSpec((8, width), lambda i: (0, 0))],
        [shape_of((rows, width), BF), shape_of((8, width), F32)],
        (x, dp, w),
        flops=2 * rows * width * w.shape[1],
    )


def qkv_weight_body(dp_ref, a0, a1, a2, a3, out_ref, bias_ref):
    heads = dp_ref.shape[2]
    total, sums = None, None
    for rel, a_ref in enumerate((a0, a1, a2, a3)):
        grads = jnp.concatenate([dp_ref[rel, 0, h] for h in range(heads)], 1)
        part, part_sum = tn(grads, a_ref[...]), column_sum(grads.astype(F32))
        total = part if total is None else total + part
        sums = part_sum if sums is None else sums + part_sum
    for h in range(heads):
        out_ref[h * HEAD_DIM : (h + 1) * HEAD_DIM, :] = total[h * LANES : h * LANES + HEAD_DIM].astype(BF)
    bias_ref[0] = sums


def qkv_weight(dp, normed):
    _, _, heads, rows, _ = dp.shape
    width = normed[0].shape[1]
    local = heads * HEAD_DIM
    return call(
        qkv_weight_body,
        "qkv_weight",
        (3,),
        [pl.BlockSpec((4, 1, heads, rows, LANES), lambda j: (0, j, 0, 0, 0))] + [whole(a) for a in normed],
        [rows_of(local, width), pl.BlockSpec((1, 1, heads * LANES), lambda j: (j, 0, 0))],
        [shape_of((3 * local, width), BF), shape_of((3, 1, heads * LANES), F32)],
        (dp, *normed),
        flops=2 * 4 * rows * 3 * heads * LANES * width,
    )


def after_attend_body(
    x_ref, o0, o1, o2, o3, w0, w1, w2, w3, bias_ref, gain_ref, shift_ref, wq_ref, bq_ref, x1_ref, b_ref, cq_ref
):
    total = x_ref[...].astype(F32) + bias_ref[0:1, :]
    for o_ref, w_ref in ((o0, w0), (o1, w1), (o2, w2), (o3, w3)):
        total = total + tn(o_ref[...], w_ref[...])
    x1_ref[...] = total
    normed, _ = standardize(total)
    b = (normed * gain_ref[1:2, :] + shift_ref[1:2, :]).astype(BF)
    b_ref[...] = b
    weight = wq_ref[...].reshape(-1, wq_ref.shape[2])
    cq_ref[...] = ((nt(b, weight) + bq_ref[...]) * (1.0 / math.sqrt(HEAD_DIM))).astype(BF)


def after_attend(x, mixed, packs, weights, out_bias, gain, shift, bq):
    rows, width = x.shape
    local = mixed[0].shape[0]
    tile = min(256, rows)
    return call(
        after_attend_body,
        "after_attend",
        (rows // tile,),
        [rows_of(tile, width)]
        + [pl.BlockSpec((local, tile), lambda i: (0, i))] * 4
        + [pl.BlockSpec((local, width), lambda i: (1, 0))] * 4
        + [whole(out_bias), whole(gain), whole(shift)]
        + [pl.BlockSpec((4, local, width), lambda i: (0, 0, 0)), whole(bq)],
        [rows_of(tile, width)] * 3,
        [shape_of((rows, width), F32), shape_of((rows, width), BF), shape_of((rows, width), BF)],
        (x, *mixed, *packs, out_bias, gain, shift, weights, bq),
        flops=4 * rows * width * width,
    )


def head_lanes(width):
    heads = width // HEAD_DIM
    count = -(-heads // 16) * 16
    row = lax.broadcasted_iota(jnp.int32, (count, width), 0)
    lane = lax.broadcasted_iota(jnp.int32, (count, width), 1)
    return (lax.shift_right_logical(lane, 6) == row).astype(BF)


def two_parts(values):
    first = values.astype(BF)
    return first, (values - first.astype(F32)).astype(BF)


def merge_parts(first, first_lse, second, second_lse):
    weight = 1.0 / (1.0 + jnp.exp(second_lse - first_lse))
    expand = head_lanes(first.shape[1])
    high, low = two_parts(weight)
    share = tn(high, expand) + tn(low, expand)
    second = second.astype(F32)
    merged = second + share * (first.astype(F32) - second)
    gap = -jnp.abs(first_lse - second_lse)
    return merged, jnp.maximum(first_lse, second_lse) + jnp.log(1.0 + jnp.exp(gap))


def merge_body(a_ref, al_ref, b_ref, bl_ref, out_ref, lse_ref):
    merged, lse = merge_parts(a_ref[0], al_ref[0], b_ref[...], bl_ref[...])
    out_ref[...] = merged.astype(BF)
    lse_ref[...] = lse


def merge(rel, parts, lses, other, other_lse):
    _, rows, width = parts.shape
    count = lses.shape[1]
    tile = min(256, rows)
    return call(
        merge_body,
        f"merge_{rel}",
        (rows // tile,),
        [
            pl.BlockSpec((1, tile, width), lambda i: (rel, i, 0)),
            pl.BlockSpec((1, count, tile), lambda i: (rel, 0, i)),
            rows_of(tile, width),
            pl.BlockSpec((count, tile), lambda i: (0, i)),
        ],
        [rows_of(tile, width), pl.BlockSpec((count, tile), lambda i: (0, i))],
        [shape_of((rows, width), BF), shape_of((count, rows), F32)],
        (parts, lses, other, other_lse),
        flops=4 * rows * width * count,
    )


def after_cross_body(
    a_ref, al_ref, b_ref, bl_ref, x1_ref, w_ref, bias_ref, gain_ref, shift_ref, co_ref, lse_ref, x2_ref, m_ref
):
    merged, lse = merge_parts(a_ref[...], al_ref[...], b_ref[...], bl_ref[...])
    mixed = merged.astype(BF)
    co_ref[...] = mixed
    lse_ref[...] = lse
    weight = w_ref[...].reshape(-1, w_ref.shape[2])
    total = x1_ref[...] + nn(mixed, weight) + bias_ref[1:2, :]
    x2_ref[...] = total
    normed, _ = standardize(total)
    m_ref[...] = (normed * gain_ref[2:3, :] + shift_ref[2:3, :]).astype(BF)


def after_cross(a, a_lse, b, b_lse, x1, weights, local, out_bias, gain, shift):
    rows, width = x1.shape
    count = a_lse.shape[0]
    tile = min(256, rows)
    stats = pl.BlockSpec((count, tile), lambda i: (0, i))
    return call(
        after_cross_body,
        "after_cross",
        (rows // tile,),
        [rows_of(tile, width), stats, rows_of(tile, width), stats, rows_of(tile, width)]
        + [pl.BlockSpec((4, local, width), lambda i: (0, 4, 0)), whole(out_bias), whole(gain), whole(shift)],
        [rows_of(tile, width), stats, rows_of(tile, width), rows_of(tile, width)],
        [
            shape_of((rows, width), BF),
            shape_of((count, rows), F32),
            shape_of((rows, width), F32),
            shape_of((rows, width), BF),
        ],
        (a, a_lse, b, b_lse, x1, weights, out_bias, gain, shift),
        flops=2 * rows * width * width,
    )


def before_cross_body(
    x2_ref, da_ref, db_ref, g_ref, co_ref, w_ref, gain_ref, g2_ref, g2r_ref, dco_ref, delta_ref, small_ref
):
    grad = da_ref[...].astype(F32) + db_ref[...].astype(F32)
    normed, inverse = standardize(x2_ref[...])
    g = g_ref[...]
    g2 = g + norm_pull(grad, normed, inverse, gain_ref[2:3, :])
    g2_ref[...] = g2
    g2r = g2.astype(BF)
    g2r_ref[...] = g2r
    weight = w_ref[...].reshape(-1, w_ref.shape[2])
    dco = nt(g2r, weight).astype(BF)
    dco_ref[...] = dco
    high, low = two_parts(dco.astype(F32) * co_ref[...].astype(F32))
    expand = head_lanes(high.shape[1])
    delta_ref[...] = nt(expand, high) + nt(expand, low)
    add_rows(small_ref, [column_sum(grad * normed), column_sum(grad), column_sum(g), column_sum(g2)])


def before_cross(x2, da, db, g, co, weights, local, gain, count):
    rows, width = x2.shape
    tile = min(256, rows)
    row = rows_of(tile, width)
    return call(
        before_cross_body,
        "before_cross",
        (rows // tile,),
        [row] * 5 + [pl.BlockSpec((4, local, width), lambda i: (0, 4, 0)), whole(gain)],
        [row, row, row, pl.BlockSpec((count, tile), lambda i: (0, i)), pl.BlockSpec((8, width), lambda i: (0, 0))],
        [
            shape_of((rows, width), F32),
            shape_of((rows, width), BF),
            shape_of((rows, width), BF),
            shape_of((count, rows), F32),
            shape_of((8, width), F32),
        ],
        (x2, da, db, g, co, weights, gain),
        flops=2 * rows * width * width,
    )


def before_attend_body(
    x1_ref, qa_ref, qb_ref, g2_ref, wq_ref, w0, w1, w2, w3, gain_ref,
    g1_ref, g1r_ref, dqc_ref, d0, d1, d2, d3, small_ref,
):
    dqc = ((qa_ref[...].astype(F32) + qb_ref[...].astype(F32)) * (1.0 / math.sqrt(HEAD_DIM))).astype(BF)
    dqc_ref[...] = dqc
    grad = nn(dqc, wq_ref[...].reshape(-1, wq_ref.shape[2]))
    normed, inverse = standardize(x1_ref[...])
    g1 = g2_ref[...] + norm_pull(grad, normed, inverse, gain_ref[1:2, :])
    g1_ref[...] = g1
    g1r = g1.astype(BF)
    g1r_ref[...] = g1r
    for w_ref, d_ref in ((w0, d0), (w1, d1), (w2, d2), (w3, d3)):
        d_ref[...] = nt(w_ref[...], g1r).astype(BF)
    add_rows(
        small_ref, [column_sum(grad * normed), column_sum(grad), column_sum(g1), column_sum(dqc.astype(F32))]
    )


def before_attend(x1, qa, qb, g2, weights, packs, local, gain):
    rows, width = x1.shape
    tile = min(256, rows)
    row = rows_of(tile, width)
    turned = pl.BlockSpec((local, tile), lambda i: (0, i))
    return call(
        before_attend_body,
        "before_attend",
        (rows // tile,),
        [row] * 4
        + [pl.BlockSpec((4, local, width), lambda i: (0, 0, 0))]
        + [pl.BlockSpec((local, width), lambda i: (1, 0))] * 4
        + [whole(gain)],
        [row, row, row] + [turned] * 4 + [pl.BlockSpec((8, width), lambda i: (0, 0))],
        [shape_of((rows, width), F32), shape_of((rows, width), BF), shape_of((rows, width), BF)]
        + [shape_of((local, rows), BF)] * 4
        + [shape_of((8, width), F32)],
        (x1, qa, qb, g2, weights, *packs, gain),
        flops=4 * rows * width * width,
    )


def split_pair(values):
    lane = lax.broadcasted_iota(jnp.int32, values.shape, 1)
    zero = jnp.zeros_like(values)
    return jnp.concatenate(
        [jnp.where(lane < HEAD_DIM, values, zero), jnp.where(lane >= HEAD_DIM, values, zero)], 0
    )


def join_pair(values):
    rows = values.shape[0] // 2
    lane = lax.broadcasted_iota(jnp.int32, (rows, values.shape[1]), 1)
    return jnp.where(lane < HEAD_DIM, values[:rows], values[rows:])


def span_place(t, slot, per_span, chunk_rows):
    first = (slot // per_span) * SPAN
    chunk = first // chunk_rows
    return pl.multiple_of((t ^ chunk) * chunk_rows + first - chunk * chunk_rows, SPAN)


def cross_body(t_ref, slot_ref, q0, q1, q2, q3, kv_ref, out_ref, lse_ref, q_ref, o_ref, st_ref, *, per_span):
    t = t_ref[0]
    rows, width = q0.shape
    blocks = slot_ref.shape[0]
    length = kv_ref.shape[0] // blocks
    for rel, ref in enumerate((q0, q1, q2, q3)):
        q_ref[rel * rows : (rel + 1) * rows, :] = ref[...]
    o_ref[...] = jnp.zeros_like(o_ref)
    st_ref[...] = jnp.full_like(st_ref, NEGATIVE)

    def one_block(p, carry):
        place = pl.ds(span_place(t, slot_ref[p], per_span, rows), SPAN)
        keys = pl.ds(pl.multiple_of(p * length, length), length)
        stats = st_ref[place, :]
        lane = lax.broadcasted_iota(jnp.int32, stats.shape, 1)
        pair_lane = lax.broadcasted_iota(jnp.int32, (SPAN, LANES), 1)
        fresh = stats
        for j in range(width // LANES):
            cut = slice(j * LANES, (j + 1) * LANES)
            scores = nt(split_pair(q_ref[place, cut]), kv_ref[keys, cut])
            top = jnp.max(scores, 1, keepdims=True)
            shifted = jnp.exp(scores - top)
            total = jnp.sum(shifted, 1, keepdims=True)
            value_cut = slice(width + j * LANES, width + (j + 1) * LANES)
            mixed = join_pair(nn(shifted.astype(BF), kv_ref[keys, value_cut]) / total)
            own = top + jnp.log(total)
            shares = []
            for side in range(2):
                mine = own[side * SPAN : (side + 1) * SPAN]
                head = 2 * j + side
                before = jnp.sum(jnp.where(lane == head, stats, 0.0), 1, keepdims=True)
                shares.append(1.0 / (1.0 + jnp.exp(before - mine)))
                both = jnp.maximum(mine, before) + jnp.log(1.0 + jnp.exp(-jnp.abs(mine - before)))
                fresh = jnp.where(lane == head, both, fresh)
            share = jnp.where(pair_lane < HEAD_DIM, shares[0], shares[1])
            old = o_ref[place, cut]
            o_ref[place, cut] = old + share * (mixed - old)
        st_ref[place, :] = fresh
        return carry

    lax.fori_loop(0, blocks, one_block, 0)
    for rel in range(4):
        place = slice(rel * rows, (rel + 1) * rows)
        out_ref[rel] = o_ref[place, :].astype(BF)
        lse_ref[rel] = st_ref[place, :].T[: lse_ref.shape[1]]


def cross(t, slots, queries, kv, per_span, count):
    rows, width = queries[0].shape
    return call(
        functools.partial(cross_body, per_span=per_span),
        "cross",
        (1,),
        [whole(q) for q in queries] + [whole(kv)],
        [
            pl.BlockSpec((4, rows, width), lambda *_: (0, 0, 0)),
            pl.BlockSpec((4, count, rows), lambda *_: (0, 0, 0)),
        ],
        [shape_of((4, rows, width), BF), shape_of((4, count, rows), F32)],
        (t, slots, *queries, kv),
        scratch=[
            pltpu.VMEM((4 * rows, width), BF),
            pltpu.VMEM((4 * rows, width), F32),
            pltpu.VMEM((4 * rows, LANES), F32),
        ],
        prefetch=2,
        flops=8 * kv.shape[0] * SPAN * width,
    )


def cross_back_body(
    t_ref, slot_ref, q0, q1, q2, q3, d0, d1, d2, d3, s0, s1, s2, s3, kv_ref, dkv_ref, dq_ref,
    q_ref, d_ref, st_ref, acc_ref, *, per_span,
):
    t = t_ref[0]
    rows, width = q0.shape
    blocks = slot_ref.shape[0]
    length = kv_ref.shape[0] // blocks
    count = s0.shape[0]
    for rel, (a, b, c) in enumerate(zip((q0, q1, q2, q3), (d0, d1, d2, d3), (s0, s1, s2, s3))):
        place = slice(rel * rows, (rel + 1) * rows)
        q_ref[place, :] = a[...]
        d_ref[place, :] = b[...]
        filler = jnp.zeros((LANES - count, rows), F32)
        st_ref[place, :] = jnp.concatenate([c[...], filler], 0).T
    acc_ref[...] = jnp.zeros_like(acc_ref)

    def one_block(p, carry):
        place = pl.ds(span_place(t, slot_ref[p], per_span, rows), SPAN)
        keys = pl.ds(pl.multiple_of(p * length, length), length)
        stats = st_ref[place, :]
        lane = lax.broadcasted_iota(jnp.int32, stats.shape, 1)

        def column(index):
            return jnp.sum(jnp.where(lane == index, stats, 0.0), 1, keepdims=True)

        for j in range(width // LANES):
            cut = slice(j * LANES, (j + 1) * LANES)
            value_cut = slice(width + j * LANES, width + (j + 1) * LANES)
            query, grad = split_pair(q_ref[place, cut]), split_pair(d_ref[place, cut])
            key, value = kv_ref[keys, cut], kv_ref[keys, value_cut]
            lse = jnp.concatenate([column(2 * j), column(2 * j + 1)], 0)
            delta = jnp.concatenate([column(count // 2 + 2 * j), column(count // 2 + 2 * j + 1)], 0)
            prob = jnp.exp(nt(query, key) - lse)
            grad_scores = (prob * (nt(grad, value) - delta)).astype(BF)
            dkv_ref[keys, cut] = tn(grad_scores, query).astype(BF)
            dkv_ref[keys, value_cut] = tn(prob.astype(BF), grad).astype(BF)
            acc_ref[place, cut] += join_pair(nn(grad_scores, key))
        return carry

    lax.fori_loop(0, blocks, one_block, 0)
    for rel in range(4):
        dq_ref[rel] = acc_ref[rel * rows : (rel + 1) * rows, :].astype(BF)


def cross_back(t, slots, queries, grads, stats, kv, per_span):
    rows, width = queries[0].shape
    return call(
        functools.partial(cross_back_body, per_span=per_span),
        "cross_back",
        (1,),
        [whole(q) for q in (*queries, *grads, *stats)] + [whole(kv)],
        [pl.BlockSpec(kv.shape, lambda *_: (0, 0)), pl.BlockSpec((4, rows, width), lambda *_: (0, 0, 0))],
        [shape_of(kv.shape, BF), shape_of((4, rows, width), BF)],
        (t, slots, *queries, *grads, *stats, kv),
        scratch=[
            pltpu.VMEM((4 * rows, width), BF),
            pltpu.VMEM((4 * rows, width), BF),
            pltpu.VMEM((4 * rows, LANES), F32),
            pltpu.VMEM((4 * rows, width), F32),
        ],
        prefetch=2,
        flops=20 * kv.shape[0] * SPAN * width,
    )


def feed_body(m_ref, g_ref, w1_ref, w2_ref, b1_ref, out_ref, dm_ref, h_ref, du_ref, db_ref):
    u = nn(m_ref[...], w1_ref[...]) + b1_ref[...]
    curve = math.sqrt(2.0 / math.pi)
    square = u * u
    bent = jnp.tanh(curve * (u + 0.044715 * u * square))
    half = 0.5 * (1.0 + bent)
    h = (u * half).astype(BF)
    h_ref[...] = h
    out_ref[...] = nn(h, w2_ref[...]).astype(BF)
    slope = half + 0.5 * u * (1.0 - bent * bent) * (curve * (1.0 + 3.0 * 0.044715 * square))
    du = (nt(g_ref[...], w2_ref[...]) * slope).astype(BF)
    du_ref[...] = du
    dm_ref[...] = nt(du, w1_ref[...]).astype(BF)
    add_rows(db_ref, [column_sum(du.astype(F32))])


def feed(rel, m, g, w1, w2, b1):
    rows, width = m.shape
    hidden = w1.shape[1]
    tile = min(256, rows)
    return call(
        feed_body,
        f"feed_{rel}",
        (rows // tile,),
        [rows_of(tile, width)] * 2 + [whole(w1), whole(w2), whole(b1)],
        [rows_of(tile, width)] * 2 + [rows_of(tile, hidden)] * 2 + [pl.BlockSpec((8, hidden), lambda i: (0, 0))],
        [shape_of((rows, width), BF)] * 2 + [shape_of((rows, hidden), BF)] * 2 + [shape_of((8, hidden), F32)],
        (m, g, w1, w2, b1),
        flops=8 * rows * width * hidden,
    )


def weight_body(*refs):
    count = (len(refs) - 1) // 2
    total = None
    for left, right in zip(refs[:count], refs[count:-1]):
        part = tn(left[...], right[...])
        total = part if total is None else total + part
    refs[-1][...] = total.astype(BF)


def weight(name, lefts, rights):
    rows, out_rows = lefts[0].shape
    width = rights[0].shape[1]
    tile = 256
    return call(
        weight_body,
        name,
        (out_rows // tile,),
        [pl.BlockSpec((rows, tile), lambda i: (0, i))] * len(lefts) + [whole(r) for r in rights],
        rows_of(tile, width),
        shape_of((out_rows, width), BF),
        (*lefts, *rights),
        flops=2 * len(lefts) * rows * out_rows * width,
    )


def cross_weight_body(
    t_ref, dqc_ref, b_ref, o0, o1, o2, o3, g1_ref, dkv_ref, memory_ref, co_ref, g2_ref, out_ref, bias_ref
):
    t = t_ref[0]
    local = out_ref.shape[2]
    width = out_ref.shape[3]

    def place(index, grad):
        for group in range(4):
            out_ref[t ^ group, index] = grad[group * local : (group + 1) * local].astype(BF)

    place(0, tn(dqc_ref[...], b_ref[...]))
    for rel, o_ref in enumerate((o0, o1, o2, o3)):
        out_ref[rel, 1] = nn(o_ref[...], g1_ref[...]).astype(BF)
    place(2, tn(dkv_ref[:, :width], memory_ref[...]))
    place(3, tn(dkv_ref[:, width:], memory_ref[...]))
    place(4, tn(co_ref[...], g2_ref[...]))
    bias_ref[...] = column_sum(dkv_ref[:, width:].astype(F32))


def cross_weight(t, dqc, b, mixed, g1r, dkv, memory, co, g2r):
    width = b.shape[1]
    local = mixed[0].shape[0]
    args = (dqc, b, *mixed, g1r, dkv, memory, co, g2r)
    return call(
        cross_weight_body,
        "cross_weight",
        (1,),
        [whole(a) for a in args],
        [
            pl.BlockSpec((4, 5, local, width), lambda *_: (0, 0, 0, 0)),
            pl.BlockSpec((1, width), lambda *_: (0, 0)),
        ],
        [shape_of((4, 5, local, width), BF), shape_of((1, width), F32)],
        (t, *args),
        prefetch=1,
        flops=2 * width * width * (3 * b.shape[0] + 2 * memory.shape[0]),
    )


def input_grad_body(x_ref, da_ref, db_ref, g1_ref, gain_ref, out_ref):
    normed, inverse = standardize(x_ref[...].astype(F32))
    grad = da_ref[...].astype(F32) + db_ref[...].astype(F32)
    out_ref[...] = g1_ref[...] + norm_pull(grad, normed, inverse, gain_ref[0:1, :])


def input_grad(x, da, db, g1, gain):
    rows, width = x.shape
    tile = min(256, rows)
    row = rows_of(tile, width)
    return call(
        input_grad_body,
        "input_grad",
        (rows // tile,),
        [row] * 4 + [whole(gain)],
        row,
        shape_of((rows, width), F32),
        (x, da, db, g1, gain),
        flops=rows * width * 16,
    )


def padded_tables(length):
    half = HEAD_DIM // 2
    frequency = 10000.0 ** (-jnp.arange(half, dtype=F32) / half)
    angles = jnp.arange(length, dtype=F32)[:, None] * frequency[None, :]
    cosine, sine = jnp.cos(angles), jnp.sin(angles)
    zero = jnp.zeros_like(sine)
    return (
        jnp.concatenate([cosine, cosine, zero, zero], 1),
        jnp.concatenate([-sine, zero, zero, zero], 1),
        jnp.concatenate([zero, sine, zero, zero], 1),
    )


def mask_lanes(segments):
    lane = lax.broadcasted_iota(jnp.int32, (segments.shape[0], LANES), 1)
    is_mask = (lane >= MASK_LANE) & (lane < MASK_LANE + DOCS)
    same = is_mask & (lane - MASK_LANE == segments[:, None])
    is_lse = (lane >= LSE_LANE) & (lane < LSE_LANE + 3)
    query_lanes = jnp.where(same, 1.0, 0.0).astype(BF)
    key_lanes = jnp.where(is_mask & ~same, NEGATIVE, jnp.where(is_lse, 1.0, 0.0)).astype(BF)
    return query_lanes, key_lanes


def pad_heads(values):
    lead = values.shape[:-1]
    heads = values.shape[-1] // HEAD_DIM
    values = values.reshape(lead + (heads, HEAD_DIM))
    values = jnp.pad(values, [(0, 0)] * (len(lead) + 1) + [(0, LANES - HEAD_DIM)])
    return values.reshape(lead[:-1] + (-1,))


def shards(
    layer_input,
    norm_gain,
    norm_bias,
    self_input_weight,
    self_input_bias,
    self_output_weight,
    out_bias,
    cross_query_weight,
    b_cross_q,
    w_cross_kv,
    b_cross_v,
    cross_output_weight,
    expand_weight_1,
    expand_bias_1,
    contract_weight_2,
    neighbours,
    segment_ids,
    span_map,
    cotangent,
):
    x = layer_input[0]
    rows, width = x.shape
    length = segment_ids.shape[1]
    local = self_input_weight.shape[2]
    heads = local // HEAD_DIM
    all_heads = width // HEAD_DIM
    count = -(-all_heads // 16) * 16
    blocks, block_rows = neighbours.shape[1], neighbours.shape[2]
    per_span = span_map.shape[1] // (length // SPAN)
    memory = neighbours[0].reshape(blocks * block_rows, width)
    grad_out = cotangent[0]
    index = lax.axis_index("tp")
    t = index.astype(jnp.int32).reshape(1)
    partners = [[(i, i ^ step) for i in range(4)] for step in (1, 2, 3)]

    xs = spread(x, partners)
    bias_parts = []
    for bias in (b_cross_q, b_cross_v):
        high = lax.reduce_precision(bias, 8, 7)
        bias_parts += [high, bias - high]
    pack = jnp.concatenate(
        [
            cross_query_weight.T,
            self_output_weight,
            w_cross_kv[:, 0].T,
            w_cross_kv[:, 1].T,
            cross_output_weight,
            jnp.pad(jnp.concatenate(bias_parts).astype(BF)[None], ((0, 15), (0, 0))),
        ],
        0,
    )
    pack, _ = lax.optimization_barrier((pack, xs[2]))
    packs = spread(pack, partners)
    gathered, _ = lax.optimization_barrier((grad_out.astype(BF), packs[2]))
    gs = spread(gathered, partners)

    tables = padded_tables(length)
    w_pad = pad_heads(self_input_weight)
    b_pad = pad_heads(self_input_bias)[None]
    normed_first, chunks = [], []
    for rel in range(4):
        a, chunk = project_rows(rel, t, xs[rel], norm_gain, norm_bias, w_pad, b_pad, tables, heads)
        normed_first.append(a)
        chunks.append(chunk)
    qx, kx = mask_lanes(segment_ids[0])
    lane = lax.broadcasted_iota(jnp.int32, (1, LANES), 1)
    vx = jnp.where((lane >= HEAD_DIM) & (lane < HEAD_DIM + 3), 1.0, 0.0).astype(BF)
    qe, ke, ve, ot, lse = attend(t, chunks, qx, kx, vx)
    mixed = exchange([ot[0], ot[1], ot[2], ot[3]], partners)

    weights = jnp.zeros((4,) + pack.shape, BF)
    for rel in range(4):
        weights = lax.dynamic_update_slice(weights, packs[rel][None], (index ^ rel, 0, 0))
    bias_rows = weights[:, 5 * local].astype(F32).reshape(4, 4, local)
    bq = (bias_rows[:, 0] + bias_rows[:, 1]).reshape(1, width)
    bv = (bias_rows[:, 2] + bias_rows[:, 3]).reshape(1, width)
    weight_kv = jnp.concatenate(
        [weights[:, k * local : (k + 1) * local].reshape(width, width) for k in (2, 3)], 0
    )
    memory_kv = (
        lax.dot_general(memory, weight_kv, (((1,), (1,)), ((), ())), preferred_element_type=F32)
        + jnp.concatenate([jnp.zeros_like(bv), bv], 1)
    ).astype(BF)
    block_ids = index * blocks + jnp.arange(blocks, dtype=jnp.int32)
    slot_ids = jnp.arange(span_map.shape[1], dtype=jnp.int32)
    slots = jnp.sum(jnp.where(span_map[0][None, :] == block_ids[:, None], slot_ids[None, :], 0), 1)

    x1, b, cq = after_attend(x, mixed, packs, weights, out_bias, norm_gain, norm_bias, bq)
    queries = spread(cq, partners)
    parts, part_lse = cross(t, slots, queries, memory_kv, per_span, count)
    core, chip, _ = partners
    far, far_lse = lax.ppermute(parts[3], "tp", core), lax.ppermute(part_lse[3], "tp", core)
    near, near_lse = lax.ppermute(parts[1], "tp", core), lax.ppermute(part_lse[1], "tp", core)
    sent, sent_lse = merge(2, parts, part_lse, far, far_lse)
    across, across_lse = lax.ppermute(sent, "tp", chip), lax.ppermute(sent_lse, "tp", chip)
    kept, kept_lse = merge(0, parts, part_lse, near, near_lse)
    co, cross_lse, x2, m = after_cross(
        kept, kept_lse, across, across_lse, x1, weights, local, out_bias, norm_gain, norm_bias
    )

    ms = spread(m, partners)
    fed = [
        feed(rel, ms[rel], gs[rel], expand_weight_1, contract_weight_2, expand_bias_1[None])
        for rel in range(4)
    ]
    dm = collect([f[1] for f in fed], partners)
    out = collect([f[0] for f in fed], partners)
    grad_w1 = weight("weight_1", ms, [f[3] for f in fed])
    grad_w2 = weight("weight_2", [f[2] for f in fed], gs)
    grad_b1 = fed[0][4] + fed[1][4] + fed[2][4] + fed[3][4]
    summed_feed = lax.psum(jnp.concatenate([grad_w1, grad_w2, grad_b1.astype(BF)], 0), "dp")
    layer_output = x2 + (out[0].astype(F32) + out[1].astype(F32)) + out_bias[2]

    g2, g2r, dco, delta, small_two = before_cross(
        x2, dm[0], dm[1], grad_out, co, weights, local, norm_gain, count
    )
    grads = spread(dco, partners)
    half = count
    stats = spread(jnp.concatenate([cross_lse[:half], delta[:half]], 0), partners)
    dkv, dq_parts = cross_back(t, slots, queries, grads, stats, memory_kv, per_span)
    dq = collect([dq_parts[r] for r in range(4)], partners)
    grad_memory = lax.dot_general(
        dkv, weight_kv, (((1,), (0,)), ((), ())), preferred_element_type=F32
    ).reshape(neighbours.shape)
    g1, g1r, dqc, *dos, small_one = before_attend(x1, dq[0], dq[1], g2, weights, packs, local, norm_gain)

    dos = exchange(dos, partners)
    grad_cross, grad_bv = cross_weight(t, dqc, b, mixed, g1r, dkv, memory, co, g2r)
    dp = attend_back(t, qe, ke, ve, dos, ot, lse, tables)
    grad_rows = [input_back(rel, xs[rel], dp, w_pad) for rel in (3, 1, 2, 0)][::-1]
    grad_rows = [grad_rows[0], grad_rows[2], grad_rows[1], grad_rows[3]]
    da = collect([g[0] for g in grad_rows], partners)
    grad_qkv, grad_bqkv = qkv_weight(dp, normed_first)
    grad_input = input_grad(x, da[0], da[1], g1, norm_gain)

    grad_far = lax.ppermute(jnp.stack([grad_cross[1], grad_cross[3]]), "tp", core)
    sent = (grad_cross[2].astype(F32) + grad_far[1].astype(F32)).astype(BF)
    across = lax.ppermute(sent, "tp", chip)
    own = (grad_cross[0].astype(F32) + grad_far[0].astype(F32) + across.astype(F32)).astype(BF)
    small_zero = grad_rows[0][1] + grad_rows[1][1] + grad_rows[2][1] + grad_rows[3][1]
    small = jnp.concatenate([small_zero[:2], small_one[:4], small_two[:4], grad_bv, jnp.zeros((5, width), F32)], 0)
    small = small + lax.ppermute(small, "tp", core)
    small = small + lax.ppermute(small, "tp", chip)
    bqkv_row = jnp.pad(grad_bqkv.reshape(3, heads, LANES)[:, :, :HEAD_DIM].reshape(1, -1), ((0, 15), (0, width - 3 * local)))
    last = jnp.concatenate([grad_qkv, own.reshape(5 * local, width), small.astype(BF), bqkv_row.astype(BF)], 0)
    last, summed_feed = lax.optimization_barrier((last, summed_feed))
    summed = lax.psum(last, "dp").astype(F32)

    summed_feed = summed_feed.astype(F32)
    hidden = expand_weight_1.shape[1]
    grad_w1, grad_w2, grad_b1 = summed_feed[:width], summed_feed[width : width + hidden], summed_feed[width + hidden]
    grad_qkv = summed[: 3 * local].T.reshape(width, 3, local)
    own = summed[3 * local : 8 * local].reshape(5, local, width)
    small = summed[8 * local : 8 * local + 16]
    bqkv = summed[8 * local + 16, : 3 * local].reshape(3, local)

    def mine(row):
        return lax.dynamic_slice_in_dim(row, index * local, local, 0)

    return (
        layer_output[None],
        grad_input[None],
        grad_memory,
        jnp.stack([small[0], small[2], small[6]]),
        jnp.stack([small[1], small[3], small[7]]),
        grad_qkv,
        bqkv,
        own[1],
        jnp.stack([small[4], small[9], small[8]]),
        own[0].T,
        mine(small[5]),
        jnp.stack([own[2].T, own[3].T], 1),
        mine(small[10]),
        own[4],
        grad_w1,
        grad_b1,
        grad_w2,
    )


def solution(mesh):
    return jax.shard_map(
        shards,
        mesh=mesh,
        in_specs=(
            P("dp", "tp", None),
            P(),
            P(),
            P(None, None, "tp"),
            P(None, "tp"),
            P("tp", None),
            P(),
            P(None, "tp"),
            P("tp"),
            P(None, None, "tp"),
            P("tp"),
            P("tp", None),
            P(None, "tp"),
            P("tp"),
            P("tp", None),
            P("dp", "tp", None, None),
            P("dp", None),
            P("dp", None),
            P("dp", "tp", None),
        ),
        out_specs=(
            P("dp", "tp", None),
            P("dp", "tp", None),
            P("dp", "tp", None, None),
            P(),
            P(),
            P(None, None, "tp"),
            P(None, "tp"),
            P("tp", None),
            P(),
            P(None, "tp"),
            P("tp"),
            P(None, None, "tp"),
            P("tp"),
            P("tp", None),
            P(None, "tp"),
            P("tp"),
            P("tp", None),
        ),
        check_vma=False,
    )
```

```python
import functools
import math

import jax
import jax.numpy as jnp
import numpy as np
from jax import lax
from jax.experimental import pallas as pl
from jax.experimental.pallas import tpu as pltpu
from jax.sharding import PartitionSpec as P

HEAD_DIM = 64
SPAN = 64
LANES = 128
QUERY_ROWS = 256
NEGATIVE = -1e30
NORM_EPS = 1e-05
BF = jnp.bfloat16
F32 = jnp.float32
VMEM_BYTES = 56 * 1024 * 1024

COST_US = {
    "prepare": 3.4,
    "qkv": 6.6,
    "attend": 18,
    "after_attend": 6,
    "memory_near": 12,
    "memory_far": 5,
    "cross": 6,
    "feed_near": 6.2,
    "feed_far": 6.2,
    "feed_weight": 11.4,
    "middle_back": 17.5,
    "cross_weight": 17.8,
    "attend_back": 25,
    "qkv_weight": 7.5,
    "input_back": 5.7,
    "block_grad": 6.8,
    "input_grad": 4,
    "return_blocks": 6,
}

DOCS = 5
MASK_LANE = HEAD_DIM
LSE_LANE = HEAD_DIM + DOCS


def nn(a, b):
    return lax.dot_general(a, b, (((1,), (0,)), ((), ())), preferred_element_type=F32)


def nt(a, b):
    return lax.dot_general(a, b, (((1,), (1,)), ((), ())), preferred_element_type=F32)


def tn(a, b):
    return lax.dot_general(a, b, (((0,), (0,)), ((), ())), preferred_element_type=F32)


def call(body, name, grid, in_specs, out_specs, out_shape, args, scratch=(), prefetch=0, aliases=None):
    return pl.pallas_call(
        body,
        out_shape=out_shape,
        grid_spec=pltpu.PrefetchScalarGridSpec(
            num_scalar_prefetch=prefetch,
            grid=grid,
            in_specs=in_specs,
            out_specs=out_specs,
            scratch_shapes=list(scratch),
        ),
        compiler_params=pltpu.CompilerParams(
            vmem_limit_bytes=VMEM_BYTES, dimension_semantics=("arbitrary",) * len(grid)
        ),
        cost_estimate=pl.CostEstimate(flops=int(COST_US[name.rstrip("_0123")] * 1e7), bytes_accessed=1, transcendentals=0),
        name=name,
        input_output_aliases=aliases or {},
    )(*args)


def whole(array):
    zeros = (0,) * len(array.shape)
    return pl.BlockSpec(array.shape, lambda *_: zeros)


def rows_of(tile, width):
    return pl.BlockSpec((tile, width), lambda i, *_: (i, 0))


def shape_of(shape, dtype):
    return jax.ShapeDtypeStruct(shape, dtype)


def standardize(values):
    centre = values - jnp.mean(values, -1, keepdims=True)
    inverse = lax.rsqrt(jnp.mean(centre * centre, -1, keepdims=True) + NORM_EPS)
    return centre * inverse, inverse


def norm_pull(grad, normed, inverse, gain):
    scaled = grad * gain
    return inverse * (
        scaled
        - jnp.mean(scaled, -1, keepdims=True)
        - normed * jnp.mean(scaled * normed, -1, keepdims=True)
    )


def column_sum(values):
    return jnp.sum(values, 0, keepdims=True)


def add_rows(out_ref, rows):
    @pl.when(pl.program_id(0) == 0)
    def _():
        out_ref[...] = jnp.zeros_like(out_ref)

    for index, row in enumerate(rows):
        out_ref[index : index + 1, :] += row


def follow(operand, earlier):
    return lax.optimization_barrier((operand, earlier))


def collect(parts, partners, earlier=None):
    core, chip, _ = partners
    far = lax.ppermute(parts[3], "tp", core)
    near = lax.ppermute(parts[1], "tp", core)
    sent = rounded_sum(parts[2], far)
    if earlier is not None:
        sent, earlier = follow(sent, earlier)
    return [parts[0], near, lax.ppermute(sent, "tp", chip)], earlier


def take_rows(values, part, rows):
    return lax.dynamic_slice_in_dim(values, part * rows, rows, 0)


def rounded_sum(*parts):
    return sum(part.astype(F32) for part in parts).astype(BF)


def swap(values, step, size):
    return lax.ppermute(values, "dp", [(i, i ^ step) for i in range(size)])


def sum_beside(values, size):
    device = lax.axis_index("dp")
    x, z = device & 1, device >> 1
    half = values.shape[0] // 2
    quarter = half // 4
    got = swap(take_rows(values, 1 - x, half), 1, size)
    part = rounded_sum(take_rows(values, x, half), got)
    got = [swap(take_rows(part, z ^ k, quarter), 2 * k, size) for k in (1, 2, 3)]
    own = rounded_sum(take_rows(part, z, quarter), *got)
    line = jnp.stack([own] + [swap(own, 2 * k, size) for k in (1, 2, 3)])
    both = jnp.concatenate([line, swap(line, 1, size)], 0)
    order = [(x ^ (i >> 2)) * 4 + (z ^ (i & 3)) for i in range(8)]
    return jnp.concatenate([lax.dynamic_index_in_dim(both, i, 0, keepdims=False) for i in order], 0)


def sum_along(values, size):
    device = lax.axis_index("dp")
    x, z = device & 1, device >> 1
    quarter = values.shape[0] // 4
    half = quarter // 2
    got = [swap(take_rows(values, z ^ k, quarter), 2 * k, size) for k in (1, 2, 3)]
    part = rounded_sum(take_rows(values, z, quarter), *got)
    own = rounded_sum(take_rows(part, x, half), swap(take_rows(part, 1 - x, half), 1, size))
    pair = jnp.stack([own, swap(own, 1, size)])
    both = jnp.concatenate([pair] + [swap(pair, 2 * k, size) for k in (1, 2, 3)], 0)
    order = [(z ^ (i >> 1)) * 2 + (x ^ (i & 1)) for i in range(8)]
    return jnp.concatenate([lax.dynamic_index_in_dim(both, i, 0, keepdims=False) for i in order], 0)


def sum_over_dp(values):
    size = lax.axis_size("dp")
    rows = values.shape[0]
    if size != 8:
        return lax.psum(values, "dp")
    unit = 8 * 16
    if rows <= 5 * unit:
        values = jnp.pad(values, ((0, -rows % unit), (0, 0)))
        return sum_beside(values, size)[:rows]
    first = -(-(rows * 5 // 8) // unit) * unit
    second = -(-(rows - first) // unit) * unit
    values = jnp.pad(values, ((0, first + second - rows), (0, 0)))
    return jnp.concatenate([sum_beside(values[:first], size), sum_along(values[first:], size)], 0)[:rows]


def exchange(parts, partners):
    return [parts[0]] + [lax.ppermute(parts[r], "tp", partners[r - 1]) for r in (1, 2, 3)]


def gather_rows(t_ref, refs, target, start=0):
    @pl.when(pl.program_id(0) == 0)
    def _():
        for rel, ref in enumerate(refs):
            count = ref.shape[0]
            target[pl.ds(pl.multiple_of((t_ref[0] ^ rel) * count + start, 16), count), :] = ref[...]


def gather_bias(t_ref, refs, start, local):
    rows = [ref[...].astype(F32)[0:1] for ref in refs]
    rows = [row[:, start : start + local] + row[:, start + local : start + 2 * local] for row in rows]
    groups = []
    for group in range(4):
        groups.append(sum(jnp.where(t_ref[0] ^ rel == group, row, 0.0) for rel, row in enumerate(rows)))
    return jnp.concatenate(groups, 1)


def pack_rows(local, width, part):
    return [pl.BlockSpec((local, width), lambda i, *_: (part, 0))] * 4


def prepare_body(qkv_ref, cq_ref, so_ref, kv_ref, co_ref, bq_ref, bv_ref, w_ref, pack_ref):
    local, width = so_ref.shape
    zeros = jnp.zeros((LANES - HEAD_DIM, width), BF)
    for j in range(3 * local // HEAD_DIM):
        part = qkv_ref[j * HEAD_DIM // local, j * HEAD_DIM % local : j * HEAD_DIM % local + HEAD_DIM, :]
        w_ref[j * LANES : j * LANES + HEAD_DIM, :] = part
        w_ref[j * LANES + HEAD_DIM : (j + 1) * LANES, :] = zeros
    for index, part in enumerate((cq_ref[...], so_ref[...], kv_ref[0], kv_ref[1], co_ref[...])):
        pack_ref[index * local : (index + 1) * local, :] = part
    parts = []
    for ref in (bq_ref, bv_ref):
        high = ref[...].astype(BF).astype(F32)
        parts += [high, ref[...] - high]
    row = jnp.concatenate(parts, 1)
    count = pack_ref.shape[0] - 5 * local
    first = lax.broadcasted_iota(jnp.int32, (count, width), 0) == 0
    pack_ref[5 * local :, :] = jnp.where(first, row, 0.0).astype(BF)


def prepare(qkv, cq, so, kv, co, bq, bv, pack_size):
    local, width = so.shape
    outs = [shape_of((3 * local // HEAD_DIM * LANES, width), BF), shape_of((pack_size, width), BF)]
    args = (qkv, cq, so, kv, co, bq, bv)
    return call(prepare_body, "prepare", (1,), [whole(a) for a in args], [whole(o) for o in outs], outs, args)


def qkv_body(t_ref, xa, xb, gain_ref, shift_ref, w_ref, b_ref, ca, sa, ta, cb, sb, tb, aa, ab, oa, ob):
    heads = oa.shape[1]
    for x_ref, cos_ref, left_ref, right_ref, a_ref, out_ref in ((xa, ca, sa, ta, aa, oa), (xb, cb, sb, tb, ab, ob)):
        normed, _ = standardize(x_ref[...].astype(F32))
        a = (normed * gain_ref[0:1, :] + shift_ref[0:1, :]).astype(BF)
        a_ref[...] = a
        proj = nt(a, w_ref[...]) + b_ref[...]
        cos, left, right = cos_ref[...], left_ref[...], right_ref[...]
        for j in range(3 * heads):
            part = proj[:, j * LANES : (j + 1) * LANES]
            if j < 2 * heads:
                part = part * cos + pltpu.roll(part, 96, 1) * left + pltpu.roll(part, 32, 1) * right
            if j < heads:
                part = part * (1.0 / math.sqrt(HEAD_DIM))
            out_ref[j // heads, j % heads] = part.astype(BF)


def project_rows(rels, t, xs, gain, shift, w, b, tables, heads):
    rows, width = xs[0].shape
    tile = min(256, rows)
    steps = rows // tile

    def table(rel):
        return pl.BlockSpec((tile, LANES), lambda i, t_ref: ((t_ref[0] ^ rel) * steps + i, 0))

    row = rows_of(tile, width)
    out = pl.BlockSpec((3, heads, tile, LANES), lambda i, t_ref: (0, 0, i, 0))
    return call(
        qkv_body,
        f"qkv_{rels[0]}{rels[1]}",
        (steps,),
        [row, row, whole(gain), whole(shift), whole(w), whole(b)] + [table(rels[0])] * 3 + [table(rels[1])] * 3,
        [row, row, out, out],
        [shape_of((rows, width), BF)] * 2 + [shape_of((3, heads, rows, LANES), BF)] * 2,
        (t, *xs, gain, shift, w, b, *tables, *tables),
        prefetch=1,
    )


def causal_corner(scores):
    keys = lax.broadcasted_iota(jnp.int32, scores.shape, 0)
    queries = lax.broadcasted_iota(jnp.int32, scores.shape, 1)
    return jnp.where(keys <= queries, scores, NEGATIVE)


def attend_body(t_ref, c0, c1, c2, c3, qx_ref, kx_ref, vx_ref, qe_ref, ke_ref, ve_ref, ot_ref, lse_ref, vt_ref):
    t = t_ref[0]
    rows = c0.shape[2]
    for rel, chunk in enumerate((c0, c1, c2, c3)):
        place = pl.ds(pl.multiple_of((t ^ rel) * rows, rows), rows)
        qe_ref[0, place, :] = chunk[0, 0] + qx_ref[place, :]
        ke_ref[0, place, :] = chunk[1, 0] + kx_ref[place, :]
        values = chunk[2, 0] + vx_ref[...]
        ve_ref[0, place, :] = values
        vt_ref[:, place] = values.astype(F32).T.astype(BF)
    step = QUERY_ROWS
    for low in range(0, qe_ref.shape[1], step):
        high = low + step
        query = qe_ref[0, low:high, :]
        corner = causal_corner(nt(ke_ref[0, low:high, :], query))
        top = jnp.max(corner, 0, keepdims=True)
        if low:
            earlier = nt(ke_ref[0, :low, :], query)
            top = jnp.maximum(top, jnp.max(earlier, 0, keepdims=True))
        mixed = nn(vt_ref[:, low:high], jnp.exp(corner - top).astype(BF))
        if low:
            mixed = mixed + nn(vt_ref[:, :low], jnp.exp(earlier - top).astype(BF))
        total = mixed[HEAD_DIM : HEAD_DIM + 1, :]
        lse_ref[0, :, low:high] = top + jnp.log(total)
        begin = low % rows
        ot_ref[t ^ (low // rows), :, begin : begin + step] = (mixed[:HEAD_DIM] / total).astype(BF)


def attend(t, chunks, qx, kx, vx):
    _, heads, rows, _ = chunks[0].shape
    length = qx.shape[0]
    chunk = pl.BlockSpec((3, 1, rows, LANES), lambda h, t_ref: (0, h, 0, 0))
    plane = pl.BlockSpec((1, length, LANES), lambda h, t_ref: (h, 0, 0))
    padded = shape_of((heads, length, LANES), BF)
    return call(
        attend_body,
        "attend",
        (heads,),
        [chunk] * 4 + [whole(qx), whole(kx), whole(vx)],
        [
            plane,
            plane,
            plane,
            pl.BlockSpec((4, HEAD_DIM, rows), lambda h, t_ref: (0, h, 0)),
            pl.BlockSpec((1, 1, length), lambda h, t_ref: (h, 0, 0)),
        ],
        [padded, padded, padded, shape_of((4, heads * HEAD_DIM, rows), BF), shape_of((heads, 1, length), F32)],
        (t, *chunks, qx, kx, vx),
        scratch=[pltpu.VMEM((LANES, length), BF)],
        prefetch=1,
    )


def three_parts(values):
    first = values.astype(BF).astype(F32)
    second = (values - first).astype(BF).astype(F32)
    return first, second, values - first - second


def attend_back_body(
    t_ref, qe_ref, ke_ref, ve_ref, d0, d1, d2, d3, ot_ref, lse_ref, cos_ref, sa_ref, sb_ref, out_ref,
    qt_ref, kt_ref, dt_ref, dk_ref, dv_ref,
):
    t = t_ref[0]
    rows = d0.shape[1]
    step = QUERY_ROWS
    length = qe_ref.shape[1]
    for rel, chunk in enumerate((d0, d1, d2, d3)):
        place = pl.ds(pl.multiple_of((t ^ rel) * rows, rows), rows)
        grad = chunk[...].astype(F32)
        delta = three_parts(jnp.sum(grad * ot_ref[rel].astype(F32), 0, keepdims=True))
        padded = jnp.concatenate([grad, jnp.zeros_like(grad)], 0)
        row = lax.broadcasted_iota(jnp.int32, padded.shape, 0)
        for index in range(3):
            padded = jnp.where(row == HEAD_DIM + index, -delta[index], padded)
        dt_ref[:, place] = padded.astype(BF)
    for low in range(0, length, rows):
        high = low + rows
        kt_ref[:, low:high] = ke_ref[0, low:high, :].astype(F32).T.astype(BF)
        turned = qe_ref[0, low:high, :].astype(F32).T
        row = lax.broadcasted_iota(jnp.int32, turned.shape, 0)
        pieces = three_parts(lse_ref[0, :, low:high])
        for index in range(3):
            turned = jnp.where(row == LSE_LANE + index, -pieces[index], turned)
        qt_ref[:, low:high] = turned.astype(BF)
    dk_ref[...] = jnp.zeros_like(dk_ref)
    dv_ref[...] = jnp.zeros_like(dv_ref)

    def unrotate(grad, place):
        return (
            grad * cos_ref[place, :]
            - pltpu.roll(grad, 96, 1) * sa_ref[place, :]
            - pltpu.roll(grad, 32, 1) * sb_ref[place, :]
        )

    for low in range(0, length, step):
        high = low + step
        query, query_t, grad_t = qe_ref[0, low:high, :], qt_ref[:, low:high], dt_ref[:, low:high]
        dq_t = None
        for begin, end in ((0, low), (low, high)):
            if begin == end:
                continue
            scores = nn(ke_ref[0, begin:end, :], query_t)
            if begin == low:
                scores = causal_corner(scores)
            prob = jnp.exp(scores)
            grad_scores = (prob * nn(ve_ref[0, begin:end, :], grad_t)).astype(BF)
            dv_ref[begin:end, :] += nt(prob.astype(BF), grad_t)
            dk_ref[begin:end, :] += nn(grad_scores, query)
            part = nn(kt_ref[:, begin:end], grad_scores)
            dq_t = part if dq_t is None else dq_t + part
        start = low % rows
        grad_query = unrotate(dq_t.T, slice(low, high)) * (1.0 / math.sqrt(HEAD_DIM))
        out_ref[t ^ (low // rows), 0, 0, start : start + step, :] = grad_query.astype(BF)
    for low in range(0, length, rows):
        place = slice(low, low + rows)
        rel = t ^ (low // rows)
        out_ref[rel, 1, 0] = unrotate(dk_ref[place, :], place).astype(BF)
        lane = lax.broadcasted_iota(jnp.int32, (rows, LANES), 1)
        out_ref[rel, 2, 0] = jnp.where(lane < HEAD_DIM, dv_ref[place, :], 0.0).astype(BF)


def attend_back(t, qe, ke, ve, grads, ot, lse, tables):
    heads, length, _ = qe.shape
    rows = grads[0].shape[1]
    plane = pl.BlockSpec((1, length, LANES), lambda h, t_ref: (h, 0, 0))
    grad = pl.BlockSpec((HEAD_DIM, rows), lambda h, t_ref: (h, 0))
    return call(
        attend_back_body,
        "attend_back",
        (heads,),
        [plane] * 3
        + [grad] * 4
        + [
            pl.BlockSpec((4, HEAD_DIM, rows), lambda h, t_ref: (0, h, 0)),
            pl.BlockSpec((1, 1, length), lambda h, t_ref: (h, 0, 0)),
        ]
        + [whole(table) for table in tables],
        pl.BlockSpec((4, 3, 1, rows, LANES), lambda h, t_ref: (0, 0, h, 0, 0)),
        shape_of((4, 3, heads, rows, LANES), BF),
        (t, qe, ke, ve, *grads, ot, lse, *tables),
        scratch=[pltpu.VMEM((LANES, length), BF)] * 3 + [pltpu.VMEM((length, LANES), F32)] * 2,
        prefetch=1,
    )


def input_back_body(xa, xb, da, db, w_ref, oa, ob, small_ref):
    heads = da.shape[2]
    totals = []
    for x_ref, dp_ref, out_ref in ((xa, da, oa), (xb, db, ob)):
        grads = jnp.concatenate([dp_ref[0, j // heads, j % heads] for j in range(3 * heads)], 1)
        grad = nn(grads, w_ref[...])
        normed, _ = standardize(x_ref[...].astype(F32))
        out_ref[...] = grad.astype(BF)
        totals.append((column_sum(grad * normed), column_sum(grad)))
    add_rows(small_ref, [totals[0][0] + totals[1][0], totals[0][1] + totals[1][1]])


def input_back(rels, xs, dp, w):
    rows, width = xs[0].shape
    heads = dp.shape[2]
    tile = min(256, rows)
    row = rows_of(tile, width)

    def part(rel):
        return pl.BlockSpec((1, 3, heads, tile, LANES), lambda i: (rel, 0, 0, i, 0))

    return call(
        input_back_body,
        f"input_back_{rels[0]}{rels[1]}",
        (rows // tile,),
        [row, row, part(rels[0]), part(rels[1]), whole(w)],
        [row, row, pl.BlockSpec((8, width), lambda i: (0, 0))],
        [shape_of((rows, width), BF)] * 2 + [shape_of((8, width), F32)],
        (*xs, dp, dp, w),
    )


def qkv_weight_body(dp_ref, a0, a1, a2, a3, out_ref, bias_ref):
    heads = dp_ref.shape[2]
    total, sums = None, None
    for rel, a_ref in enumerate((a0, a1, a2, a3)):
        grads = jnp.concatenate([dp_ref[rel, 0, h] for h in range(heads)], 1)
        part, part_sum = tn(grads, a_ref[...]), column_sum(grads.astype(F32))
        total = part if total is None else total + part
        sums = part_sum if sums is None else sums + part_sum
    for h in range(heads):
        out_ref[h * HEAD_DIM : (h + 1) * HEAD_DIM, :] = total[h * LANES : h * LANES + HEAD_DIM].astype(BF)
    bias_ref[0] = sums


def qkv_weight(dp, normed):
    _, _, heads, rows, _ = dp.shape
    width = normed[0].shape[1]
    local = heads * HEAD_DIM
    return call(
        qkv_weight_body,
        "qkv_weight",
        (3,),
        [pl.BlockSpec((4, 1, heads, rows, LANES), lambda j: (0, j, 0, 0, 0))] + [whole(a) for a in normed],
        [rows_of(local, width), pl.BlockSpec((1, 1, heads * LANES), lambda j: (j, 0, 0))],
        [shape_of((3 * local, width), BF), shape_of((3, 1, heads * LANES), F32)],
        (dp, *normed),
    )


def after_attend_body(
    t_ref, x_ref, o0, o1, o2, o3, w0, w1, w2, w3, q0, q1, q2, q3, b0, b1, b2, b3, bias_ref, gain_ref, shift_ref,
    x1_ref, b_ref, cq_ref, wq_ref,
):
    gather_rows(t_ref, (q0, q1, q2, q3), wq_ref)
    total = x_ref[...].astype(F32) + bias_ref[0:1, :]
    for o_ref, w_ref in ((o0, w0), (o1, w1), (o2, w2), (o3, w3)):
        total = total + tn(o_ref[...], w_ref[...])
    x1_ref[...] = total
    normed, _ = standardize(total)
    b = (normed * gain_ref[1:2, :] + shift_ref[1:2, :]).astype(BF)
    b_ref[...] = b
    bias = gather_bias(t_ref, (b0, b1, b2, b3), 0, w0.shape[0])
    cq_ref[...] = ((nt(b, wq_ref[...]) + bias) * (1.0 / math.sqrt(HEAD_DIM))).astype(BF)


def after_attend(t, x, mixed, packs, out_bias, gain, shift):
    rows, width = x.shape
    local = mixed[0].shape[0]
    tile = min(256, rows)
    return call(
        after_attend_body,
        "after_attend",
        (rows // tile,),
        [rows_of(tile, width)]
        + [pl.BlockSpec((local, tile), lambda i, *_: (0, i))] * 4
        + pack_rows(local, width, 1)
        + pack_rows(local, width, 0)
        + pack_rows(16, width, 5 * local // 16)
        + [whole(out_bias), whole(gain), whole(shift)],
        [rows_of(tile, width)] * 3,
        [shape_of((rows, width), F32), shape_of((rows, width), BF), shape_of((rows, width), BF)],
        (t, x, *mixed, *packs, *packs, *packs, out_bias, gain, shift),
        scratch=[pltpu.VMEM((width, width), BF)],
        prefetch=1,
    )


def split_pair(values):
    lane = lax.broadcasted_iota(jnp.int32, values.shape, 1)
    zero = jnp.zeros_like(values)
    return jnp.concatenate(
        [jnp.where(lane < HEAD_DIM, values, zero), jnp.where(lane >= HEAD_DIM, values, zero)], 0
    )


def join_pair(values):
    rows = values.shape[0] // 2
    lane = lax.broadcasted_iota(jnp.int32, (rows, values.shape[1]), 1)
    return jnp.where(lane < HEAD_DIM, values[:rows], values[rows:])


def lane_cuts(width):
    return [slice(start, start + LANES) for start in range(0, width, LANES)]


def cross_body(
    t_ref, cq_ref, kv_ref, x1_ref, w0, w1, w2, w3, bias_ref, gain_ref, shift_ref, co_ref, lse_ref, x2_ref, m_ref, w_ref
):
    gather_rows(t_ref, (w0, w1, w2, w3), w_ref)
    width = cq_ref.shape[1]
    spans, side, _ = lse_ref.shape
    keys = kv_ref.shape[0] // spans
    cuts = lane_cuts(width)
    for span in range(spans):
        place = slice(span * SPAN, (span + 1) * SPAN)
        query = cq_ref[place, :]
        key, value = kv_ref[span * keys : (span + 1) * keys, :width], kv_ref[span * keys : (span + 1) * keys, width:]
        scores = [nt(key[:, cut], split_pair(query[:, cut])) for cut in cuts]
        tops = [jnp.max(score, 0, keepdims=True) for score in scores]
        shifted = [jnp.exp(score - top) for score, top in zip(scores, tops)]
        totals = [jnp.sum(part, 0, keepdims=True) for part in shifted]
        probs = [(part * (1.0 / total)).astype(BF) for part, total in zip(shifted, totals)]
        mixed = [join_pair(tn(prob, value[:, cut])) for prob, cut in zip(probs, cuts)]
        co_ref[place, :] = jnp.concatenate(mixed, 1).astype(BF)
        rows = [top + jnp.log(total) for top, total in zip(tops, totals)]
        lse_ref[span] = jnp.concatenate(rows + [jnp.zeros((side - len(rows), LANES), F32)], 0)
    total = x1_ref[...] + nn(co_ref[...], w_ref[...]) + bias_ref[1:2, :]
    x2_ref[...] = total
    normed, _ = standardize(total)
    m_ref[...] = (normed * gain_ref[2:3, :] + shift_ref[2:3, :]).astype(BF)


def cross(t, half, cq, kv, x1, packs, local, out_bias, gain, shift):
    rows, width = x1.shape
    tile = rows // 2
    ratio = kv.shape[0] // rows
    side = -(-(width // LANES) // 8) * 8
    spans = tile // SPAN

    def rows_at(count, columns):
        return pl.BlockSpec((count, columns), lambda i, *_: (half, 0))

    row = rows_at(tile, width)
    outs = [
        shape_of((tile, width), BF),
        shape_of((spans, side, LANES), F32),
        shape_of((tile, width), F32),
        shape_of((tile, width), BF),
    ]
    return call(
        cross_body,
        f"cross_{half}",
        (1,),
        [row, rows_at(ratio * tile, 2 * width), row]
        + pack_rows(local, width, 4)
        + [whole(out_bias), whole(gain), whole(shift)],
        [whole(out) for out in outs],
        outs,
        (t, cq, kv, x1, *packs, out_bias, gain, shift),
        scratch=[pltpu.VMEM((width, width), BF)],
        prefetch=1,
    )


def middle_back_body(
    t_ref, x2a, x2b, da0, da1, da2, db0, db1, db2, lsea, lseb, g_ref, gain_ref, cq_ref, kv_ref, x1_ref,
    c0, c1, c2, c3, q0, q1, q2, q3, w0, w1, w2, w3,
    g2r_ref, dkv_ref, g1_ref, g1r_ref, dqc_ref, d0, d1, d2, d3, small_ref,
    dco_ref, dq_ref, x2_ref, dm_ref, lse_ref, co_w_ref, wq_ref,
):
    gather_rows(t_ref, (c0, c1, c2, c3), co_w_ref)
    gather_rows(t_ref, (q0, q1, q2, q3), wq_ref)
    for side, (x2, parts, lse) in enumerate(((x2a, (da0, da1, da2), lsea), (x2b, (db0, db1, db2), lseb))):

        @pl.when(pl.program_id(0) == side)
        def _(x2=x2, parts=parts, lse=lse):
            x2_ref[...] = x2[...]
            dm_ref[...] = sum(part[...].astype(F32) for part in parts)
            lse_ref[...] = lse[...]

    width = cq_ref.shape[1]
    spans = lse_ref.shape[0]
    keys = kv_ref.shape[0] // spans
    cuts = lane_cuts(width)
    grad_m = dm_ref[...]
    normed_m, inverse = standardize(x2_ref[...])
    g = g_ref[...]
    g2 = g + norm_pull(grad_m, normed_m, inverse, gain_ref[2:3, :])
    g2r = g2.astype(BF)
    g2r_ref[...] = g2r
    dco_ref[...] = nt(g2r, co_w_ref[...]).astype(BF)
    for span in range(spans):
        place = slice(span * SPAN, (span + 1) * SPAN)
        block = slice(span * keys, (span + 1) * keys)
        query, grad = cq_ref[place, :], dco_ref[place, :]
        key, value = kv_ref[block, :width], kv_ref[block, width:]
        stats = lse_ref[span]
        queries = [split_pair(query[:, cut]) for cut in cuts]
        grads = [split_pair(grad[:, cut]) for cut in cuts]
        probs = [jnp.exp(nt(key[:, cut], q) - stats[j : j + 1]) for j, (cut, q) in enumerate(zip(cuts, queries))]
        pulls = [nt(value[:, cut], part) for cut, part in zip(cuts, grads)]
        deltas = [jnp.sum(prob * pull, 0, keepdims=True) for prob, pull in zip(probs, pulls)]
        scores = [(prob * (pull - delta)).astype(BF) for prob, pull, delta in zip(probs, pulls, deltas)]
        keys_back = [nn(score, q).astype(BF) for score, q in zip(scores, queries)]
        values_back = [nn(prob.astype(BF), part).astype(BF) for prob, part in zip(probs, grads)]
        dkv_ref[block, :] = jnp.concatenate(keys_back + values_back, 1)
        dq_ref[place, :] = jnp.concatenate([join_pair(tn(score, key[:, cut])) for score, cut in zip(scores, cuts)], 1)
    dqc = (dq_ref[...] * (1.0 / math.sqrt(HEAD_DIM))).astype(BF)
    dqc_ref[...] = dqc
    grad_b = nn(dqc, wq_ref[...])
    normed_b, inverse = standardize(x1_ref[...])
    g1 = g2 + norm_pull(grad_b, normed_b, inverse, gain_ref[1:2, :])
    g1_ref[...] = g1
    g1r = g1.astype(BF)
    g1r_ref[...] = g1r
    for w_ref, d_ref in ((w0, d0), (w1, d1), (w2, d2), (w3, d3)):
        d_ref[...] = nt(w_ref[...], g1r).astype(BF)
    add_rows(
        small_ref,
        [
            column_sum(grad_b * normed_b),
            column_sum(grad_b),
            column_sum(grad_m * normed_m),
            column_sum(grad_m),
            column_sum(g1),
            column_sum(g2),
            column_sum(g),
            column_sum(dqc.astype(F32)),
            column_sum(dkv_ref[:, width:].astype(F32)),
        ],
    )


def middle_back(t, x2, dm, lse, g, packs, local, gain, cq, kv, x1):
    rows, width = x1.shape
    tile = rows // 2
    ratio = kv.shape[0] // rows
    row = rows_of(tile, width)
    wide = rows_of(ratio * tile, 2 * width)
    turned = pl.BlockSpec((local, tile), lambda i, *_: (0, i))
    half = shape_of((rows, width), BF)
    halves = (*x2, *dm[0], *dm[1], *lse)
    return call(
        middle_back_body,
        "middle_back",
        (2,),
        [whole(value) for value in halves]
        + [row, whole(gain), row, wide, row]
        + pack_rows(local, width, 4)
        + pack_rows(local, width, 0)
        + pack_rows(local, width, 1),
        [row, wide, row, row, row] + [turned] * 4 + [pl.BlockSpec((16, width), lambda i, *_: (0, 0))],
        [half, shape_of(kv.shape, BF), shape_of((rows, width), F32), half, half]
        + [shape_of((local, rows), BF)] * 4
        + [shape_of((16, width), F32)],
        (t, *halves, g, gain, cq, kv, x1, *packs, *packs, *packs),
        scratch=[
            pltpu.VMEM((tile, width), BF),
            pltpu.VMEM((tile, width), F32),
            pltpu.VMEM((tile, width), F32),
            pltpu.VMEM((tile, width), F32),
            pltpu.VMEM(lse[0].shape, F32),
            pltpu.VMEM((width, width), BF),
            pltpu.VMEM((width, width), BF),
        ],
        prefetch=1,
    )


def block_place(block, blocks, t, piece):
    rel, start, count = piece
    inside = block % blocks - start
    held = ((block // blocks) ^ t == rel) & (inside >= 0) & (inside < count)
    return held, jnp.where(held, inside, 0)


def anywhere():
    return pl.BlockSpec(memory_space=pl.ANY)


def fetch_block(t_ref, block, blocks, refs, pieces, target, semaphore):
    found = False
    for ref, piece in zip(refs, pieces):
        held, index = block_place(block, blocks, t_ref[0], piece)

        @pl.when(held)
        def _(ref=ref, index=index):
            pltpu.make_async_copy(ref.at[index], target, semaphore).start()

        found = held | found
    return found


def gather_pair(t_ref, refs, target):
    width = target.shape[1]
    local = refs[0].shape[0] // 2
    gather_rows(t_ref, [ref.at[:local, :] for ref in refs], target)
    gather_rows(t_ref, [ref.at[local:, :] for ref in refs], target, width)


def memory_body(t_ref, id_ref, *refs, pieces, first):
    count = len(pieces)
    packs, biases = refs[count : count + 4], refs[count + 4 : count + 8]
    kv_ref, chosen_ref, w_ref, x_ref, out_ref, in_sem, kv_sem, out_sem = refs[count + 8 + (0 if first else 2) :]
    blocks, length, width = x_ref.shape
    held = [
        fetch_block(t_ref, id_ref[slot], blocks, refs, pieces, x_ref.at[slot], in_sem.at[slot])
        for slot in range(blocks)
    ]
    gather_pair(t_ref, packs, w_ref)
    local = packs[0].shape[0] // 2
    bias = gather_bias(t_ref, biases, 2 * local, local)

    def copies(slot):
        rows = pl.ds(slot * length, length)
        return (
            pltpu.make_async_copy(out_ref.at[slot], kv_ref.at[rows, :], kv_sem.at[slot]),
            pltpu.make_async_copy(x_ref.at[slot], chosen_ref.at[rows, :], out_sem.at[slot]),
        )

    for slot in range(blocks):

        @pl.when(held[slot])
        def _(slot=slot):
            pltpu.make_async_copy(refs[0].at[0], x_ref.at[slot], in_sem.at[slot]).wait()
            kv = nt(x_ref[slot], w_ref[...])
            out_ref[slot, :, :width] = kv[:, :width].astype(BF)
            out_ref[slot, :, width:] = (kv[:, width:] + bias).astype(BF)
            for copy in copies(slot):
                copy.start()

    for slot in range(blocks):

        @pl.when(held[slot])
        def _(slot=slot):
            for copy in copies(slot):
                copy.wait()


def memory_rows(name, t, ids, memories, pieces, packs, local, earlier=None):
    blocks = ids.shape[0]
    _, length, width = memories[0].shape
    outs = [shape_of((blocks * length, 2 * width), BF), shape_of((blocks * length, width), BF)]
    more = () if earlier is None else tuple(earlier)
    count = 2 + len(memories) + 8
    return call(
        functools.partial(memory_body, pieces=pieces, first=earlier is None),
        name,
        (1,),
        [anywhere()] * len(memories)
        + pack_rows(2 * local, width, 1)
        + pack_rows(16, width, 5 * local // 16)
        + [anywhere()] * len(more),
        [anywhere()] * 2,
        outs,
        (t, ids, *memories, *packs, *packs, *more),
        scratch=[
            pltpu.VMEM((2 * width, width), BF),
            pltpu.VMEM((blocks, length, width), BF),
            pltpu.VMEM((blocks, length, 2 * width), BF),
            pltpu.SemaphoreType.DMA((blocks,)),
            pltpu.SemaphoreType.DMA((blocks,)),
            pltpu.SemaphoreType.DMA((blocks,)),
        ],
        prefetch=2,
        aliases={count: 0, count + 1: 1} if more else {},
    )


def block_grad_body(t_ref, dkv_ref, w0, w1, w2, w3, out_ref, w_ref):
    gather_pair(t_ref, (w0, w1, w2, w3), w_ref)
    out_ref[...] = nn(dkv_ref[...], w_ref[...]).astype(BF).reshape(out_ref.shape)


def block_grad(t, half, dkv, packs, local, blocks):
    rows, width = dkv.shape[0], dkv.shape[1] // 2
    length = rows // blocks
    steps = blocks // 4
    return call(
        block_grad_body,
        f"block_grad_{half}",
        (steps,),
        [pl.BlockSpec((2 * length, 2 * width), lambda i, *_: (half * steps + i, 0))] + pack_rows(2 * local, width, 1),
        pl.BlockSpec((2, length, width), lambda i, *_: (i, 0, 0)),
        shape_of((blocks // 2, length, width), BF),
        (t, dkv, *packs),
        scratch=[pltpu.VMEM((2 * width, width), BF)],
        prefetch=1,
    )


def return_body(t_ref, id_ref, *refs, pieces):
    out_ref, x_ref, semaphores = refs[len(pieces) :]
    blocks = id_ref.shape[0]
    step, steps = pl.program_id(0), pl.num_programs(0)
    sides = x_ref.shape[1]

    def fetch(at):
        for side in range(sides):
            slot = at % 2
            block = id_ref[at * sides + side]
            fetch_block(t_ref, block, blocks, refs, pieces, x_ref.at[slot, side], semaphores.at[slot, side])

    @pl.when(step == 0)
    def _():
        fetch(0)

    @pl.when(step + 1 < steps)
    def _():
        fetch(step + 1)

    now = step % 2
    for side in range(sides):
        pltpu.make_async_copy(refs[0].at[0], x_ref.at[now, side], semaphores.at[now, side]).wait()
        out_ref[side] = x_ref[now, side].astype(out_ref.dtype)


def return_blocks(t, slots, grads, pieces):
    blocks = slots.shape[0]
    sides = 4
    _, length, width = grads[0].shape
    return call(
        functools.partial(return_body, pieces=pieces),
        "return_blocks",
        (blocks // sides,),
        [anywhere()] * len(grads),
        pl.BlockSpec((sides, length, width), lambda i, *_: (i, 0, 0)),
        shape_of((blocks, length, width), F32),
        (t, slots, *grads),
        scratch=[pltpu.VMEM((2, sides, length, width), BF), pltpu.SemaphoreType.DMA((2, sides))],
        prefetch=2,
    )


def feed_body(ma, mb, ga, gb, w1_ref, w2_ref, b1_ref, oa, ob, da, db, ha, hb, ua, ub, sum_ref):
    curve = math.sqrt(2.0 / math.pi)
    total = None
    for m_ref, g_ref, out_ref, dm_ref, h_ref, du_ref in ((ma, ga, oa, da, ha, ua), (mb, gb, ob, db, hb, ub)):
        u = nn(m_ref[...], w1_ref[...]) + b1_ref[...]
        square = u * u
        bent = jnp.tanh(curve * (u + 0.044715 * u * square))
        half = 0.5 * (1.0 + bent)
        h = (u * half).astype(BF)
        h_ref[...] = h
        slope = half + 0.5 * u * (1.0 - bent * bent) * (curve * (1.0 + 3.0 * 0.044715 * square))
        du = (nt(g_ref[...], w2_ref[...]) * slope).astype(BF)
        du_ref[...] = du
        dm_ref[...] = nt(du, w1_ref[...]).astype(BF)
        out_ref[...] = nn(h, w2_ref[...]).astype(BF)
        part = column_sum(du.astype(F32))
        total = part if total is None else total + part
    add_rows(sum_ref, [total])


def feed(name, half, ms, gs, w1, w2, b1):
    rows, width = ms[0].shape
    hidden = w1.shape[1]
    row, wide = shape_of((rows, width), BF), shape_of((rows, hidden), BF)
    outs = [row] * 4 + [wide] * 4 + [shape_of((8, hidden), F32)]
    return list(call(
        feed_body,
        name,
        (1,),
        [whole(row)] * 2 + [pl.BlockSpec((rows, width), lambda i: (half, 0))] * 2 + [whole(w1), whole(w2), whole(b1)],
        [whole(out) for out in outs],
        outs,
        (*ms, *gs, w1, w2, b1),
    ))


def feed_weight_body(*refs):
    out_ref = refs[-1]
    count = (len(refs) - 1) // 7
    ms, dus, hs, gs = refs[: 2 * count], refs[2 * count : 4 * count], refs[4 * count : 6 * count], refs[6 * count : -1]
    rows = dus[0].shape[0]
    half = pl.num_programs(0) // 2

    @pl.when(pl.program_id(0) < half)
    def _():
        out_ref[...] = sum(tn(m[...], du[...]) for m, du in zip(ms, dus)).astype(BF)

    @pl.when(pl.program_id(0) >= half)
    def _():
        total = 0.0
        for index, h in enumerate(hs):
            side = index % 2
            total = total + tn(h[...], gs[index // 2][side * rows : (side + 1) * rows, :])
        out_ref[...] = total.astype(BF)


def feed_weight(ms, dus, hs, gs):
    rows, width = ms[0].shape
    hidden = hs[0].shape[1]
    tile = 256
    first, second = width // tile, hidden // tile
    return call(
        feed_weight_body,
        "feed_weight",
        (first + second,),
        [pl.BlockSpec((rows, tile), lambda i: (0, jnp.minimum(i, first - 1)))] * len(ms)
        + [whole(r) for r in dus]
        + [pl.BlockSpec((rows, tile), lambda i: (0, jnp.maximum(i - first, 0)))] * len(hs)
        + [whole(r) for r in gs],
        rows_of(tile, width),
        shape_of((width + hidden, width), BF),
        (*ms, *dus, *hs, *gs),
    )


def cross_weight_body(t_ref, *refs):
    count = (len(refs) - 5) // 2
    sources, (out0, out1, out2, out3), buffers, semaphores = refs[:count], refs[count : count + 4], refs[count + 4 : -1], refs[-1]
    outs = (out0, out1, out2, out3)
    local, width = out0.shape[1:]
    copies = [
        pltpu.make_async_copy(source, buffer, semaphores.at[index])
        for index, (source, buffer) in enumerate(zip(sources, buffers))
    ]
    for copy in copies:
        copy.start()
    dqc, b, o0, o1, o2, o3, g1, co_a, co_b, g2, memory, dkv = buffers

    def place(index, grad):
        for group in range(4):
            part = grad[group * local : (group + 1) * local].astype(BF)
            for rel, out_ref in enumerate(outs):

                @pl.when(t_ref[0] ^ rel == group)
                def _(out_ref=out_ref, part=part):
                    out_ref[index] = part

    copies[0].wait()
    copies[1].wait()
    place(0, tn(dqc[...], b[...]))
    for copy in copies[2:7]:
        copy.wait()
    for out_ref, o_ref in zip(outs, (o0, o1, o2, o3)):
        out_ref[1] = nn(o_ref[...], g1[...]).astype(BF)
    for copy in copies[7:10]:
        copy.wait()
    half = co_a.shape[0]
    place(4, tn(co_a[...], g2[:half, :]) + tn(co_b[...], g2[half:, :]))
    copies[10].wait()
    copies[11].wait()
    place(2, tn(dkv[:, :width], memory[...]))
    place(3, tn(dkv[:, width:], memory[...]))


def cross_weight(t, dqc, b, mixed, g1r, dkv, memory, co, g2r):
    width = b.shape[1]
    local = mixed[0].shape[0]
    args = (dqc, b, *mixed, g1r, *co, g2r, memory, dkv)
    out = shape_of((5, local, width), BF)
    return call(
        cross_weight_body,
        "cross_weight",
        (1,),
        [anywhere()] * len(args),
        [whole(out)] * 4,
        [out] * 4,
        (t, *args),
        scratch=[pltpu.VMEM(a.shape, a.dtype) for a in args] + [pltpu.SemaphoreType.DMA((len(args),))],
        prefetch=1,
    )


def input_grad_body(x_ref, da_ref, db_ref, dc_ref, g1_ref, gain_ref, out_ref):
    normed, inverse = standardize(x_ref[...].astype(F32))
    grad = da_ref[...].astype(F32) + db_ref[...].astype(F32) + dc_ref[...].astype(F32)
    out_ref[...] = g1_ref[...] + norm_pull(grad, normed, inverse, gain_ref[0:1, :])


def input_grad(x, parts, g1, gain):
    rows, width = x.shape
    tile = min(256, rows)
    row = rows_of(tile, width)
    return call(
        input_grad_body,
        "input_grad",
        (rows // tile,),
        [row] * 5 + [whole(gain)],
        row,
        shape_of((rows, width), F32),
        (x, *parts, g1, gain),
    )


def padded_tables(length):
    half = HEAD_DIM // 2
    frequency = np.float32(10000.0) ** (-np.arange(half, dtype=np.float32) / np.float32(half))
    angles = np.arange(length, dtype=np.float32)[:, None] * frequency[None, :]
    cosine = np.cos(angles.astype(np.float64)).astype(np.float32)
    sine = np.sin(angles.astype(np.float64)).astype(np.float32)
    zero = np.zeros_like(sine)
    return (
        jnp.asarray(np.concatenate([cosine, cosine, zero, zero], 1)),
        jnp.asarray(np.concatenate([-sine, zero, zero, zero], 1)),
        jnp.asarray(np.concatenate([zero, sine, zero, zero], 1)),
    )


def mask_lanes(segments):
    lane = lax.broadcasted_iota(jnp.int32, (segments.shape[0], LANES), 1)
    is_mask = (lane >= MASK_LANE) & (lane < MASK_LANE + DOCS)
    same = is_mask & (lane - MASK_LANE == segments[:, None])
    is_lse = (lane >= LSE_LANE) & (lane < LSE_LANE + 3)
    query_lanes = jnp.where(same, 1.0, 0.0).astype(BF)
    key_lanes = jnp.where(is_mask & ~same, NEGATIVE, jnp.where(is_lse, 1.0, 0.0)).astype(BF)
    return query_lanes, key_lanes


def pad_heads(values):
    lead = values.shape[:-1]
    heads = values.shape[-1] // HEAD_DIM
    values = values.reshape(lead + (heads, HEAD_DIM))
    values = jnp.pad(values, [(0, 0)] * (len(lead) + 1) + [(0, LANES - HEAD_DIM)])
    return values.reshape(lead[:-1] + (-1,))


def shards(
    layer_input,
    norm_gain,
    norm_bias,
    self_input_weight,
    self_input_bias,
    self_output_weight,
    out_bias,
    cross_query_weight,
    b_cross_q,
    w_cross_kv,
    b_cross_v,
    cross_output_weight,
    expand_weight_1,
    expand_bias_1,
    contract_weight_2,
    neighbours,
    segment_ids,
    span_map,
    cotangent,
):
    x = layer_input[0]
    rows, width = x.shape
    length = segment_ids.shape[1]
    local = self_input_weight.shape[2]
    heads = local // HEAD_DIM
    blocks, block_rows = neighbours.shape[1], neighbours.shape[2]
    grad_out = cotangent[0]
    index = lax.axis_index("tp")
    t = index.astype(jnp.int32).reshape(1)
    partners = [[(i, i ^ step) for i in range(4)] for step in (1, 2, 3)]

    tables = padded_tables(length)
    b_pad = pad_heads(self_input_bias)[None]
    piece = -(-(5 * local + 16) // (16 * lax.axis_size("dp"))) * 16
    w_pad, pack = prepare(
        self_input_weight.transpose(1, 2, 0),
        cross_query_weight.T,
        self_output_weight,
        w_cross_kv.transpose(1, 2, 0),
        cross_output_weight,
        b_cross_q[None],
        b_cross_v[None],
        piece * lax.axis_size("dp"),
    )
    qx, kx = mask_lanes(segment_ids[0])
    lane = lax.broadcasted_iota(jnp.int32, (1, LANES), 1)
    vx = jnp.where((lane >= HEAD_DIM) & (lane < HEAD_DIM + 3), 1.0, 0.0).astype(BF)
    core, chip, _ = partners

    half = blocks // 2

    across = lax.ppermute(x, "tp", chip)
    beside = lax.ppermute(x, "tp", core)
    a0, a1, c0, c1 = project_rows((0, 1), t, (x, beside), norm_gain, norm_bias, w_pad, b_pad, tables, heads)
    across, c0 = lax.optimization_barrier((across, c0))
    pack_piece, blocks_first, across = lax.optimization_barrier(
        (take_rows(pack, lax.axis_index("dp"), piece), neighbours[0][:half], across)
    )
    pack_piece = lax.ppermute(pack_piece, "tp", chip)
    blocks_first = lax.ppermute(blocks_first, "tp", chip)
    pack_across = lax.all_gather(pack_piece, "dp", axis=0, tiled=True)
    pack_beside = lax.ppermute(pack, "tp", core)
    xs = [x, beside, across, lax.ppermute(across, "tp", core)]
    blocks_beside = lax.ppermute(neighbours[0], "tp", core)
    a2, a3, c2, c3 = project_rows((2, 3), t, xs[2:], norm_gain, norm_bias, w_pad, b_pad, tables, heads)
    qe, ke, ve, ot, lse = attend(t, (c0, c1, c2, c3), qx, kx, vx)
    normed_first = [a0, a1, a2, a3]
    ot, blocks_first = follow(ot, blocks_first)
    mixed = exchange([ot[0], ot[1], ot[2], ot[3]], partners)
    blocks_second, mixed = follow(neighbours[0][half:], tuple(mixed))
    blocks_second = lax.ppermute(blocks_second, "tp", chip)
    packs = [pack, pack_beside, pack_across, lax.ppermute(pack_across, "tp", core)]

    block_ids = index * blocks + jnp.arange(blocks, dtype=jnp.int32)
    slot_ids = jnp.arange(span_map.shape[1], dtype=jnp.int32)
    slots = jnp.sum(jnp.where(span_map[0][None, :] == block_ids[:, None], slot_ids[None, :], 0), 1)
    chosen_ids = lax.dynamic_slice_in_dim(span_map[0], index * blocks, blocks, 0)

    x1, b, cq = after_attend(t, x, mixed, packs, out_bias, norm_gain, norm_bias)
    memories = [neighbours[0], blocks_beside, blocks_first, lax.ppermute(blocks_first, "tp", core)]
    pieces = [(0, 0, blocks), (1, 0, blocks), (2, 0, half), (3, 0, half)]
    memory_near = memory_rows("memory_near", t, chosen_ids, memories, pieces, packs, local)
    gathered, blocks_second, cq, memory_near = lax.optimization_barrier(
        (grad_out.astype(BF), blocks_second, cq, tuple(memory_near))
    )
    memories = [blocks_second, lax.ppermute(blocks_second, "tp", core)]
    pieces = [(2, half, half), (3, half, half)]
    grad_across = lax.ppermute(gathered, "tp", chip)
    grad_beside = lax.ppermute(gathered, "tp", core)
    kv, memory = memory_rows("memory_far", t, chosen_ids, memories, pieces, packs, local, memory_near)
    cross_args = (packs, local, out_bias, norm_gain, norm_bias)
    co_a, cross_lse_a, x2_a, m_a = cross(t, 0, cq, kv, x1, *cross_args)
    x1_late, m_a = lax.optimization_barrier((x1, m_a))
    co_b, cross_lse_b, x2_b, m_b = cross(t, 1, cq, kv, x1_late, *cross_args)

    feed_args = (expand_weight_1, contract_weight_2, expand_bias_1[None])
    m_a, grad_across = follow(m_a, grad_across)
    across_a = lax.ppermute(m_a, "tp", chip)
    beside_a = lax.ppermute(m_a, "tp", core)
    gs = [gathered, grad_beside, grad_across, lax.ppermute(grad_across, "tp", core)]
    near_a = feed("feed_near_0", 0, (m_a, beside_a), gs[:2], *feed_args)
    across_b = lax.ppermute(m_b, "tp", chip)
    beside_b = lax.ppermute(m_b, "tp", core)
    across_a, near_a[0] = lax.optimization_barrier((across_a, near_a[0]))
    diagonal_a = lax.ppermute(across_a, "tp", core)
    near_b = feed("feed_near_1", 1, (m_b, beside_b), gs[:2], *feed_args)
    diagonal_a, across_b, near_b[0] = lax.optimization_barrier((diagonal_a, across_b, near_b[0]))
    diagonal_b = lax.ppermute(across_b, "tp", core)
    far_a = feed("feed_far_0", 0, (across_a, diagonal_a), gs[2:], *feed_args)
    diagonal_b, far_a[0] = lax.optimization_barrier((diagonal_b, far_a[0]))
    far_b = feed("feed_far_1", 1, (across_b, diagonal_b), gs[2:], *feed_args)
    dm_a, _ = collect([*near_a[2:4], *far_a[2:4]], partners)
    dm_b, _ = collect([*near_b[2:4], *far_b[2:4]], partners)
    ms = [m_a, m_b, beside_a, beside_b, across_a, across_b, diagonal_a, diagonal_b]
    ordered = [(near_a, 0), (near_b, 0), (near_a, 1), (near_b, 1), (far_a, 0), (far_b, 0), (far_a, 1), (far_b, 1)]
    grad_feed = feed_weight(ms, [f[6 + i] for f, i in ordered], [f[4 + i] for f, i in ordered], gs)
    grad_b1 = near_a[8] + near_b[8] + far_a[8] + far_b[8]

    out_far = [lax.ppermute(part[1], "tp", core) for part in (far_a, far_b, near_a, near_b)]
    out_sent = (rounded_sum(far_a[0], out_far[0]), rounded_sum(far_b[0], out_far[1]))
    dm_a[2], dm_b[2], grad_feed = lax.optimization_barrier((dm_a[2], dm_b[2], grad_feed))
    summed_feed = lax.psum(grad_feed, "dp")
    g2r, dkv, g1, g1r, dqc, *dos, small_middle = middle_back(
        t, (x2_a, x2_b), (dm_a, dm_b), (cross_lse_a, cross_lse_b), grad_out, packs, local, norm_gain, cq, kv, x1
    )

    dos = exchange(dos, partners)
    dos[1], g1r = lax.optimization_barrier((dos[1], g1r))
    grad_cross = cross_weight(t, dqc, b, mixed, g1r, dkv, memory, (co_a, co_b), g2r)
    dos[2], dos[3], grad_cross, out_sent = lax.optimization_barrier((dos[2], dos[3], tuple(grad_cross), out_sent))
    out_across = tuple(lax.ppermute(part, "tp", chip) for part in out_sent)
    grad_far = [lax.ppermute(grad_cross[r], "tp", core) for r in (3, 1)]
    dp = attend_back(t, qe, ke, ve, dos, ot, lse, tables)
    dp, grad_far[0], out_across = lax.optimization_barrier((dp, grad_far[0], out_across))
    across = lax.ppermute(rounded_sum(grad_cross[2], grad_far[0]), "tp", chip)
    grad_qkv, grad_bqkv = qkv_weight(dp, normed_first)
    da3, da1, small_a = input_back((3, 1), (xs[3], xs[1]), dp, w_pad)
    da2, da0, small_b = input_back((2, 0), (xs[2], xs[0]), dp, w_pad)
    dkv, small_a, small_b = lax.optimization_barrier((dkv, small_a, small_b))
    grad_near = [block_grad(t, side, dkv, packs, local, blocks) for side in range(2)]
    (da0, da1, da2, da3, grad_qkv, small_zero, grad_near, grad_far[1], summed_feed) = lax.optimization_barrier(
        (da0, da1, da2, da3, grad_qkv, small_a + small_b, tuple(grad_near), grad_far[1], summed_feed)
    )

    da, across = collect([da0, da1, da2, da3], partners, across)
    grad_near, da[2] = follow(grad_near, da[2])
    own = rounded_sum(grad_cross[0], grad_far[1], across).reshape(5 * local, width)
    summed_cross = lax.psum(own, "dp")
    grad_first, grad_second = [lax.ppermute(value, "tp", chip) for value in grad_near]
    small = jnp.concatenate([small_zero[:2], small_middle[:9], jnp.zeros((5, width), F32)], 0)
    small = small + lax.ppermute(small, "tp", core)
    small = small + lax.ppermute(small, "tp", chip)
    returned = [*grad_near] + [lax.ppermute(value, "tp", core) for value in grad_near]
    returned += [grad_first, grad_second] + [lax.ppermute(value, "tp", core) for value in (grad_first, grad_second)]
    halves = [(rel, start, half) for rel in range(4) for start in (0, half)]
    grad_memory = return_blocks(t, slots, returned, halves)
    summed_cross, grad_memory = lax.optimization_barrier((summed_cross, grad_memory))
    grad_input = input_grad(x, da, g1, norm_gain)
    kept = jnp.concatenate([rounded_sum(near_a[0], out_far[2]), rounded_sum(near_b[0], out_far[3])], 0)
    layer_output = jnp.concatenate([x2_a, x2_b], 0) + kept.astype(F32) + jnp.concatenate(out_across, 0).astype(F32) + out_bias[2]

    bqkv_row = grad_bqkv.reshape(3, heads, LANES)[:, :, :HEAD_DIM].reshape(1, -1)
    bqkv_row = jnp.pad(bqkv_row, ((0, 0), (0, width - 3 * local)))
    tail = jnp.concatenate([bqkv_row, grad_b1[:1], jnp.zeros((14, width), F32)], 0)
    last = jnp.concatenate([grad_qkv, small.astype(BF), tail.astype(BF)], 0)
    summed = sum_over_dp(last).astype(F32)

    summed_feed = summed_feed.astype(F32)
    hidden = expand_weight_1.shape[1]
    grad_qkv = summed[: 3 * local].T.reshape(width, 3, local)
    summed_cross = summed_cross.astype(F32)
    own = summed_cross.reshape(5, local, width)
    small = summed[3 * local : 3 * local + 16]
    bqkv = summed[3 * local + 16, : 3 * local].reshape(3, local)

    def mine(row):
        return lax.dynamic_slice_in_dim(row, index * local, local, 0)

    return (
        layer_output[None],
        grad_input[None],
        grad_memory[None],
        jnp.stack([small[0], small[2], small[4]]),
        jnp.stack([small[1], small[3], small[5]]),
        grad_qkv,
        bqkv,
        own[1],
        jnp.stack([small[6], small[7], small[8]]),
        own[0].T,
        mine(small[9]),
        jnp.stack([own[2].T, own[3].T], 1),
        mine(small[10]),
        own[4],
        summed_feed[:width],
        summed[3 * local + 17],
        summed_feed[width : width + hidden],
    )


def solution(mesh):
    return jax.shard_map(
        shards,
        mesh=mesh,
        in_specs=(
            P("dp", "tp", None),
            P(),
            P(),
            P(None, None, "tp"),
            P(None, "tp"),
            P("tp", None),
            P(),
            P(None, "tp"),
            P("tp"),
            P(None, None, "tp"),
            P("tp"),
            P("tp", None),
            P(None, "tp"),
            P("tp"),
            P("tp", None),
            P("dp", "tp", None, None),
            P("dp", None),
            P("dp", None),
            P("dp", "tp", None),
        ),
        out_specs=(
            P("dp", "tp", None),
            P("dp", "tp", None),
            P("dp", "tp", None, None),
            P(),
            P(),
            P(None, None, "tp"),
            P(None, "tp"),
            P("tp", None),
            P(),
            P(None, "tp"),
            P("tp"),
            P(None, None, "tp"),
            P("tp"),
            P("tp", None),
            P(None, "tp"),
            P("tp"),
            P("tp", None),
        ),
        check_vma=False,
    )
```

```python
import functools
import math

import jax
import jax.numpy as jnp
import numpy as np
from jax import lax
from jax.experimental import pallas as pl
from jax.experimental.pallas import tpu as pltpu
from jax.sharding import PartitionSpec as P

HEAD_DIM = 64
SPAN = 64
LANES = 128
QUERY_ROWS = 256
NEGATIVE = -1e30
NORM_EPS = 1e-05
BF = jnp.bfloat16
F32 = jnp.float32
VMEM_BYTES = 56 * 1024 * 1024

PIECES = ((0, 2), (2, 4), (4, 5))

COST_US = {"widen": 30}

DOCS = 5
MASK_LANE = HEAD_DIM
LSE_LANE = HEAD_DIM + DOCS


def nn(a, b):
    return lax.dot_general(a, b, (((1,), (0,)), ((), ())), preferred_element_type=F32)


def nt(a, b):
    return lax.dot_general(a, b, (((1,), (1,)), ((), ())), preferred_element_type=F32)


def tn(a, b):
    return lax.dot_general(a, b, (((0,), (0,)), ((), ())), preferred_element_type=F32)


def call(body, name, grid, in_specs, out_specs, out_shape, args, scratch=(), prefetch=0, aliases=None):
    return pl.pallas_call(
        body,
        out_shape=out_shape,
        grid_spec=pltpu.PrefetchScalarGridSpec(
            num_scalar_prefetch=prefetch,
            grid=grid,
            in_specs=in_specs,
            out_specs=out_specs,
            scratch_shapes=list(scratch),
        ),
        compiler_params=pltpu.CompilerParams(
            vmem_limit_bytes=VMEM_BYTES, dimension_semantics=("arbitrary",) * len(grid)
        ),
        cost_estimate=pl.CostEstimate(flops=int(COST_US.get(name, 0.01) * 1e9), bytes_accessed=1, transcendentals=0),
        name=name,
        input_output_aliases=aliases or {},
    )(*args)


def whole(array):
    zeros = (0,) * len(array.shape)
    return pl.BlockSpec(array.shape, lambda *_: zeros)


def rows_of(tile, width):
    return pl.BlockSpec((tile, width), lambda i, *_: (i, 0))


def shape_of(shape, dtype):
    return jax.ShapeDtypeStruct(shape, dtype)


def standardize(values):
    centre = values - jnp.mean(values, -1, keepdims=True)
    inverse = lax.rsqrt(jnp.mean(centre * centre, -1, keepdims=True) + NORM_EPS)
    return centre * inverse, inverse


def norm_pull(grad, normed, inverse, gain):
    scaled = grad * gain
    return inverse * (
        scaled
        - jnp.mean(scaled, -1, keepdims=True)
        - normed * jnp.mean(scaled * normed, -1, keepdims=True)
    )


def column_sum(values):
    return jnp.sum(values, 0, keepdims=True)


def add_rows(out_ref, rows):
    @pl.when(pl.program_id(0) == 0)
    def _():
        out_ref[...] = jnp.zeros_like(out_ref)

    for index, row in enumerate(rows):
        out_ref[index : index + 1, :] += row


def follow(operand, earlier):
    return lax.optimization_barrier((operand, earlier))


def collect(parts, partners, earlier=None):
    core, chip, _ = partners
    far = lax.ppermute(parts[3], "tp", core)
    near = lax.ppermute(parts[1], "tp", core)
    sent = rounded_sum(parts[2], far)
    if earlier is not None:
        sent, earlier = follow(sent, earlier)
    return [parts[0], near, lax.ppermute(sent, "tp", chip)], earlier


def take_rows(values, part, rows):
    return lax.dynamic_slice_in_dim(values, part * rows, rows, 0)


def rounded_sum(*parts):
    return sum(part.astype(F32) for part in parts).astype(BF)


def small_rows_body(first_a, first_b, middle_ref, out_ref):
    out_ref[...] = jnp.zeros_like(out_ref)
    out_ref[0:2, :] = first_a[0:2, :] + first_b[0:2, :]
    out_ref[2:11, :] = middle_ref[0:9, :]


def small_rows(first_a, first_b, middle):
    args = (first_a, first_b, middle)
    return call(small_rows_body, "small_rows", (1,), [whole(a) for a in args], whole(middle), shape_of(middle.shape, F32), args)


def last_rows_body(*refs):
    parts = [refs[n * len(PIECES) : (n + 1) * len(PIECES)] for n in range(3)]
    qkv_ref, small_ref, bias_ref, s0, s1, s2, s3, out_ref = refs[3 * len(PIECES) :]
    heads = bias_ref.shape[2] // LANES
    local, width = parts[0][0].shape[1:]
    start, rows, count = 0, qkv_ref.shape[0], small_ref.shape[0]
    for own_ref, near_ref, far_ref in zip(*parts):
        for j in range(own_ref.shape[0]):
            total = own_ref[j].astype(F32) + near_ref[j].astype(F32) + far_ref[j].astype(F32)
            out_ref[start : start + local, :] = total.astype(BF)
            start += local
    out_ref[start : start + rows, :] = qkv_ref[...]
    start += rows
    out_ref[start : start + count, :] = small_ref[...].astype(BF)
    parts = [bias_ref[j][:, h * LANES : h * LANES + HEAD_DIM] for j in range(3) for h in range(heads)]
    bias = jnp.concatenate(parts + [jnp.zeros((1, width - rows), F32)], 1)
    other = sum(ref[0:1, :] for ref in (s0, s1, s2, s3))
    row = lax.broadcasted_iota(jnp.int32, (count, width), 0)
    out_ref[start + count :, :] = jnp.where(row == 0, bias, jnp.where(row == 1, other, 0.0)).astype(BF)


def last_rows(own, near, far, qkv, small, bias, sums):
    width = qkv.shape[1]
    total = sum(part.shape[0] * part.shape[1] for part in own)
    args = (*own, *near, *far, qkv, small, bias, *sums)
    out = shape_of((total + qkv.shape[0] + 2 * small.shape[0], width), BF)
    return call(last_rows_body, "last_rows", (1,), [whole(a) for a in args], whole(out), out, args)


def widen_body(t_ref, x_ref, cq_ref, so_ref, kv_ref, co_ref, qkv_ref, gain_ref, shift_ref, out_ref, bqkv_ref, bq_ref, bv_ref, b1_ref):
    local, width = cq_ref.shape
    start = 0

    def take(count):
        nonlocal start
        start += count
        return x_ref[start - count : start, :].astype(F32)

    cq_ref[...] = take(local)
    so_ref[...] = take(local)
    for target in (kv_ref.at[0], kv_ref.at[1], co_ref, qkv_ref.at[0], qkv_ref.at[1], qkv_ref.at[2]):
        target[...] = take(local)
    small, tail = take(16), take(16)

    def pick(rows):
        return jnp.concatenate([small[row : row + 1] for row in rows], 0)

    def mine(row):
        cuts = [row[:, group * local : (group + 1) * local] for group in range(4)]
        return sum(jnp.where(t_ref[0] == group, cut, 0.0) for group, cut in enumerate(cuts))

    gain_ref[...] = pick((0, 2, 4))
    shift_ref[...] = pick((1, 3, 5))
    out_ref[...] = pick((6, 7, 8))
    bqkv_ref[...] = jnp.concatenate([tail[0:1, j * local : (j + 1) * local] for j in range(3)], 0)
    bq_ref[...] = mine(small[9:10])
    bv_ref[...] = mine(small[10:11])
    b1_ref[...] = tail[1:2]


def widen(t, rows, local):
    width = rows.shape[1]
    shapes = [(local, width), (local, width), (2, local, width), (local, width), (3, local, width)]
    shapes += [(3, width)] * 3 + [(3, local), (1, local), (1, local), (1, width)]
    outs = [shape_of(shape, F32) for shape in shapes]
    return call(widen_body, "widen", (1,), [whole(rows)], [whole(o) for o in outs], outs, (t, rows), prefetch=1)


def widen_feed_body(x_ref, first_ref, second_ref):
    rows = first_ref.shape[0]
    first_ref[...] = x_ref[:rows, :].astype(F32)
    second_ref[...] = x_ref[rows:, :].astype(F32)


def widen_feed(rows, width):
    outs = [shape_of((width, width), F32), shape_of((rows.shape[0] - width, width), F32)]
    return call(widen_feed_body, "widen_feed", (1,), [whole(rows)], [whole(o) for o in outs], outs, (rows,))


def exchange(parts, partners):
    return [parts[0]] + [lax.ppermute(parts[r], "tp", partners[r - 1]) for r in (1, 2, 3)]


def gather_rows(t_ref, refs, target, start=0):
    @pl.when(pl.program_id(0) == 0)
    def _():
        for rel, ref in enumerate(refs):
            count = ref.shape[0]
            target[pl.ds(pl.multiple_of((t_ref[0] ^ rel) * count + start, 16), count), :] = ref[...]


def gather_bias(t_ref, refs, start, local):
    rows = [ref[...].astype(F32)[0:1] for ref in refs]
    rows = [row[:, start : start + local] + row[:, start + local : start + 2 * local] for row in rows]
    groups = []
    for group in range(4):
        groups.append(sum(jnp.where(t_ref[0] ^ rel == group, row, 0.0) for rel, row in enumerate(rows)))
    return jnp.concatenate(groups, 1)


def pack_rows(local, width, part):
    return [pl.BlockSpec((local, width), lambda i, *_: (part, 0))] * 4


def prepare_body(qkv_ref, cq_ref, so_ref, kv_ref, co_ref, bq_ref, bv_ref, w_ref, pack_ref):
    local, width = so_ref.shape
    zeros = jnp.zeros((LANES - HEAD_DIM, width), BF)
    for j in range(3 * local // HEAD_DIM):
        part = qkv_ref[j * HEAD_DIM // local, j * HEAD_DIM % local : j * HEAD_DIM % local + HEAD_DIM, :]
        w_ref[j * LANES : j * LANES + HEAD_DIM, :] = part
        w_ref[j * LANES + HEAD_DIM : (j + 1) * LANES, :] = zeros
    for index, part in enumerate((cq_ref[...], so_ref[...], kv_ref[0], kv_ref[1], co_ref[...])):
        pack_ref[index * local : (index + 1) * local, :] = part
    parts = []
    for ref in (bq_ref, bv_ref):
        high = ref[...].astype(BF).astype(F32)
        parts += [high, ref[...] - high]
    row = jnp.concatenate(parts, 1)
    count = pack_ref.shape[0] - 5 * local
    first = lax.broadcasted_iota(jnp.int32, (count, width), 0) == 0
    pack_ref[5 * local :, :] = jnp.where(first, row, 0.0).astype(BF)


def prepare(qkv, cq, so, kv, co, bq, bv, pack_size):
    local, width = so.shape
    outs = [shape_of((3 * local // HEAD_DIM * LANES, width), BF), shape_of((pack_size, width), BF)]
    args = (qkv, cq, so, kv, co, bq, bv)
    return call(prepare_body, "prepare", (1,), [whole(a) for a in args], [whole(o) for o in outs], outs, args)


def qkv_body(t_ref, xa, xb, gain_ref, shift_ref, w_ref, b_ref, ca, sa, ta, cb, sb, tb, aa, ab, oa, ob):
    heads = oa.shape[1]
    for x_ref, cos_ref, left_ref, right_ref, a_ref, out_ref in ((xa, ca, sa, ta, aa, oa), (xb, cb, sb, tb, ab, ob)):
        normed, _ = standardize(x_ref[...].astype(F32))
        a = (normed * gain_ref[0:1, :] + shift_ref[0:1, :]).astype(BF)
        a_ref[...] = a
        proj = nt(a, w_ref[...]) + b_ref[...]
        cos, left, right = cos_ref[...], left_ref[...], right_ref[...]
        for j in range(3 * heads):
            part = proj[:, j * LANES : (j + 1) * LANES]
            if j < 2 * heads:
                part = part * cos + pltpu.roll(part, 96, 1) * left + pltpu.roll(part, 32, 1) * right
            if j < heads:
                part = part * (1.0 / math.sqrt(HEAD_DIM))
            out_ref[j // heads, j % heads] = part.astype(BF)


def project_rows(rels, t, xs, gain, shift, w, b, tables, heads):
    rows, width = xs[0].shape
    tile = min(256, rows)
    steps = rows // tile

    def table(rel):
        return pl.BlockSpec((tile, LANES), lambda i, t_ref: ((t_ref[0] ^ rel) * steps + i, 0))

    row = rows_of(tile, width)
    out = pl.BlockSpec((3, heads, tile, LANES), lambda i, t_ref: (0, 0, i, 0))
    return call(
        qkv_body,
        f"qkv_{rels[0]}{rels[1]}",
        (steps,),
        [row, row, whole(gain), whole(shift), whole(w), whole(b)] + [table(rels[0])] * 3 + [table(rels[1])] * 3,
        [row, row, out, out],
        [shape_of((rows, width), BF)] * 2 + [shape_of((3, heads, rows, LANES), BF)] * 2,
        (t, *xs, gain, shift, w, b, *tables, *tables),
        prefetch=1,
    )


def causal_corner(scores):
    keys = lax.broadcasted_iota(jnp.int32, scores.shape, 0)
    queries = lax.broadcasted_iota(jnp.int32, scores.shape, 1)
    return jnp.where(keys <= queries, scores, NEGATIVE)


def attend_body(t_ref, c0, c1, c2, c3, qx_ref, kx_ref, vx_ref, qe_ref, ke_ref, ve_ref, ot_ref, lse_ref, vt_ref):
    t = t_ref[0]
    rows = c0.shape[2]
    for rel, chunk in enumerate((c0, c1, c2, c3)):
        place = pl.ds(pl.multiple_of((t ^ rel) * rows, rows), rows)
        qe_ref[0, place, :] = chunk[0, 0] + qx_ref[place, :]
        ke_ref[0, place, :] = chunk[1, 0] + kx_ref[place, :]
        values = chunk[2, 0] + vx_ref[...]
        ve_ref[0, place, :] = values
        vt_ref[:, place] = values.astype(F32).T.astype(BF)
    step = QUERY_ROWS
    for low in range(0, qe_ref.shape[1], step):
        high = low + step
        query = qe_ref[0, low:high, :]
        corner = causal_corner(nt(ke_ref[0, low:high, :], query))
        top = jnp.max(corner, 0, keepdims=True)
        if low:
            earlier = nt(ke_ref[0, :low, :], query)
            top = jnp.maximum(top, jnp.max(earlier, 0, keepdims=True))
        mixed = nn(vt_ref[:, low:high], jnp.exp(corner - top).astype(BF))
        if low:
            mixed = mixed + nn(vt_ref[:, :low], jnp.exp(earlier - top).astype(BF))
        total = mixed[HEAD_DIM : HEAD_DIM + 1, :]
        lse_ref[0, :, low:high] = top + jnp.log(total)
        begin = low % rows
        ot_ref[t ^ (low // rows), :, begin : begin + step] = (mixed[:HEAD_DIM] / total).astype(BF)


def attend(t, chunks, qx, kx, vx):
    _, heads, rows, _ = chunks[0].shape
    length = qx.shape[0]
    chunk = pl.BlockSpec((3, 1, rows, LANES), lambda h, t_ref: (0, h, 0, 0))
    plane = pl.BlockSpec((1, length, LANES), lambda h, t_ref: (h, 0, 0))
    padded = shape_of((heads, length, LANES), BF)
    return call(
        attend_body,
        "attend",
        (heads,),
        [chunk] * 4 + [whole(qx), whole(kx), whole(vx)],
        [
            plane,
            plane,
            plane,
            pl.BlockSpec((4, HEAD_DIM, rows), lambda h, t_ref: (0, h, 0)),
            pl.BlockSpec((1, 1, length), lambda h, t_ref: (h, 0, 0)),
        ],
        [padded, padded, padded, shape_of((4, heads * HEAD_DIM, rows), BF), shape_of((heads, 1, length), F32)],
        (t, *chunks, qx, kx, vx),
        scratch=[pltpu.VMEM((LANES, length), BF)],
        prefetch=1,
    )


def three_parts(values):
    first = values.astype(BF).astype(F32)
    second = (values - first).astype(BF).astype(F32)
    return first, second, values - first - second


def attend_back_body(
    t_ref, qe_ref, ke_ref, ve_ref, d0, d1, d2, d3, ot_ref, lse_ref, cos_ref, sa_ref, sb_ref, out_ref,
    qt_ref, kt_ref, dt_ref, dk_ref, dv_ref,
):
    t = t_ref[0]
    rows = d0.shape[1]
    step = QUERY_ROWS
    length = qe_ref.shape[1]
    for rel, chunk in enumerate((d0, d1, d2, d3)):
        place = pl.ds(pl.multiple_of((t ^ rel) * rows, rows), rows)
        grad = chunk[...].astype(F32)
        delta = three_parts(jnp.sum(grad * ot_ref[rel].astype(F32), 0, keepdims=True))
        padded = jnp.concatenate([grad, jnp.zeros_like(grad)], 0)
        row = lax.broadcasted_iota(jnp.int32, padded.shape, 0)
        for index in range(3):
            padded = jnp.where(row == HEAD_DIM + index, -delta[index], padded)
        dt_ref[:, place] = padded.astype(BF)
    for low in range(0, length, rows):
        high = low + rows
        kt_ref[:, low:high] = ke_ref[0, low:high, :].astype(F32).T.astype(BF)
        turned = qe_ref[0, low:high, :].astype(F32).T
        row = lax.broadcasted_iota(jnp.int32, turned.shape, 0)
        pieces = three_parts(lse_ref[0, :, low:high])
        for index in range(3):
            turned = jnp.where(row == LSE_LANE + index, -pieces[index], turned)
        qt_ref[:, low:high] = turned.astype(BF)
    dk_ref[...] = jnp.zeros_like(dk_ref)
    dv_ref[...] = jnp.zeros_like(dv_ref)

    def unrotate(grad, place):
        return (
            grad * cos_ref[place, :]
            - pltpu.roll(grad, 96, 1) * sa_ref[place, :]
            - pltpu.roll(grad, 32, 1) * sb_ref[place, :]
        )

    for low in range(0, length, step):
        high = low + step
        query, query_t, grad_t = qe_ref[0, low:high, :], qt_ref[:, low:high], dt_ref[:, low:high]
        dq_t = None
        for begin, end in ((0, low), (low, high)):
            if begin == end:
                continue
            scores = nn(ke_ref[0, begin:end, :], query_t)
            if begin == low:
                scores = causal_corner(scores)
            prob = jnp.exp(scores)
            grad_scores = (prob * nn(ve_ref[0, begin:end, :], grad_t)).astype(BF)
            dv_ref[begin:end, :] += nt(prob.astype(BF), grad_t)
            dk_ref[begin:end, :] += nn(grad_scores, query)
            part = nn(kt_ref[:, begin:end], grad_scores)
            dq_t = part if dq_t is None else dq_t + part
        start = low % rows
        grad_query = unrotate(dq_t.T, slice(low, high)) * (1.0 / math.sqrt(HEAD_DIM))
        out_ref[t ^ (low // rows), 0, 0, start : start + step, :] = grad_query.astype(BF)
    for low in range(0, length, rows):
        place = slice(low, low + rows)
        rel = t ^ (low // rows)
        out_ref[rel, 1, 0] = unrotate(dk_ref[place, :], place).astype(BF)
        lane = lax.broadcasted_iota(jnp.int32, (rows, LANES), 1)
        out_ref[rel, 2, 0] = jnp.where(lane < HEAD_DIM, dv_ref[place, :], 0.0).astype(BF)


def attend_back(t, qe, ke, ve, grads, ot, lse, tables):
    heads, length, _ = qe.shape
    rows = grads[0].shape[1]
    plane = pl.BlockSpec((1, length, LANES), lambda h, t_ref: (h, 0, 0))
    grad = pl.BlockSpec((HEAD_DIM, rows), lambda h, t_ref: (h, 0))
    return call(
        attend_back_body,
        "attend_back",
        (heads,),
        [plane] * 3
        + [grad] * 4
        + [
            pl.BlockSpec((4, HEAD_DIM, rows), lambda h, t_ref: (0, h, 0)),
            pl.BlockSpec((1, 1, length), lambda h, t_ref: (h, 0, 0)),
        ]
        + [whole(table) for table in tables],
        pl.BlockSpec((4, 3, 1, rows, LANES), lambda h, t_ref: (0, 0, h, 0, 0)),
        shape_of((4, 3, heads, rows, LANES), BF),
        (t, qe, ke, ve, *grads, ot, lse, *tables),
        scratch=[pltpu.VMEM((LANES, length), BF)] * 3 + [pltpu.VMEM((length, LANES), F32)] * 2,
        prefetch=1,
    )


def input_back_body(xa, xb, da, db, w_ref, oa, ob, small_ref):
    heads = da.shape[2]
    totals = []
    for x_ref, dp_ref, out_ref in ((xa, da, oa), (xb, db, ob)):
        grads = jnp.concatenate([dp_ref[0, j // heads, j % heads] for j in range(3 * heads)], 1)
        grad = nn(grads, w_ref[...])
        normed, _ = standardize(x_ref[...].astype(F32))
        out_ref[...] = grad.astype(BF)
        totals.append((column_sum(grad * normed), column_sum(grad)))
    add_rows(small_ref, [totals[0][0] + totals[1][0], totals[0][1] + totals[1][1]])


def input_back(rels, xs, dp, w):
    rows, width = xs[0].shape
    heads = dp.shape[2]
    tile = min(256, rows)
    row = rows_of(tile, width)

    def part(rel):
        return pl.BlockSpec((1, 3, heads, tile, LANES), lambda i: (rel, 0, 0, i, 0))

    return call(
        input_back_body,
        f"input_back_{rels[0]}{rels[1]}",
        (rows // tile,),
        [row, row, part(rels[0]), part(rels[1]), whole(w)],
        [row, row, pl.BlockSpec((8, width), lambda i: (0, 0))],
        [shape_of((rows, width), BF)] * 2 + [shape_of((8, width), F32)],
        (*xs, dp, dp, w),
    )


def qkv_weight_body(dp_ref, a0, a1, a2, a3, out_ref, bias_ref):
    heads = dp_ref.shape[2]
    total, sums = None, None
    for rel, a_ref in enumerate((a0, a1, a2, a3)):
        grads = jnp.concatenate([dp_ref[rel, 0, h] for h in range(heads)], 1)
        part, part_sum = tn(grads, a_ref[...]), column_sum(grads.astype(F32))
        total = part if total is None else total + part
        sums = part_sum if sums is None else sums + part_sum
    for h in range(heads):
        out_ref[h * HEAD_DIM : (h + 1) * HEAD_DIM, :] = total[h * LANES : h * LANES + HEAD_DIM].astype(BF)
    bias_ref[0] = sums


def qkv_weight(dp, normed):
    _, _, heads, rows, _ = dp.shape
    width = normed[0].shape[1]
    local = heads * HEAD_DIM
    return call(
        qkv_weight_body,
        "qkv_weight",
        (3,),
        [pl.BlockSpec((4, 1, heads, rows, LANES), lambda j: (0, j, 0, 0, 0))] + [whole(a) for a in normed],
        [rows_of(local, width), pl.BlockSpec((1, 1, heads * LANES), lambda j: (j, 0, 0))],
        [shape_of((3 * local, width), BF), shape_of((3, 1, heads * LANES), F32)],
        (dp, *normed),
    )


def after_attend_body(
    t_ref, x_ref, o0, o1, o2, o3, w0, w1, w2, w3, q0, q1, q2, q3, b0, b1, b2, b3, bias_ref, gain_ref, shift_ref,
    x1_ref, b_ref, cq_ref, wq_ref,
):
    gather_rows(t_ref, (q0, q1, q2, q3), wq_ref)
    total = x_ref[...].astype(F32) + bias_ref[0:1, :]
    for o_ref, w_ref in ((o0, w0), (o1, w1), (o2, w2), (o3, w3)):
        total = total + tn(o_ref[...], w_ref[...])
    x1_ref[...] = total
    normed, _ = standardize(total)
    b = (normed * gain_ref[1:2, :] + shift_ref[1:2, :]).astype(BF)
    b_ref[...] = b
    bias = gather_bias(t_ref, (b0, b1, b2, b3), 0, w0.shape[0])
    cq_ref[...] = ((nt(b, wq_ref[...]) + bias) * (1.0 / math.sqrt(HEAD_DIM))).astype(BF)


def after_attend(t, x, mixed, packs, out_bias, gain, shift):
    rows, width = x.shape
    local = mixed[0].shape[0]
    tile = min(256, rows)
    return call(
        after_attend_body,
        "after_attend",
        (rows // tile,),
        [rows_of(tile, width)]
        + [pl.BlockSpec((local, tile), lambda i, *_: (0, i))] * 4
        + pack_rows(local, width, 1)
        + pack_rows(local, width, 0)
        + pack_rows(16, width, 5 * local // 16)
        + [whole(out_bias), whole(gain), whole(shift)],
        [rows_of(tile, width)] * 3,
        [shape_of((rows, width), F32), shape_of((rows, width), BF), shape_of((rows, width), BF)],
        (t, x, *mixed, *packs, *packs, *packs, out_bias, gain, shift),
        scratch=[pltpu.VMEM((width, width), BF)],
        prefetch=1,
    )


def split_pair(values):
    lane = lax.broadcasted_iota(jnp.int32, values.shape, 1)
    zero = jnp.zeros_like(values)
    return jnp.concatenate(
        [jnp.where(lane < HEAD_DIM, values, zero), jnp.where(lane >= HEAD_DIM, values, zero)], 0
    )


def join_pair(values):
    rows = values.shape[0] // 2
    lane = lax.broadcasted_iota(jnp.int32, (rows, values.shape[1]), 1)
    return jnp.where(lane < HEAD_DIM, values[:rows], values[rows:])


def lane_cuts(width):
    return [slice(start, start + LANES) for start in range(0, width, LANES)]


def cross_body(
    t_ref, cq_ref, kv_ref, x1_ref, w0, w1, w2, w3, bias_ref, gain_ref, shift_ref, co_ref, lse_ref, x2_ref, m_ref, w_ref
):
    gather_rows(t_ref, (w0, w1, w2, w3), w_ref)
    width = cq_ref.shape[1]
    spans, side, _ = lse_ref.shape
    keys = kv_ref.shape[0] // spans
    cuts = lane_cuts(width)
    for span in range(spans):
        place = slice(span * SPAN, (span + 1) * SPAN)
        query = cq_ref[place, :]
        key, value = kv_ref[span * keys : (span + 1) * keys, :width], kv_ref[span * keys : (span + 1) * keys, width:]
        scores = [nt(key[:, cut], split_pair(query[:, cut])) for cut in cuts]
        tops = [jnp.max(score, 0, keepdims=True) for score in scores]
        shifted = [jnp.exp(score - top) for score, top in zip(scores, tops)]
        totals = [jnp.sum(part, 0, keepdims=True) for part in shifted]
        probs = [(part * (1.0 / total)).astype(BF) for part, total in zip(shifted, totals)]
        mixed = [join_pair(tn(prob, value[:, cut])) for prob, cut in zip(probs, cuts)]
        co_ref[place, :] = jnp.concatenate(mixed, 1).astype(BF)
        rows = [top + jnp.log(total) for top, total in zip(tops, totals)]
        lse_ref[span] = jnp.concatenate(rows + [jnp.zeros((side - len(rows), LANES), F32)], 0)
    total = x1_ref[...] + nn(co_ref[...], w_ref[...]) + bias_ref[1:2, :]
    x2_ref[...] = total
    normed, _ = standardize(total)
    m_ref[...] = (normed * gain_ref[2:3, :] + shift_ref[2:3, :]).astype(BF)


def cross(t, half, cq, kv, x1, packs, local, out_bias, gain, shift):
    rows, width = x1.shape
    tile = rows // 2
    ratio = kv.shape[0] // rows
    side = -(-(width // LANES) // 8) * 8
    spans = tile // SPAN

    def rows_at(count, columns):
        return pl.BlockSpec((count, columns), lambda i, *_: (half, 0))

    row = rows_at(tile, width)
    outs = [
        shape_of((tile, width), BF),
        shape_of((spans, side, LANES), F32),
        shape_of((tile, width), F32),
        shape_of((tile, width), BF),
    ]
    return call(
        cross_body,
        f"cross_{half}",
        (1,),
        [row, rows_at(ratio * tile, 2 * width), row]
        + pack_rows(local, width, 4)
        + [whole(out_bias), whole(gain), whole(shift)],
        [whole(out) for out in outs],
        outs,
        (t, cq, kv, x1, *packs, out_bias, gain, shift),
        scratch=[pltpu.VMEM((width, width), BF)],
        prefetch=1,
    )


def middle_back_body(
    t_ref, x2a, x2b, da0, da1, db0, db1, lsea, lseb, across_ref, g_ref, gain_ref, cq_ref, kv_ref, x1_ref,
    c0, c1, c2, c3, q0, q1, q2, q3, w0, w1, w2, w3,
    g2r_ref, dkv_ref, g1_ref, g1r_ref, dqc_ref, d0, d1, d2, d3, small_ref,
    dco_ref, dq_ref, x2_ref, dm_ref, lse_ref, co_w_ref, wq_ref,
):
    gather_rows(t_ref, (c0, c1, c2, c3), co_w_ref)
    gather_rows(t_ref, (q0, q1, q2, q3), wq_ref)
    for side, (x2, parts, lse) in enumerate(((x2a, (da0, da1), lsea), (x2b, (db0, db1), lseb))):

        @pl.when(pl.program_id(0) == side)
        def _(x2=x2, parts=parts, lse=lse):
            x2_ref[...] = x2[...]
            dm_ref[...] = sum(part[...].astype(F32) for part in parts) + across_ref[...].astype(F32)
            lse_ref[...] = lse[...]

    width = cq_ref.shape[1]
    spans = lse_ref.shape[0]
    keys = kv_ref.shape[0] // spans
    cuts = lane_cuts(width)
    grad_m = dm_ref[...]
    normed_m, inverse = standardize(x2_ref[...])
    g = g_ref[...]
    g2 = g + norm_pull(grad_m, normed_m, inverse, gain_ref[2:3, :])
    g2r = g2.astype(BF)
    g2r_ref[...] = g2r
    dco_ref[...] = nt(g2r, co_w_ref[...]).astype(BF)
    for span in range(spans):
        place = slice(span * SPAN, (span + 1) * SPAN)
        block = slice(span * keys, (span + 1) * keys)
        query, grad = cq_ref[place, :], dco_ref[place, :]
        key, value = kv_ref[block, :width], kv_ref[block, width:]
        stats = lse_ref[span]
        queries = [split_pair(query[:, cut]) for cut in cuts]
        grads = [split_pair(grad[:, cut]) for cut in cuts]
        probs = [jnp.exp(nt(key[:, cut], q) - stats[j : j + 1]) for j, (cut, q) in enumerate(zip(cuts, queries))]
        pulls = [nt(value[:, cut], part) for cut, part in zip(cuts, grads)]
        deltas = [jnp.sum(prob * pull, 0, keepdims=True) for prob, pull in zip(probs, pulls)]
        scores = [(prob * (pull - delta)).astype(BF) for prob, pull, delta in zip(probs, pulls, deltas)]
        keys_back = [nn(score, q).astype(BF) for score, q in zip(scores, queries)]
        values_back = [nn(prob.astype(BF), part).astype(BF) for prob, part in zip(probs, grads)]
        dkv_ref[block, :] = jnp.concatenate(keys_back + values_back, 1)
        dq_ref[place, :] = jnp.concatenate([join_pair(tn(score, key[:, cut])) for score, cut in zip(scores, cuts)], 1)
    dqc = (dq_ref[...] * (1.0 / math.sqrt(HEAD_DIM))).astype(BF)
    dqc_ref[...] = dqc
    grad_b = nn(dqc, wq_ref[...])
    normed_b, inverse = standardize(x1_ref[...])
    g1 = g2 + norm_pull(grad_b, normed_b, inverse, gain_ref[1:2, :])
    g1_ref[...] = g1
    g1r = g1.astype(BF)
    g1r_ref[...] = g1r
    for w_ref, d_ref in ((w0, d0), (w1, d1), (w2, d2), (w3, d3)):
        d_ref[...] = nt(w_ref[...], g1r).astype(BF)
    add_rows(
        small_ref,
        [
            column_sum(grad_b * normed_b),
            column_sum(grad_b),
            column_sum(grad_m * normed_m),
            column_sum(grad_m),
            column_sum(g1),
            column_sum(g2),
            column_sum(g),
            column_sum(dqc.astype(F32)),
            column_sum(dkv_ref[:, width:].astype(F32)),
        ],
    )


def middle_back(t, x2, dm, across, lse, g, packs, local, gain, cq, kv, x1):
    rows, width = x1.shape
    tile = rows // 2
    ratio = kv.shape[0] // rows
    row = rows_of(tile, width)
    wide = rows_of(ratio * tile, 2 * width)
    turned = pl.BlockSpec((local, tile), lambda i, *_: (0, i))
    half = shape_of((rows, width), BF)
    halves = (*x2, *dm[0], *dm[1], *lse)
    return call(
        middle_back_body,
        "middle_back",
        (2,),
        [whole(value) for value in halves]
        + [row, row, whole(gain), row, wide, row]
        + pack_rows(local, width, 4)
        + pack_rows(local, width, 0)
        + pack_rows(local, width, 1),
        [row, wide, row, row, row] + [turned] * 4 + [pl.BlockSpec((16, width), lambda i, *_: (0, 0))],
        [half, shape_of(kv.shape, BF), shape_of((rows, width), F32), half, half]
        + [shape_of((local, rows), BF)] * 4
        + [shape_of((16, width), F32)],
        (t, *halves, across, g, gain, cq, kv, x1, *packs, *packs, *packs),
        scratch=[
            pltpu.VMEM((tile, width), BF),
            pltpu.VMEM((tile, width), F32),
            pltpu.VMEM((tile, width), F32),
            pltpu.VMEM((tile, width), F32),
            pltpu.VMEM(lse[0].shape, F32),
            pltpu.VMEM((width, width), BF),
            pltpu.VMEM((width, width), BF),
        ],
        prefetch=1,
    )


def block_place(block, blocks, t, piece):
    rel, start, count = piece
    inside = block % blocks - start
    held = ((block // blocks) ^ t == rel) & (inside >= 0) & (inside < count)
    return held, jnp.where(held, inside, 0)


def anywhere():
    return pl.BlockSpec(memory_space=pl.ANY)


def fetch_block(t_ref, block, blocks, refs, pieces, target, semaphore):
    found = False
    for ref, piece in zip(refs, pieces):
        held, index = block_place(block, blocks, t_ref[0], piece)

        @pl.when(held)
        def _(ref=ref, index=index):
            pltpu.make_async_copy(ref.at[index], target, semaphore).start()

        found = held | found
    return found


def gather_pair(t_ref, refs, target):
    width = target.shape[1]
    local = refs[0].shape[0] // 2
    gather_rows(t_ref, [ref.at[:local, :] for ref in refs], target)
    gather_rows(t_ref, [ref.at[local:, :] for ref in refs], target, width)


def memory_body(t_ref, id_ref, *refs, pieces, first):
    count = len(pieces)
    packs, biases = refs[count : count + 4], refs[count + 4 : count + 8]
    kv_ref, chosen_ref, w_ref, x_ref, out_ref, in_sem, kv_sem, out_sem = refs[count + 8 + (0 if first else 2) :]
    blocks, length, width = x_ref.shape
    held = [
        fetch_block(t_ref, id_ref[slot], blocks, refs, pieces, x_ref.at[slot], in_sem.at[slot])
        for slot in range(blocks)
    ]
    gather_pair(t_ref, packs, w_ref)
    local = packs[0].shape[0] // 2
    bias = gather_bias(t_ref, biases, 2 * local, local)

    def copies(slot):
        rows = pl.ds(slot * length, length)
        return (
            pltpu.make_async_copy(out_ref.at[slot], kv_ref.at[rows, :], kv_sem.at[slot]),
            pltpu.make_async_copy(x_ref.at[slot], chosen_ref.at[rows, :], out_sem.at[slot]),
        )

    for slot in range(blocks):

        @pl.when(held[slot])
        def _(slot=slot):
            pltpu.make_async_copy(refs[0].at[0], x_ref.at[slot], in_sem.at[slot]).wait()
            kv = nt(x_ref[slot], w_ref[...])
            out_ref[slot, :, :width] = kv[:, :width].astype(BF)
            out_ref[slot, :, width:] = (kv[:, width:] + bias).astype(BF)
            for copy in copies(slot):
                copy.start()

    for slot in range(blocks):

        @pl.when(held[slot])
        def _(slot=slot):
            for copy in copies(slot):
                copy.wait()


def memory_rows(name, t, ids, memories, pieces, packs, local, earlier=None):
    blocks = ids.shape[0]
    _, length, width = memories[0].shape
    outs = [shape_of((blocks * length, 2 * width), BF), shape_of((blocks * length, width), BF)]
    more = () if earlier is None else tuple(earlier)
    count = 2 + len(memories) + 8
    return call(
        functools.partial(memory_body, pieces=pieces, first=earlier is None),
        name,
        (1,),
        [anywhere()] * len(memories)
        + pack_rows(2 * local, width, 1)
        + pack_rows(16, width, 5 * local // 16)
        + [anywhere()] * len(more),
        [anywhere()] * 2,
        outs,
        (t, ids, *memories, *packs, *packs, *more),
        scratch=[
            pltpu.VMEM((2 * width, width), BF),
            pltpu.VMEM((blocks, length, width), BF),
            pltpu.VMEM((blocks, length, 2 * width), BF),
            pltpu.SemaphoreType.DMA((blocks,)),
            pltpu.SemaphoreType.DMA((blocks,)),
            pltpu.SemaphoreType.DMA((blocks,)),
        ],
        prefetch=2,
        aliases={count: 0, count + 1: 1} if more else {},
    )


def block_grad_body(t_ref, dkv_ref, w0, w1, w2, w3, out_ref, w_ref):
    gather_pair(t_ref, (w0, w1, w2, w3), w_ref)
    out_ref[...] = nn(dkv_ref[...], w_ref[...]).astype(BF).reshape(out_ref.shape)


def block_grad(t, half, dkv, packs, local, blocks):
    rows, width = dkv.shape[0], dkv.shape[1] // 2
    length = rows // blocks
    steps = blocks // 4
    return call(
        block_grad_body,
        f"block_grad_{half}",
        (steps,),
        [pl.BlockSpec((2 * length, 2 * width), lambda i, *_: (half * steps + i, 0))] + pack_rows(2 * local, width, 1),
        pl.BlockSpec((2, length, width), lambda i, *_: (i, 0, 0)),
        shape_of((blocks // 2, length, width), BF),
        (t, dkv, *packs),
        scratch=[pltpu.VMEM((2 * width, width), BF)],
        prefetch=1,
    )


def return_body(t_ref, id_ref, *refs, pieces):
    out_ref, x_ref, semaphores = refs[len(pieces) :]
    blocks = id_ref.shape[0]
    step, steps = pl.program_id(0), pl.num_programs(0)
    sides = x_ref.shape[1]

    def fetch(at):
        for side in range(sides):
            slot = at % 2
            block = id_ref[at * sides + side]
            fetch_block(t_ref, block, blocks, refs, pieces, x_ref.at[slot, side], semaphores.at[slot, side])

    @pl.when(step == 0)
    def _():
        fetch(0)

    @pl.when(step + 1 < steps)
    def _():
        fetch(step + 1)

    now = step % 2
    for side in range(sides):
        pltpu.make_async_copy(refs[0].at[0], x_ref.at[now, side], semaphores.at[now, side]).wait()
        out_ref[side] = x_ref[now, side].astype(out_ref.dtype)


def return_blocks(t, slots, grads, pieces):
    blocks = slots.shape[0]
    sides = 4
    _, length, width = grads[0].shape
    return call(
        functools.partial(return_body, pieces=pieces),
        "return_blocks",
        (blocks // sides,),
        [anywhere()] * len(grads),
        pl.BlockSpec((sides, length, width), lambda i, *_: (i, 0, 0)),
        shape_of((blocks, length, width), F32),
        (t, slots, *grads),
        scratch=[pltpu.VMEM((2, sides, length, width), BF), pltpu.SemaphoreType.DMA((2, sides))],
        prefetch=2,
    )


def feed_body(ma, mb, ga, gb, w1_ref, w2_ref, b1_ref, oa, ob, da, db, ha, hb, ua, ub, sum_ref):
    curve = math.sqrt(2.0 / math.pi)
    total = None
    for m_ref, g_ref, out_ref, dm_ref, h_ref, du_ref in ((ma, ga, oa, da, ha, ua), (mb, gb, ob, db, hb, ub)):
        u = nn(m_ref[...], w1_ref[...]) + b1_ref[...]
        square = u * u
        bent = jnp.tanh(curve * (u + 0.044715 * u * square))
        half = 0.5 * (1.0 + bent)
        h = (u * half).astype(BF)
        h_ref[...] = h
        slope = half + 0.5 * u * (1.0 - bent * bent) * (curve * (1.0 + 3.0 * 0.044715 * square))
        du = (nt(g_ref[...], w2_ref[...]) * slope).astype(BF)
        du_ref[...] = du
        dm_ref[...] = nt(du, w1_ref[...]).astype(BF)
        out_ref[...] = nn(h, w2_ref[...]).astype(BF)
        part = column_sum(du.astype(F32))
        total = part if total is None else total + part
    add_rows(sum_ref, [total])


def feed(name, half, ms, gs, w1, w2, b1):
    rows, width = ms[0].shape
    hidden = w1.shape[1]
    row, wide = shape_of((rows, width), BF), shape_of((rows, hidden), BF)
    outs = [row] * 4 + [wide] * 4 + [shape_of((8, hidden), F32)]
    return list(call(
        feed_body,
        name,
        (1,),
        [whole(row)] * 2 + [pl.BlockSpec((rows, width), lambda i: (half, 0))] * 2 + [whole(w1), whole(w2), whole(b1)],
        [whole(out) for out in outs],
        outs,
        (*ms, *gs, w1, w2, b1),
    ))


def feed_weight_body(*refs):
    out_ref = refs[-1]
    count = (len(refs) - 1) // 7
    ms, dus, hs, gs = refs[: 2 * count], refs[2 * count : 4 * count], refs[4 * count : 6 * count], refs[6 * count : -1]
    rows = dus[0].shape[0]
    half = pl.num_programs(0) // 2

    @pl.when(pl.program_id(0) < half)
    def _():
        out_ref[...] = sum(tn(m[...], du[...]) for m, du in zip(ms, dus)).astype(BF)

    @pl.when(pl.program_id(0) >= half)
    def _():
        total = 0.0
        for index, h in enumerate(hs):
            side = index % 2
            total = total + tn(h[...], gs[index // 2][side * rows : (side + 1) * rows, :])
        out_ref[...] = total.astype(BF)


def feed_weight(ms, dus, hs, gs):
    rows, width = ms[0].shape
    hidden = hs[0].shape[1]
    tile = 256
    first, second = width // tile, hidden // tile
    return call(
        feed_weight_body,
        "feed_weight",
        (first + second,),
        [pl.BlockSpec((rows, tile), lambda i: (0, jnp.minimum(i, first - 1)))] * len(ms)
        + [whole(r) for r in dus]
        + [pl.BlockSpec((rows, tile), lambda i: (0, jnp.maximum(i - first, 0)))] * len(hs)
        + [whole(r) for r in gs],
        rows_of(tile, width),
        shape_of((width + hidden, width), BF),
        (*ms, *dus, *hs, *gs),
    )


def cross_weight_body(t_ref, *refs):
    pieces = len(PIECES)
    count = (len(refs) - 1 - 4 * pieces) // 2
    sources, buffers, semaphores = refs[:count], refs[count + 4 * pieces : -1], refs[-1]
    outs = [refs[count + rel * pieces : count + (rel + 1) * pieces] for rel in range(4)]
    local, width = outs[0][0].shape[1:]
    copies = [
        pltpu.make_async_copy(source, buffer, semaphores.at[index])
        for index, (source, buffer) in enumerate(zip(sources, buffers))
    ]
    for copy in copies:
        copy.start()
    dqc, b, o0, o1, o2, o3, g1, co_a, co_b, g2, memory, dkv = buffers

    def store(rel, index, part):
        for out_ref, (start, end) in zip(outs[rel], PIECES):
            if start <= index < end:
                out_ref[index - start] = part

    def place(index, grad):
        for group in range(4):
            part = grad[group * local : (group + 1) * local].astype(BF)
            for rel in range(4):

                @pl.when(t_ref[0] ^ rel == group)
                def _(rel=rel, part=part):
                    store(rel, index, part)

    copies[0].wait()
    copies[1].wait()
    place(0, tn(dqc[...], b[...]))
    for copy in copies[2:7]:
        copy.wait()
    for rel, o_ref in enumerate((o0, o1, o2, o3)):
        store(rel, 1, nn(o_ref[...], g1[...]).astype(BF))
    for copy in copies[7:10]:
        copy.wait()
    half = co_a.shape[0]
    place(4, tn(co_a[...], g2[:half, :]) + tn(co_b[...], g2[half:, :]))
    copies[10].wait()
    copies[11].wait()
    place(2, tn(dkv[:, :width], memory[...]))
    place(3, tn(dkv[:, width:], memory[...]))


def cross_weight(t, dqc, b, mixed, g1r, dkv, memory, co, g2r):
    width = b.shape[1]
    local = mixed[0].shape[0]
    args = (dqc, b, *mixed, g1r, *co, g2r, memory, dkv)
    outs = [shape_of((end - start, local, width), BF) for start, end in PIECES] * 4
    flat = call(
        cross_weight_body,
        "cross_weight",
        (1,),
        [anywhere()] * len(args),
        [whole(out) for out in outs],
        outs,
        (t, *args),
        scratch=[pltpu.VMEM(a.shape, a.dtype) for a in args] + [pltpu.SemaphoreType.DMA((len(args),))],
        prefetch=1,
    )
    return [tuple(flat[rel * len(PIECES) : (rel + 1) * len(PIECES)]) for rel in range(4)]


def input_grad_body(x_ref, da_ref, db_ref, dc_ref, g1_ref, gain_ref, out_ref):
    normed, inverse = standardize(x_ref[...].astype(F32))
    grad = da_ref[...].astype(F32) + db_ref[...].astype(F32) + dc_ref[...].astype(F32)
    out_ref[...] = g1_ref[...] + norm_pull(grad, normed, inverse, gain_ref[0:1, :])


def input_grad(x, parts, g1, gain):
    rows, width = x.shape
    tile = min(256, rows)
    row = rows_of(tile, width)
    return call(
        input_grad_body,
        "input_grad",
        (rows // tile,),
        [row] * 5 + [whole(gain)],
        row,
        shape_of((rows, width), F32),
        (x, *parts, g1, gain),
    )


def padded_tables(length):
    half = HEAD_DIM // 2
    frequency = np.float32(10000.0) ** (-np.arange(half, dtype=np.float32) / np.float32(half))
    angles = np.arange(length, dtype=np.float32)[:, None] * frequency[None, :]
    cosine = np.cos(angles.astype(np.float64)).astype(np.float32)
    sine = np.sin(angles.astype(np.float64)).astype(np.float32)
    zero = np.zeros_like(sine)
    return (
        jnp.asarray(np.concatenate([cosine, cosine, zero, zero], 1)),
        jnp.asarray(np.concatenate([-sine, zero, zero, zero], 1)),
        jnp.asarray(np.concatenate([zero, sine, zero, zero], 1)),
    )


def mask_lanes(segments):
    lane = lax.broadcasted_iota(jnp.int32, (segments.shape[0], LANES), 1)
    is_mask = (lane >= MASK_LANE) & (lane < MASK_LANE + DOCS)
    same = is_mask & (lane - MASK_LANE == segments[:, None])
    is_lse = (lane >= LSE_LANE) & (lane < LSE_LANE + 3)
    query_lanes = jnp.where(same, 1.0, 0.0).astype(BF)
    key_lanes = jnp.where(is_mask & ~same, NEGATIVE, jnp.where(is_lse, 1.0, 0.0)).astype(BF)
    return query_lanes, key_lanes


def pad_heads(values):
    lead = values.shape[:-1]
    heads = values.shape[-1] // HEAD_DIM
    values = values.reshape(lead + (heads, HEAD_DIM))
    values = jnp.pad(values, [(0, 0)] * (len(lead) + 1) + [(0, LANES - HEAD_DIM)])
    return values.reshape(lead[:-1] + (-1,))


def shards(
    layer_input,
    norm_gain,
    norm_bias,
    self_input_weight,
    self_input_bias,
    self_output_weight,
    out_bias,
    cross_query_weight,
    b_cross_q,
    w_cross_kv,
    b_cross_v,
    cross_output_weight,
    expand_weight_1,
    expand_bias_1,
    contract_weight_2,
    neighbours,
    segment_ids,
    span_map,
    cotangent,
):
    x = layer_input[0]
    rows, width = x.shape
    length = segment_ids.shape[1]
    local = self_input_weight.shape[2]
    heads = local // HEAD_DIM
    blocks, block_rows = neighbours.shape[1], neighbours.shape[2]
    grad_out = cotangent[0]
    index = lax.axis_index("tp")
    t = index.astype(jnp.int32).reshape(1)
    partners = [[(i, i ^ step) for i in range(4)] for step in (1, 2, 3)]

    tables = padded_tables(length)
    b_pad = pad_heads(self_input_bias)[None]
    piece = -(-(5 * local + 16) // (16 * lax.axis_size("dp"))) * 16
    w_pad, pack = prepare(
        self_input_weight.transpose(1, 2, 0),
        cross_query_weight.T,
        self_output_weight,
        w_cross_kv.transpose(1, 2, 0),
        cross_output_weight,
        b_cross_q[None],
        b_cross_v[None],
        piece * lax.axis_size("dp"),
    )
    qx, kx = mask_lanes(segment_ids[0])
    lane = lax.broadcasted_iota(jnp.int32, (1, LANES), 1)
    vx = jnp.where((lane >= HEAD_DIM) & (lane < HEAD_DIM + 3), 1.0, 0.0).astype(BF)
    core, chip, _ = partners

    half = blocks // 2

    across = lax.ppermute(x, "tp", chip)
    beside = lax.ppermute(x, "tp", core)
    a0, a1, c0, c1 = project_rows((0, 1), t, (x, beside), norm_gain, norm_bias, w_pad, b_pad, tables, heads)
    across, c0 = lax.optimization_barrier((across, c0))
    pack_piece, blocks_first, across = lax.optimization_barrier(
        (take_rows(pack, lax.axis_index("dp"), piece), neighbours[0][:half], across)
    )
    pack_piece = lax.ppermute(pack_piece, "tp", chip)
    blocks_first = lax.ppermute(blocks_first, "tp", chip)
    pack_across = lax.all_gather(pack_piece, "dp", axis=0, tiled=True)
    pack_beside = lax.ppermute(pack, "tp", core)
    xs = [x, beside, across, lax.ppermute(across, "tp", core)]
    blocks_beside = lax.ppermute(neighbours[0], "tp", core)
    a2, a3, c2, c3 = project_rows((2, 3), t, xs[2:], norm_gain, norm_bias, w_pad, b_pad, tables, heads)
    qe, ke, ve, ot, lse = attend(t, (c0, c1, c2, c3), qx, kx, vx)
    normed_first = [a0, a1, a2, a3]
    ot, blocks_first = follow(ot, blocks_first)
    mixed = exchange([ot[0], ot[1], ot[2], ot[3]], partners)
    blocks_second, mixed = follow(neighbours[0][half:], tuple(mixed))
    blocks_second = lax.ppermute(blocks_second, "tp", chip)
    packs = [pack, pack_beside, pack_across, lax.ppermute(pack_across, "tp", core)]

    block_ids = index * blocks + jnp.arange(blocks, dtype=jnp.int32)
    slot_ids = jnp.arange(span_map.shape[1], dtype=jnp.int32)
    slots = jnp.sum(jnp.where(span_map[0][None, :] == block_ids[:, None], slot_ids[None, :], 0), 1)
    chosen_ids = lax.dynamic_slice_in_dim(span_map[0], index * blocks, blocks, 0)

    x1, b, cq = after_attend(t, x, mixed, packs, out_bias, norm_gain, norm_bias)
    memories = [neighbours[0], blocks_beside, blocks_first, lax.ppermute(blocks_first, "tp", core)]
    pieces = [(0, 0, blocks), (1, 0, blocks), (2, 0, half), (3, 0, half)]
    memory_near = memory_rows("memory_near", t, chosen_ids, memories, pieces, packs, local)
    gathered, blocks_second, cq, memory_near = lax.optimization_barrier(
        (grad_out.astype(BF), blocks_second, cq, tuple(memory_near))
    )
    memories = [blocks_second, lax.ppermute(blocks_second, "tp", core)]
    pieces = [(2, half, half), (3, half, half)]
    grad_across = lax.ppermute(gathered, "tp", chip)
    grad_beside = lax.ppermute(gathered, "tp", core)
    kv, memory = memory_rows("memory_far", t, chosen_ids, memories, pieces, packs, local, memory_near)
    cross_args = (packs, local, out_bias, norm_gain, norm_bias)
    co_a, cross_lse_a, x2_a, m_a = cross(t, 0, cq, kv, x1, *cross_args)
    x1_late, m_a = lax.optimization_barrier((x1, m_a))
    co_b, cross_lse_b, x2_b, m_b = cross(t, 1, cq, kv, x1_late, *cross_args)

    feed_args = (expand_weight_1, contract_weight_2, expand_bias_1[None])
    m_a, grad_across = follow(m_a, grad_across)
    across_a = lax.ppermute(m_a, "tp", chip)
    beside_a = lax.ppermute(m_a, "tp", core)
    gs = [gathered, grad_beside, grad_across, lax.ppermute(grad_across, "tp", core)]
    near_a = feed("feed_near_0", 0, (m_a, beside_a), gs[:2], *feed_args)
    across_b = lax.ppermute(m_b, "tp", chip)
    beside_b = lax.ppermute(m_b, "tp", core)
    across_a, near_a[0] = lax.optimization_barrier((across_a, near_a[0]))
    diagonal_a = lax.ppermute(across_a, "tp", core)
    near_b = feed("feed_near_1", 1, (m_b, beside_b), gs[:2], *feed_args)
    diagonal_a, across_b, near_b[0] = lax.optimization_barrier((diagonal_a, across_b, near_b[0]))
    diagonal_b = lax.ppermute(across_b, "tp", core)
    far_a = feed("feed_far_0", 0, (across_a, diagonal_a), gs[2:], *feed_args)
    diagonal_b, far_a[0] = lax.optimization_barrier((diagonal_b, far_a[0]))
    far_b = feed("feed_far_1", 1, (across_b, diagonal_b), gs[2:], *feed_args)
    dm_far = [lax.ppermute(part[3], "tp", core) for part in (far_a, far_b)]
    sent = jnp.concatenate([rounded_sum(far_a[2], dm_far[0]), rounded_sum(far_b[2], dm_far[1])], 0)
    dm_across = lax.ppermute(sent, "tp", chip)
    dm_a, dm_b = [(part[2], lax.ppermute(part[3], "tp", core)) for part in (near_a, near_b)]
    ms = [m_a, m_b, beside_a, beside_b, across_a, across_b, diagonal_a, diagonal_b]
    ordered = [(near_a, 0), (near_b, 0), (near_a, 1), (near_b, 1), (far_a, 0), (far_b, 0), (far_a, 1), (far_b, 1)]
    grad_feed = feed_weight(ms, [f[6 + i] for f, i in ordered], [f[4 + i] for f, i in ordered], gs)

    out_far = [lax.ppermute(part[1], "tp", core) for part in (far_a, far_b, near_a, near_b)]
    out_sent = (rounded_sum(far_a[0], out_far[0]), rounded_sum(far_b[0], out_far[1]))
    dm_across, grad_feed = lax.optimization_barrier((dm_across, grad_feed))
    summed_feed = lax.psum(grad_feed, "dp")
    g2r, dkv, g1, g1r, dqc, *dos, small_middle = middle_back(
        t, (x2_a, x2_b), (dm_a, dm_b), dm_across, (cross_lse_a, cross_lse_b), grad_out, packs, local, norm_gain, cq, kv, x1
    )

    dos = exchange(dos, partners)
    dos[1], g1r = lax.optimization_barrier((dos[1], g1r))
    grad_cross = cross_weight(t, dqc, b, mixed, g1r, dkv, memory, (co_a, co_b), g2r)
    dos[2], dos[3], grad_cross, out_sent = lax.optimization_barrier((dos[2], dos[3], tuple(grad_cross), out_sent))
    out_across = tuple(lax.ppermute(part, "tp", chip) for part in out_sent)
    grad_far = [tuple(lax.ppermute(part, "tp", core) for part in grad_cross[r]) for r in (3, 1)]
    dp = attend_back(t, qe, ke, ve, dos, ot, lse, tables)
    dp, grad_far[0], out_across = lax.optimization_barrier((dp, grad_far[0], out_across))
    across = tuple(lax.ppermute(rounded_sum(a, b), "tp", chip) for a, b in zip(grad_cross[2], grad_far[0]))
    grad_qkv, grad_bqkv = qkv_weight(dp, normed_first)
    da3, da1, small_a = input_back((3, 1), (xs[3], xs[1]), dp, w_pad)
    da2, da0, small_b = input_back((2, 0), (xs[2], xs[0]), dp, w_pad)
    dkv, small_a, small_b = lax.optimization_barrier((dkv, small_a, small_b))
    grad_near = [block_grad(t, side, dkv, packs, local, blocks) for side in range(2)]
    da0, da1, da2, da3, grad_qkv, small_a, grad_near, grad_far[1], across, summed_feed = lax.optimization_barrier(
        (da0, da1, da2, da3, grad_qkv, small_a, tuple(grad_near), grad_far[1], across, summed_feed)
    )

    small = small_rows(small_a, small_b, small_middle)
    small = small + lax.ppermute(small, "tp", core)
    small = small + lax.ppermute(small, "tp", chip)
    small, grad_near = lax.optimization_barrier((small, grad_near))
    blocks_far = [lax.ppermute(value, "tp", chip) for value in grad_near]
    da, _ = collect([da0, da1, da2, da3], partners)
    sums = (near_a[8], near_b[8], far_a[8], far_b[8])
    last = lax.psum(last_rows(grad_cross[0], grad_far[1], across, grad_qkv, small, grad_bqkv, sums), "dp")
    returned = [*grad_near] + [lax.ppermute(value, "tp", core) for value in grad_near]
    returned += blocks_far + [lax.ppermute(value, "tp", core) for value in blocks_far]
    halves = [(rel, start, half) for rel in range(4) for start in (0, half)]
    grad_memory = return_blocks(t, slots, returned, halves)
    grad_input = input_grad(x, da, g1, norm_gain)
    kept = jnp.concatenate([rounded_sum(near_a[0], out_far[2]), rounded_sum(near_b[0], out_far[3])], 0)
    layer_output = jnp.concatenate([x2_a, x2_b], 0) + kept.astype(F32) + jnp.concatenate(out_across, 0).astype(F32) + out_bias[2]

    grad_w1, grad_w2 = widen_feed(summed_feed, width)
    last, grad_memory, grad_input, layer_output, grad_w1, grad_w2 = lax.optimization_barrier(
        (last, grad_memory, grad_input, layer_output, grad_w1, grad_w2)
    )
    cq_t, grad_so, kv_t, grad_co, qkv_t, gains, shifts, biases, bqkv, bq, bv, b1 = widen(t, last, local)

    return (
        layer_output[None],
        grad_input[None],
        grad_memory[None],
        gains,
        shifts,
        qkv_t.transpose(2, 0, 1),
        bqkv,
        grad_so,
        biases,
        cq_t.T,
        bq[0],
        kv_t.transpose(2, 0, 1),
        bv[0],
        grad_co,
        grad_w1,
        b1[0],
        grad_w2,
    )


def solution(mesh):
    return jax.shard_map(
        shards,
        mesh=mesh,
        in_specs=(
            P("dp", "tp", None),
            P(),
            P(),
            P(None, None, "tp"),
            P(None, "tp"),
            P("tp", None),
            P(),
            P(None, "tp"),
            P("tp"),
            P(None, None, "tp"),
            P("tp"),
            P("tp", None),
            P(None, "tp"),
            P("tp"),
            P("tp", None),
            P("dp", "tp", None, None),
            P("dp", None),
            P("dp", None),
            P("dp", "tp", None),
        ),
        out_specs=(
            P("dp", "tp", None),
            P("dp", "tp", None),
            P("dp", "tp", None, None),
            P(),
            P(),
            P(None, None, "tp"),
            P(None, "tp"),
            P("tp", None),
            P(),
            P(None, "tp"),
            P("tp"),
            P(None, None, "tp"),
            P("tp"),
            P("tp", None),
            P(None, "tp"),
            P("tp"),
            P("tp", None),
        ),
        check_vma=False,
    )
```

```python
import functools
import math

import jax
import jax.numpy as jnp
import numpy as np
from jax import lax
from jax.experimental import pallas as pl
from jax.experimental.pallas import tpu as pltpu
from jax.sharding import PartitionSpec as P

HEAD_DIM = 64
SPAN = 64
LANES = 128
QUERY_ROWS = 256
NEGATIVE = -1e30
NORM_EPS = 1e-05
BF = jnp.bfloat16
F32 = jnp.float32
VMEM_BYTES = 56 * 1024 * 1024

PIECES = ((0, 2), (2, 4), (4, 5))

COST_US = {"widen": 30}

DOCS = 5
MASK_LANE = HEAD_DIM
LSE_LANE = HEAD_DIM + DOCS


def nn(a, b):
    return lax.dot_general(a, b, (((1,), (0,)), ((), ())), preferred_element_type=F32)


def nt(a, b):
    return lax.dot_general(a, b, (((1,), (1,)), ((), ())), preferred_element_type=F32)


def tn(a, b):
    return lax.dot_general(a, b, (((0,), (0,)), ((), ())), preferred_element_type=F32)


def call(body, name, grid, in_specs, out_specs, out_shape, args, scratch=(), prefetch=0, aliases=None):
    return pl.pallas_call(
        body,
        out_shape=out_shape,
        grid_spec=pltpu.PrefetchScalarGridSpec(
            num_scalar_prefetch=prefetch,
            grid=grid,
            in_specs=in_specs,
            out_specs=out_specs,
            scratch_shapes=list(scratch),
        ),
        compiler_params=pltpu.CompilerParams(
            vmem_limit_bytes=VMEM_BYTES, dimension_semantics=("arbitrary",) * len(grid)
        ),
        cost_estimate=pl.CostEstimate(flops=int(COST_US.get(name, 0.01) * 1e9), bytes_accessed=1, transcendentals=0),
        name=name,
        input_output_aliases=aliases or {},
    )(*args)


def whole(array):
    zeros = (0,) * len(array.shape)
    return pl.BlockSpec(array.shape, lambda *_: zeros)


def rows_of(tile, width):
    return pl.BlockSpec((tile, width), lambda i, *_: (i, 0))


def shape_of(shape, dtype):
    return jax.ShapeDtypeStruct(shape, dtype)


def standardize(values):
    centre = values - jnp.mean(values, -1, keepdims=True)
    inverse = lax.rsqrt(jnp.mean(centre * centre, -1, keepdims=True) + NORM_EPS)
    return centre * inverse, inverse


def norm_pull(grad, normed, inverse, gain):
    scaled = grad * gain
    return inverse * (
        scaled
        - jnp.mean(scaled, -1, keepdims=True)
        - normed * jnp.mean(scaled * normed, -1, keepdims=True)
    )


def column_sum(values):
    return jnp.sum(values, 0, keepdims=True)


def add_rows(out_ref, rows):
    @pl.when(pl.program_id(0) == 0)
    def _():
        out_ref[...] = jnp.zeros_like(out_ref)

    for index, row in enumerate(rows):
        out_ref[index : index + 1, :] += row


def follow(operand, earlier):
    return lax.optimization_barrier((operand, earlier))


def collect(parts, partners, earlier=None):
    core, chip, _ = partners
    far = lax.ppermute(parts[3], "tp", core)
    near = lax.ppermute(parts[1], "tp", core)
    sent = rounded_sum(parts[2], far)
    if earlier is not None:
        sent, earlier = follow(sent, earlier)
    return [parts[0], near, lax.ppermute(sent, "tp", chip)], earlier


def take_rows(values, part, rows):
    return lax.dynamic_slice_in_dim(values, part * rows, rows, 0)


def rounded_sum(*parts):
    return sum(part.astype(F32) for part in parts).astype(BF)


def small_rows_body(first_a, first_b, middle_ref, out_ref):
    out_ref[...] = jnp.zeros_like(out_ref)
    out_ref[0:2, :] = first_a[0:2, :] + first_b[0:2, :]
    out_ref[2:11, :] = middle_ref[0:9, :]


def small_rows(first_a, first_b, middle):
    args = (first_a, first_b, middle)
    return call(small_rows_body, "small_rows", (1,), [whole(a) for a in args], whole(middle), shape_of(middle.shape, F32), args)


def last_rows_body(*refs):
    parts = [refs[n * len(PIECES) : (n + 1) * len(PIECES)] for n in range(3)]
    qkv_ref, small_ref, bias_ref, s0, s1, s2, s3, out_ref = refs[3 * len(PIECES) :]
    heads = bias_ref.shape[2] // LANES
    local, width = parts[0][0].shape[1:]
    start, rows, count = 0, qkv_ref.shape[0], small_ref.shape[0]
    for own_ref, near_ref, far_ref in zip(*parts):
        for j in range(own_ref.shape[0]):
            total = own_ref[j].astype(F32) + near_ref[j].astype(F32) + far_ref[j].astype(F32)
            out_ref[start : start + local, :] = total.astype(BF)
            start += local
    out_ref[start : start + rows, :] = qkv_ref[...]
    start += rows
    out_ref[start : start + count, :] = small_ref[...].astype(BF)
    parts = [bias_ref[j][:, h * LANES : h * LANES + HEAD_DIM] for j in range(3) for h in range(heads)]
    bias = jnp.concatenate(parts + [jnp.zeros((1, width - rows), F32)], 1)
    other = sum(ref[0:1, :] for ref in (s0, s1, s2, s3))
    row = lax.broadcasted_iota(jnp.int32, (count, width), 0)
    out_ref[start + count :, :] = jnp.where(row == 0, bias, jnp.where(row == 1, other, 0.0)).astype(BF)


def last_rows(own, near, far, qkv, small, bias, sums):
    width = qkv.shape[1]
    total = sum(part.shape[0] * part.shape[1] for part in own)
    args = (*own, *near, *far, qkv, small, bias, *sums)
    out = shape_of((total + qkv.shape[0] + 2 * small.shape[0], width), BF)
    return call(last_rows_body, "last_rows", (1,), [whole(a) for a in args], whole(out), out, args)


def widen_body(x_ref, cq_ref, so_ref, kv_ref, co_ref, qkv_ref, bqkv_ref, b1_ref):
    local, width = cq_ref.shape
    start = 0

    def take(count):
        nonlocal start
        start += count
        return x_ref[start - count : start, :].astype(F32)

    cq_ref[...] = take(local)
    so_ref[...] = take(local)
    for target in (kv_ref.at[0], kv_ref.at[1], co_ref, qkv_ref.at[0], qkv_ref.at[1], qkv_ref.at[2]):
        target[...] = take(local)
    start += 16
    tail = take(16)
    bqkv_ref[...] = jnp.concatenate([tail[0:1, j * local : (j + 1) * local] for j in range(3)], 0)
    b1_ref[...] = tail[1:2]


def widen(rows, local):
    width = rows.shape[1]
    shapes = [(local, width), (local, width), (2, local, width), (local, width), (3, local, width)]
    shapes += [(3, local), (1, width)]
    outs = [shape_of(shape, F32) for shape in shapes]
    return call(widen_body, "widen", (1,), [whole(rows)], [whole(o) for o in outs], outs, (rows,))


def finish_body(t_ref, own_ref, other_ref, gain_ref, shift_ref, out_ref, bq_ref, bv_ref):
    small = own_ref[...] + other_ref[...]
    local = bq_ref.shape[1]

    def pick(rows):
        return jnp.concatenate([small[row : row + 1] for row in rows], 0)

    def mine(row):
        cuts = [row[:, group * local : (group + 1) * local] for group in range(4)]
        return sum(jnp.where(t_ref[0] == group, cut, 0.0) for group, cut in enumerate(cuts))

    gain_ref[...] = pick((0, 2, 4))
    shift_ref[...] = pick((1, 3, 5))
    out_ref[...] = pick((6, 7, 8))
    bq_ref[...] = mine(small[9:10])
    bv_ref[...] = mine(small[10:11])


def finish(t, own, other, local):
    width = own.shape[1]
    outs = [shape_of(shape, F32) for shape in [(3, width)] * 3 + [(1, local)] * 2]
    args = (own, other)
    return call(finish_body, "finish", (1,), [whole(a) for a in args], [whole(o) for o in outs], outs, (t, *args), prefetch=1)


def widen_feed_body(x_ref, first_ref, second_ref):
    rows = first_ref.shape[0]
    first_ref[...] = x_ref[:rows, :].astype(F32)
    second_ref[...] = x_ref[rows:, :].astype(F32)


def widen_feed(rows, width):
    outs = [shape_of((width, width), F32), shape_of((rows.shape[0] - width, width), F32)]
    return call(widen_feed_body, "widen_feed", (1,), [whole(rows)], [whole(o) for o in outs], outs, (rows,))


def exchange(parts, partners):
    return [parts[0]] + [lax.ppermute(parts[r], "tp", partners[r - 1]) for r in (1, 2, 3)]


def gather_rows(t_ref, refs, target, start=0):
    @pl.when(pl.program_id(0) == 0)
    def _():
        for rel, ref in enumerate(refs):
            count = ref.shape[0]
            target[pl.ds(pl.multiple_of((t_ref[0] ^ rel) * count + start, 16), count), :] = ref[...]


def gather_bias(t_ref, refs, start, local):
    rows = [ref[...].astype(F32)[0:1] for ref in refs]
    rows = [row[:, start : start + local] + row[:, start + local : start + 2 * local] for row in rows]
    groups = []
    for group in range(4):
        groups.append(sum(jnp.where(t_ref[0] ^ rel == group, row, 0.0) for rel, row in enumerate(rows)))
    return jnp.concatenate(groups, 1)


def pack_rows(local, width, part):
    return [pl.BlockSpec((local, width), lambda i, *_: (part, 0))] * 4


def prepare_body(qkv_ref, cq_ref, so_ref, kv_ref, co_ref, bq_ref, bv_ref, w_ref, pack_ref):
    local, width = so_ref.shape
    zeros = jnp.zeros((LANES - HEAD_DIM, width), BF)
    for j in range(3 * local // HEAD_DIM):
        part = qkv_ref[j * HEAD_DIM // local, j * HEAD_DIM % local : j * HEAD_DIM % local + HEAD_DIM, :]
        w_ref[j * LANES : j * LANES + HEAD_DIM, :] = part
        w_ref[j * LANES + HEAD_DIM : (j + 1) * LANES, :] = zeros
    for index, part in enumerate((cq_ref[...], so_ref[...], kv_ref[0], kv_ref[1], co_ref[...])):
        pack_ref[index * local : (index + 1) * local, :] = part
    parts = []
    for ref in (bq_ref, bv_ref):
        high = ref[...].astype(BF).astype(F32)
        parts += [high, ref[...] - high]
    row = jnp.concatenate(parts, 1)
    count = pack_ref.shape[0] - 5 * local
    first = lax.broadcasted_iota(jnp.int32, (count, width), 0) == 0
    pack_ref[5 * local :, :] = jnp.where(first, row, 0.0).astype(BF)


def prepare(qkv, cq, so, kv, co, bq, bv, pack_size):
    local, width = so.shape
    outs = [shape_of((3 * local // HEAD_DIM * LANES, width), BF), shape_of((pack_size, width), BF)]
    args = (qkv, cq, so, kv, co, bq, bv)
    return call(prepare_body, "prepare", (1,), [whole(a) for a in args], [whole(o) for o in outs], outs, args)


def qkv_body(t_ref, xa, xb, gain_ref, shift_ref, w_ref, b_ref, ca, sa, ta, cb, sb, tb, aa, ab, oa, ob):
    heads = oa.shape[1]
    for x_ref, cos_ref, left_ref, right_ref, a_ref, out_ref in ((xa, ca, sa, ta, aa, oa), (xb, cb, sb, tb, ab, ob)):
        normed, _ = standardize(x_ref[...].astype(F32))
        a = (normed * gain_ref[0:1, :] + shift_ref[0:1, :]).astype(BF)
        a_ref[...] = a
        proj = nt(a, w_ref[...]) + b_ref[...]
        cos, left, right = cos_ref[...], left_ref[...], right_ref[...]
        for j in range(3 * heads):
            part = proj[:, j * LANES : (j + 1) * LANES]
            if j < 2 * heads:
                part = part * cos + pltpu.roll(part, 96, 1) * left + pltpu.roll(part, 32, 1) * right
            if j < heads:
                part = part * (1.0 / math.sqrt(HEAD_DIM))
            out_ref[j // heads, j % heads] = part.astype(BF)


def project_rows(rels, t, xs, gain, shift, w, b, tables, heads):
    rows, width = xs[0].shape
    tile = min(256, rows)
    steps = rows // tile

    def table(rel):
        return pl.BlockSpec((tile, LANES), lambda i, t_ref: ((t_ref[0] ^ rel) * steps + i, 0))

    row = rows_of(tile, width)
    out = pl.BlockSpec((3, heads, tile, LANES), lambda i, t_ref: (0, 0, i, 0))
    return call(
        qkv_body,
        f"qkv_{rels[0]}{rels[1]}",
        (steps,),
        [row, row, whole(gain), whole(shift), whole(w), whole(b)] + [table(rels[0])] * 3 + [table(rels[1])] * 3,
        [row, row, out, out],
        [shape_of((rows, width), BF)] * 2 + [shape_of((3, heads, rows, LANES), BF)] * 2,
        (t, *xs, gain, shift, w, b, *tables, *tables),
        prefetch=1,
    )


def causal_corner(scores):
    keys = lax.broadcasted_iota(jnp.int32, scores.shape, 0)
    queries = lax.broadcasted_iota(jnp.int32, scores.shape, 1)
    return jnp.where(keys <= queries, scores, NEGATIVE)


def attend_body(t_ref, c0, c1, c2, c3, qx_ref, kx_ref, vx_ref, qe_ref, ke_ref, ve_ref, ot_ref, lse_ref, vt_ref):
    t = t_ref[0]
    rows = c0.shape[2]
    for rel, chunk in enumerate((c0, c1, c2, c3)):
        place = pl.ds(pl.multiple_of((t ^ rel) * rows, rows), rows)
        qe_ref[0, place, :] = chunk[0, 0] + qx_ref[place, :]
        ke_ref[0, place, :] = chunk[1, 0] + kx_ref[place, :]
        values = chunk[2, 0] + vx_ref[...]
        ve_ref[0, place, :] = values
        vt_ref[:, place] = values.astype(F32).T.astype(BF)
    step = QUERY_ROWS
    for low in range(0, qe_ref.shape[1], step):
        high = low + step
        query = qe_ref[0, low:high, :]
        corner = causal_corner(nt(ke_ref[0, low:high, :], query))
        top = jnp.max(corner, 0, keepdims=True)
        if low:
            earlier = nt(ke_ref[0, :low, :], query)
            top = jnp.maximum(top, jnp.max(earlier, 0, keepdims=True))
        mixed = nn(vt_ref[:, low:high], jnp.exp(corner - top).astype(BF))
        if low:
            mixed = mixed + nn(vt_ref[:, :low], jnp.exp(earlier - top).astype(BF))
        total = mixed[HEAD_DIM : HEAD_DIM + 1, :]
        lse_ref[0, :, low:high] = top + jnp.log(total)
        begin = low % rows
        ot_ref[t ^ (low // rows), :, begin : begin + step] = (mixed[:HEAD_DIM] / total).astype(BF)


def attend(t, chunks, qx, kx, vx):
    _, heads, rows, _ = chunks[0].shape
    length = qx.shape[0]
    chunk = pl.BlockSpec((3, 1, rows, LANES), lambda h, t_ref: (0, h, 0, 0))
    plane = pl.BlockSpec((1, length, LANES), lambda h, t_ref: (h, 0, 0))
    padded = shape_of((heads, length, LANES), BF)
    return call(
        attend_body,
        "attend",
        (heads,),
        [chunk] * 4 + [whole(qx), whole(kx), whole(vx)],
        [
            plane,
            plane,
            plane,
            pl.BlockSpec((4, HEAD_DIM, rows), lambda h, t_ref: (0, h, 0)),
            pl.BlockSpec((1, 1, length), lambda h, t_ref: (h, 0, 0)),
        ],
        [padded, padded, padded, shape_of((4, heads * HEAD_DIM, rows), BF), shape_of((heads, 1, length), F32)],
        (t, *chunks, qx, kx, vx),
        scratch=[pltpu.VMEM((LANES, length), BF)],
        prefetch=1,
    )


def three_parts(values):
    first = values.astype(BF).astype(F32)
    second = (values - first).astype(BF).astype(F32)
    return first, second, values - first - second


def attend_back_body(
    t_ref, qe_ref, ke_ref, ve_ref, d0, d1, d2, d3, ot_ref, lse_ref, cos_ref, sa_ref, sb_ref, out_ref,
    qt_ref, kt_ref, dt_ref, dk_ref, dv_ref,
):
    t = t_ref[0]
    rows = d0.shape[1]
    step = QUERY_ROWS
    length = qe_ref.shape[1]
    for rel, chunk in enumerate((d0, d1, d2, d3)):
        place = pl.ds(pl.multiple_of((t ^ rel) * rows, rows), rows)
        grad = chunk[...].astype(F32)
        delta = three_parts(jnp.sum(grad * ot_ref[rel].astype(F32), 0, keepdims=True))
        padded = jnp.concatenate([grad, jnp.zeros_like(grad)], 0)
        row = lax.broadcasted_iota(jnp.int32, padded.shape, 0)
        for index in range(3):
            padded = jnp.where(row == HEAD_DIM + index, -delta[index], padded)
        dt_ref[:, place] = padded.astype(BF)
    for low in range(0, length, rows):
        high = low + rows
        kt_ref[:, low:high] = ke_ref[0, low:high, :].astype(F32).T.astype(BF)
        turned = qe_ref[0, low:high, :].astype(F32).T
        row = lax.broadcasted_iota(jnp.int32, turned.shape, 0)
        pieces = three_parts(lse_ref[0, :, low:high])
        for index in range(3):
            turned = jnp.where(row == LSE_LANE + index, -pieces[index], turned)
        qt_ref[:, low:high] = turned.astype(BF)
    dk_ref[...] = jnp.zeros_like(dk_ref)
    dv_ref[...] = jnp.zeros_like(dv_ref)

    def unrotate(grad, place):
        return (
            grad * cos_ref[place, :]
            - pltpu.roll(grad, 96, 1) * sa_ref[place, :]
            - pltpu.roll(grad, 32, 1) * sb_ref[place, :]
        )

    for low in range(0, length, step):
        high = low + step
        query, query_t, grad_t = qe_ref[0, low:high, :], qt_ref[:, low:high], dt_ref[:, low:high]
        dq_t = None
        for begin, end in ((0, low), (low, high)):
            if begin == end:
                continue
            scores = nn(ke_ref[0, begin:end, :], query_t)
            if begin == low:
                scores = causal_corner(scores)
            prob = jnp.exp(scores)
            grad_scores = (prob * nn(ve_ref[0, begin:end, :], grad_t)).astype(BF)
            dv_ref[begin:end, :] += nt(prob.astype(BF), grad_t)
            dk_ref[begin:end, :] += nn(grad_scores, query)
            part = nn(kt_ref[:, begin:end], grad_scores)
            dq_t = part if dq_t is None else dq_t + part
        start = low % rows
        grad_query = unrotate(dq_t.T, slice(low, high)) * (1.0 / math.sqrt(HEAD_DIM))
        out_ref[t ^ (low // rows), 0, 0, start : start + step, :] = grad_query.astype(BF)
    for low in range(0, length, rows):
        place = slice(low, low + rows)
        rel = t ^ (low // rows)
        out_ref[rel, 1, 0] = unrotate(dk_ref[place, :], place).astype(BF)
        lane = lax.broadcasted_iota(jnp.int32, (rows, LANES), 1)
        out_ref[rel, 2, 0] = jnp.where(lane < HEAD_DIM, dv_ref[place, :], 0.0).astype(BF)


def attend_back(t, qe, ke, ve, grads, ot, lse, tables):
    heads, length, _ = qe.shape
    rows = grads[0].shape[1]
    plane = pl.BlockSpec((1, length, LANES), lambda h, t_ref: (h, 0, 0))
    grad = pl.BlockSpec((HEAD_DIM, rows), lambda h, t_ref: (h, 0))
    return call(
        attend_back_body,
        "attend_back",
        (heads,),
        [plane] * 3
        + [grad] * 4
        + [
            pl.BlockSpec((4, HEAD_DIM, rows), lambda h, t_ref: (0, h, 0)),
            pl.BlockSpec((1, 1, length), lambda h, t_ref: (h, 0, 0)),
        ]
        + [whole(table) for table in tables],
        pl.BlockSpec((4, 3, 1, rows, LANES), lambda h, t_ref: (0, 0, h, 0, 0)),
        shape_of((4, 3, heads, rows, LANES), BF),
        (t, qe, ke, ve, *grads, ot, lse, *tables),
        scratch=[pltpu.VMEM((LANES, length), BF)] * 3 + [pltpu.VMEM((length, LANES), F32)] * 2,
        prefetch=1,
    )


def input_back_body(xa, xb, da, db, w_ref, oa, ob, small_ref):
    heads = da.shape[2]
    totals = []
    for x_ref, dp_ref, out_ref in ((xa, da, oa), (xb, db, ob)):
        grads = jnp.concatenate([dp_ref[0, j // heads, j % heads] for j in range(3 * heads)], 1)
        grad = nn(grads, w_ref[...])
        normed, _ = standardize(x_ref[...].astype(F32))
        out_ref[...] = grad.astype(BF)
        totals.append((column_sum(grad * normed), column_sum(grad)))
    add_rows(small_ref, [totals[0][0] + totals[1][0], totals[0][1] + totals[1][1]])


def input_back(rels, xs, dp, w):
    rows, width = xs[0].shape
    heads = dp.shape[2]
    tile = min(256, rows)
    row = rows_of(tile, width)

    def part(rel):
        return pl.BlockSpec((1, 3, heads, tile, LANES), lambda i: (rel, 0, 0, i, 0))

    return call(
        input_back_body,
        f"input_back_{rels[0]}{rels[1]}",
        (rows // tile,),
        [row, row, part(rels[0]), part(rels[1]), whole(w)],
        [row, row, pl.BlockSpec((8, width), lambda i: (0, 0))],
        [shape_of((rows, width), BF)] * 2 + [shape_of((8, width), F32)],
        (*xs, dp, dp, w),
    )


def qkv_weight_body(dp_ref, a0, a1, a2, a3, out_ref, bias_ref):
    heads = dp_ref.shape[2]
    total, sums = None, None
    for rel, a_ref in enumerate((a0, a1, a2, a3)):
        grads = jnp.concatenate([dp_ref[rel, 0, h] for h in range(heads)], 1)
        part, part_sum = tn(grads, a_ref[...]), column_sum(grads.astype(F32))
        total = part if total is None else total + part
        sums = part_sum if sums is None else sums + part_sum
    for h in range(heads):
        out_ref[h * HEAD_DIM : (h + 1) * HEAD_DIM, :] = total[h * LANES : h * LANES + HEAD_DIM].astype(BF)
    bias_ref[0] = sums


def qkv_weight(dp, normed):
    _, _, heads, rows, _ = dp.shape
    width = normed[0].shape[1]
    local = heads * HEAD_DIM
    return call(
        qkv_weight_body,
        "qkv_weight",
        (3,),
        [pl.BlockSpec((4, 1, heads, rows, LANES), lambda j: (0, j, 0, 0, 0))] + [whole(a) for a in normed],
        [rows_of(local, width), pl.BlockSpec((1, 1, heads * LANES), lambda j: (j, 0, 0))],
        [shape_of((3 * local, width), BF), shape_of((3, 1, heads * LANES), F32)],
        (dp, *normed),
    )


def after_attend_body(
    t_ref, x_ref, o0, o1, o2, o3, w0, w1, w2, w3, q0, q1, q2, q3, b0, b1, b2, b3, bias_ref, gain_ref, shift_ref,
    x1_ref, b_ref, cq_ref, wq_ref,
):
    gather_rows(t_ref, (q0, q1, q2, q3), wq_ref)
    total = x_ref[...].astype(F32) + bias_ref[0:1, :]
    for o_ref, w_ref in ((o0, w0), (o1, w1), (o2, w2), (o3, w3)):
        total = total + tn(o_ref[...], w_ref[...])
    x1_ref[...] = total
    normed, _ = standardize(total)
    b = (normed * gain_ref[1:2, :] + shift_ref[1:2, :]).astype(BF)
    b_ref[...] = b
    bias = gather_bias(t_ref, (b0, b1, b2, b3), 0, w0.shape[0])
    cq_ref[...] = ((nt(b, wq_ref[...]) + bias) * (1.0 / math.sqrt(HEAD_DIM))).astype(BF)


def after_attend(t, x, mixed, packs, out_bias, gain, shift):
    rows, width = x.shape
    local = mixed[0].shape[0]
    tile = min(256, rows)
    return call(
        after_attend_body,
        "after_attend",
        (rows // tile,),
        [rows_of(tile, width)]
        + [pl.BlockSpec((local, tile), lambda i, *_: (0, i))] * 4
        + pack_rows(local, width, 1)
        + pack_rows(local, width, 0)
        + pack_rows(16, width, 5 * local // 16)
        + [whole(out_bias), whole(gain), whole(shift)],
        [rows_of(tile, width)] * 3,
        [shape_of((rows, width), F32), shape_of((rows, width), BF), shape_of((rows, width), BF)],
        (t, x, *mixed, *packs, *packs, *packs, out_bias, gain, shift),
        scratch=[pltpu.VMEM((width, width), BF)],
        prefetch=1,
    )


def split_pair(values):
    lane = lax.broadcasted_iota(jnp.int32, values.shape, 1)
    zero = jnp.zeros_like(values)
    return jnp.concatenate(
        [jnp.where(lane < HEAD_DIM, values, zero), jnp.where(lane >= HEAD_DIM, values, zero)], 0
    )


def join_pair(values):
    rows = values.shape[0] // 2
    lane = lax.broadcasted_iota(jnp.int32, (rows, values.shape[1]), 1)
    return jnp.where(lane < HEAD_DIM, values[:rows], values[rows:])


def lane_cuts(width):
    return [slice(start, start + LANES) for start in range(0, width, LANES)]


def cross_body(
    t_ref, cq_ref, kv_ref, x1_ref, w0, w1, w2, w3, bias_ref, gain_ref, shift_ref, co_ref, lse_ref, x2_ref, m_ref, w_ref
):
    gather_rows(t_ref, (w0, w1, w2, w3), w_ref)
    width = cq_ref.shape[1]
    spans, side, _ = lse_ref.shape
    keys = kv_ref.shape[0] // spans
    cuts = lane_cuts(width)
    for span in range(spans):
        place = slice(span * SPAN, (span + 1) * SPAN)
        query = cq_ref[place, :]
        key, value = kv_ref[span * keys : (span + 1) * keys, :width], kv_ref[span * keys : (span + 1) * keys, width:]
        scores = [nt(key[:, cut], split_pair(query[:, cut])) for cut in cuts]
        tops = [jnp.max(score, 0, keepdims=True) for score in scores]
        shifted = [jnp.exp(score - top) for score, top in zip(scores, tops)]
        totals = [jnp.sum(part, 0, keepdims=True) for part in shifted]
        probs = [(part * (1.0 / total)).astype(BF) for part, total in zip(shifted, totals)]
        mixed = [join_pair(tn(prob, value[:, cut])) for prob, cut in zip(probs, cuts)]
        co_ref[place, :] = jnp.concatenate(mixed, 1).astype(BF)
        rows = [top + jnp.log(total) for top, total in zip(tops, totals)]
        lse_ref[span] = jnp.concatenate(rows + [jnp.zeros((side - len(rows), LANES), F32)], 0)
    total = x1_ref[...] + nn(co_ref[...], w_ref[...]) + bias_ref[1:2, :]
    x2_ref[...] = total
    normed, _ = standardize(total)
    m_ref[...] = (normed * gain_ref[2:3, :] + shift_ref[2:3, :]).astype(BF)


def cross(t, half, cq, kv, x1, packs, local, out_bias, gain, shift):
    rows, width = x1.shape
    tile = rows // 2
    ratio = kv.shape[0] // rows
    side = -(-(width // LANES) // 8) * 8
    spans = tile // SPAN

    def rows_at(count, columns):
        return pl.BlockSpec((count, columns), lambda i, *_: (half, 0))

    row = rows_at(tile, width)
    outs = [
        shape_of((tile, width), BF),
        shape_of((spans, side, LANES), F32),
        shape_of((tile, width), F32),
        shape_of((tile, width), BF),
    ]
    return call(
        cross_body,
        f"cross_{half}",
        (1,),
        [row, rows_at(ratio * tile, 2 * width), row]
        + pack_rows(local, width, 4)
        + [whole(out_bias), whole(gain), whole(shift)],
        [whole(out) for out in outs],
        outs,
        (t, cq, kv, x1, *packs, out_bias, gain, shift),
        scratch=[pltpu.VMEM((width, width), BF)],
        prefetch=1,
    )


def middle_back_body(
    t_ref, x2a, x2b, da0, da1, db0, db1, lsea, lseb, across_ref, g_ref, gain_ref, cq_ref, kv_ref, x1_ref,
    c0, c1, c2, c3, q0, q1, q2, q3, w0, w1, w2, w3,
    g2r_ref, dkv_ref, g1_ref, g1r_ref, dqc_ref, d0, d1, d2, d3, small_ref,
    dco_ref, dq_ref, x2_ref, dm_ref, lse_ref, co_w_ref, wq_ref,
):
    gather_rows(t_ref, (c0, c1, c2, c3), co_w_ref)
    gather_rows(t_ref, (q0, q1, q2, q3), wq_ref)
    for side, (x2, parts, lse) in enumerate(((x2a, (da0, da1), lsea), (x2b, (db0, db1), lseb))):

        @pl.when(pl.program_id(0) == side)
        def _(x2=x2, parts=parts, lse=lse):
            x2_ref[...] = x2[...]
            dm_ref[...] = sum(part[...].astype(F32) for part in parts) + across_ref[...].astype(F32)
            lse_ref[...] = lse[...]

    width = cq_ref.shape[1]
    spans = lse_ref.shape[0]
    keys = kv_ref.shape[0] // spans
    cuts = lane_cuts(width)
    grad_m = dm_ref[...]
    normed_m, inverse = standardize(x2_ref[...])
    g = g_ref[...]
    g2 = g + norm_pull(grad_m, normed_m, inverse, gain_ref[2:3, :])
    g2r = g2.astype(BF)
    g2r_ref[...] = g2r
    dco_ref[...] = nt(g2r, co_w_ref[...]).astype(BF)
    for span in range(spans):
        place = slice(span * SPAN, (span + 1) * SPAN)
        block = slice(span * keys, (span + 1) * keys)
        query, grad = cq_ref[place, :], dco_ref[place, :]
        key, value = kv_ref[block, :width], kv_ref[block, width:]
        stats = lse_ref[span]
        queries = [split_pair(query[:, cut]) for cut in cuts]
        grads = [split_pair(grad[:, cut]) for cut in cuts]
        probs = [jnp.exp(nt(key[:, cut], q) - stats[j : j + 1]) for j, (cut, q) in enumerate(zip(cuts, queries))]
        pulls = [nt(value[:, cut], part) for cut, part in zip(cuts, grads)]
        deltas = [jnp.sum(prob * pull, 0, keepdims=True) for prob, pull in zip(probs, pulls)]
        scores = [(prob * (pull - delta)).astype(BF) for prob, pull, delta in zip(probs, pulls, deltas)]
        keys_back = [nn(score, q).astype(BF) for score, q in zip(scores, queries)]
        values_back = [nn(prob.astype(BF), part).astype(BF) for prob, part in zip(probs, grads)]
        dkv_ref[block, :] = jnp.concatenate(keys_back + values_back, 1)
        dq_ref[place, :] = jnp.concatenate([join_pair(tn(score, key[:, cut])) for score, cut in zip(scores, cuts)], 1)
    dqc = (dq_ref[...] * (1.0 / math.sqrt(HEAD_DIM))).astype(BF)
    dqc_ref[...] = dqc
    grad_b = nn(dqc, wq_ref[...])
    normed_b, inverse = standardize(x1_ref[...])
    g1 = g2 + norm_pull(grad_b, normed_b, inverse, gain_ref[1:2, :])
    g1_ref[...] = g1
    g1r = g1.astype(BF)
    g1r_ref[...] = g1r
    for w_ref, d_ref in ((w0, d0), (w1, d1), (w2, d2), (w3, d3)):
        d_ref[...] = nt(w_ref[...], g1r).astype(BF)
    add_rows(
        small_ref,
        [
            column_sum(grad_b * normed_b),
            column_sum(grad_b),
            column_sum(grad_m * normed_m),
            column_sum(grad_m),
            column_sum(g1),
            column_sum(g2),
            column_sum(g),
            column_sum(dqc.astype(F32)),
            column_sum(dkv_ref[:, width:].astype(F32)),
        ],
    )


def middle_back(t, x2, dm, across, lse, g, packs, local, gain, cq, kv, x1):
    rows, width = x1.shape
    tile = rows // 2
    ratio = kv.shape[0] // rows
    row = rows_of(tile, width)
    wide = rows_of(ratio * tile, 2 * width)
    turned = pl.BlockSpec((local, tile), lambda i, *_: (0, i))
    half = shape_of((rows, width), BF)
    halves = (*x2, *dm[0], *dm[1], *lse)
    return call(
        middle_back_body,
        "middle_back",
        (2,),
        [whole(value) for value in halves]
        + [row, row, whole(gain), row, wide, row]
        + pack_rows(local, width, 4)
        + pack_rows(local, width, 0)
        + pack_rows(local, width, 1),
        [row, wide, row, row, row] + [turned] * 4 + [pl.BlockSpec((16, width), lambda i, *_: (0, 0))],
        [half, shape_of(kv.shape, BF), shape_of((rows, width), F32), half, half]
        + [shape_of((local, rows), BF)] * 4
        + [shape_of((16, width), F32)],
        (t, *halves, across, g, gain, cq, kv, x1, *packs, *packs, *packs),
        scratch=[
            pltpu.VMEM((tile, width), BF),
            pltpu.VMEM((tile, width), F32),
            pltpu.VMEM((tile, width), F32),
            pltpu.VMEM((tile, width), F32),
            pltpu.VMEM(lse[0].shape, F32),
            pltpu.VMEM((width, width), BF),
            pltpu.VMEM((width, width), BF),
        ],
        prefetch=1,
    )


def block_place(block, blocks, t, piece):
    rel, start, count = piece
    inside = block % blocks - start
    held = ((block // blocks) ^ t == rel) & (inside >= 0) & (inside < count)
    return held, jnp.where(held, inside, 0)


def anywhere():
    return pl.BlockSpec(memory_space=pl.ANY)


def fetch_block(t_ref, block, blocks, refs, pieces, target, semaphore):
    found = False
    for ref, piece in zip(refs, pieces):
        held, index = block_place(block, blocks, t_ref[0], piece)

        @pl.when(held)
        def _(ref=ref, index=index):
            pltpu.make_async_copy(ref.at[index], target, semaphore).start()

        found = held | found
    return found


def gather_pair(t_ref, refs, target):
    width = target.shape[1]
    local = refs[0].shape[0] // 2
    gather_rows(t_ref, [ref.at[:local, :] for ref in refs], target)
    gather_rows(t_ref, [ref.at[local:, :] for ref in refs], target, width)


def memory_body(t_ref, id_ref, *refs, pieces, first):
    count = len(pieces)
    packs, biases = refs[count : count + 4], refs[count + 4 : count + 8]
    kv_ref, chosen_ref, w_ref, x_ref, out_ref, in_sem, kv_sem, out_sem = refs[count + 8 + (0 if first else 2) :]
    blocks, length, width = x_ref.shape
    held = [
        fetch_block(t_ref, id_ref[slot], blocks, refs, pieces, x_ref.at[slot], in_sem.at[slot])
        for slot in range(blocks)
    ]
    gather_pair(t_ref, packs, w_ref)
    local = packs[0].shape[0] // 2
    bias = gather_bias(t_ref, biases, 2 * local, local)

    def copies(slot):
        rows = pl.ds(slot * length, length)
        return (
            pltpu.make_async_copy(out_ref.at[slot], kv_ref.at[rows, :], kv_sem.at[slot]),
            pltpu.make_async_copy(x_ref.at[slot], chosen_ref.at[rows, :], out_sem.at[slot]),
        )

    for slot in range(blocks):

        @pl.when(held[slot])
        def _(slot=slot):
            pltpu.make_async_copy(refs[0].at[0], x_ref.at[slot], in_sem.at[slot]).wait()
            kv = nt(x_ref[slot], w_ref[...])
            out_ref[slot, :, :width] = kv[:, :width].astype(BF)
            out_ref[slot, :, width:] = (kv[:, width:] + bias).astype(BF)
            for copy in copies(slot):
                copy.start()

    for slot in range(blocks):

        @pl.when(held[slot])
        def _(slot=slot):
            for copy in copies(slot):
                copy.wait()


def memory_rows(name, t, ids, memories, pieces, packs, local, earlier=None):
    blocks = ids.shape[0]
    _, length, width = memories[0].shape
    outs = [shape_of((blocks * length, 2 * width), BF), shape_of((blocks * length, width), BF)]
    more = () if earlier is None else tuple(earlier)
    count = 2 + len(memories) + 8
    return call(
        functools.partial(memory_body, pieces=pieces, first=earlier is None),
        name,
        (1,),
        [anywhere()] * len(memories)
        + pack_rows(2 * local, width, 1)
        + pack_rows(16, width, 5 * local // 16)
        + [anywhere()] * len(more),
        [anywhere()] * 2,
        outs,
        (t, ids, *memories, *packs, *packs, *more),
        scratch=[
            pltpu.VMEM((2 * width, width), BF),
            pltpu.VMEM((blocks, length, width), BF),
            pltpu.VMEM((blocks, length, 2 * width), BF),
            pltpu.SemaphoreType.DMA((blocks,)),
            pltpu.SemaphoreType.DMA((blocks,)),
            pltpu.SemaphoreType.DMA((blocks,)),
        ],
        prefetch=2,
        aliases={count: 0, count + 1: 1} if more else {},
    )


def block_grad_body(t_ref, dkv_ref, w0, w1, w2, w3, out_ref, w_ref):
    gather_pair(t_ref, (w0, w1, w2, w3), w_ref)
    out_ref[...] = nn(dkv_ref[...], w_ref[...]).astype(BF).reshape(out_ref.shape)


def block_grad(t, half, dkv, packs, local, blocks):
    rows, width = dkv.shape[0], dkv.shape[1] // 2
    length = rows // blocks
    steps = blocks // 4
    return call(
        block_grad_body,
        f"block_grad_{half}",
        (steps,),
        [pl.BlockSpec((2 * length, 2 * width), lambda i, *_: (half * steps + i, 0))] + pack_rows(2 * local, width, 1),
        pl.BlockSpec((2, length, width), lambda i, *_: (i, 0, 0)),
        shape_of((blocks // 2, length, width), BF),
        (t, dkv, *packs),
        scratch=[pltpu.VMEM((2 * width, width), BF)],
        prefetch=1,
    )


def return_body(t_ref, id_ref, *refs, pieces):
    out_ref, x_ref, semaphores = refs[len(pieces) :]
    blocks = id_ref.shape[0]
    step, steps = pl.program_id(0), pl.num_programs(0)
    sides = x_ref.shape[1]

    def fetch(at):
        for side in range(sides):
            slot = at % 2
            block = id_ref[at * sides + side]
            fetch_block(t_ref, block, blocks, refs, pieces, x_ref.at[slot, side], semaphores.at[slot, side])

    @pl.when(step == 0)
    def _():
        fetch(0)

    @pl.when(step + 1 < steps)
    def _():
        fetch(step + 1)

    now = step % 2
    for side in range(sides):
        pltpu.make_async_copy(refs[0].at[0], x_ref.at[now, side], semaphores.at[now, side]).wait()
        out_ref[side] = x_ref[now, side].astype(out_ref.dtype)


def return_blocks(t, slots, grads, pieces):
    blocks = slots.shape[0]
    sides = 4
    _, length, width = grads[0].shape
    return call(
        functools.partial(return_body, pieces=pieces),
        "return_blocks",
        (blocks // sides,),
        [anywhere()] * len(grads),
        pl.BlockSpec((sides, length, width), lambda i, *_: (i, 0, 0)),
        shape_of((blocks, length, width), F32),
        (t, slots, *grads),
        scratch=[pltpu.VMEM((2, sides, length, width), BF), pltpu.SemaphoreType.DMA((2, sides))],
        prefetch=2,
    )


def feed_body(ma, mb, ga, gb, w1_ref, w2_ref, b1_ref, oa, ob, da, db, ha, hb, ua, ub, sum_ref):
    curve = math.sqrt(2.0 / math.pi)
    total = None
    for m_ref, g_ref, out_ref, dm_ref, h_ref, du_ref in ((ma, ga, oa, da, ha, ua), (mb, gb, ob, db, hb, ub)):
        u = nn(m_ref[...], w1_ref[...]) + b1_ref[...]
        square = u * u
        bent = jnp.tanh(curve * (u + 0.044715 * u * square))
        half = 0.5 * (1.0 + bent)
        h = (u * half).astype(BF)
        h_ref[...] = h
        slope = half + 0.5 * u * (1.0 - bent * bent) * (curve * (1.0 + 3.0 * 0.044715 * square))
        du = (nt(g_ref[...], w2_ref[...]) * slope).astype(BF)
        du_ref[...] = du
        dm_ref[...] = nt(du, w1_ref[...]).astype(BF)
        out_ref[...] = nn(h, w2_ref[...]).astype(BF)
        part = column_sum(du.astype(F32))
        total = part if total is None else total + part
    add_rows(sum_ref, [total])


def feed(name, half, ms, gs, w1, w2, b1):
    rows, width = ms[0].shape
    hidden = w1.shape[1]
    row, wide = shape_of((rows, width), BF), shape_of((rows, hidden), BF)
    outs = [row] * 4 + [wide] * 4 + [shape_of((8, hidden), F32)]
    return list(call(
        feed_body,
        name,
        (1,),
        [whole(row)] * 2 + [pl.BlockSpec((rows, width), lambda i: (half, 0))] * 2 + [whole(w1), whole(w2), whole(b1)],
        [whole(out) for out in outs],
        outs,
        (*ms, *gs, w1, w2, b1),
    ))


def feed_weight_body(*refs):
    out_ref = refs[-1]
    count = (len(refs) - 1) // 7
    ms, dus, hs, gs = refs[: 2 * count], refs[2 * count : 4 * count], refs[4 * count : 6 * count], refs[6 * count : -1]
    rows = dus[0].shape[0]
    half = pl.num_programs(0) // 2

    @pl.when(pl.program_id(0) < half)
    def _():
        out_ref[...] = sum(tn(m[...], du[...]) for m, du in zip(ms, dus)).astype(BF)

    @pl.when(pl.program_id(0) >= half)
    def _():
        total = 0.0
        for index, h in enumerate(hs):
            side = index % 2
            total = total + tn(h[...], gs[index // 2][side * rows : (side + 1) * rows, :])
        out_ref[...] = total.astype(BF)


def feed_weight(ms, dus, hs, gs):
    rows, width = ms[0].shape
    hidden = hs[0].shape[1]
    tile = 256
    first, second = width // tile, hidden // tile
    return call(
        feed_weight_body,
        "feed_weight",
        (first + second,),
        [pl.BlockSpec((rows, tile), lambda i: (0, jnp.minimum(i, first - 1)))] * len(ms)
        + [whole(r) for r in dus]
        + [pl.BlockSpec((rows, tile), lambda i: (0, jnp.maximum(i - first, 0)))] * len(hs)
        + [whole(r) for r in gs],
        rows_of(tile, width),
        shape_of((width + hidden, width), BF),
        (*ms, *dus, *hs, *gs),
    )


def cross_weight_body(t_ref, *refs):
    pieces = len(PIECES)
    count = (len(refs) - 1 - 4 * pieces) // 2
    sources, buffers, semaphores = refs[:count], refs[count + 4 * pieces : -1], refs[-1]
    outs = [refs[count + rel * pieces : count + (rel + 1) * pieces] for rel in range(4)]
    local, width = outs[0][0].shape[1:]
    copies = [
        pltpu.make_async_copy(source, buffer, semaphores.at[index])
        for index, (source, buffer) in enumerate(zip(sources, buffers))
    ]
    for copy in copies:
        copy.start()
    dqc, b, o0, o1, o2, o3, g1, co_a, co_b, g2, memory, dkv = buffers

    def store(rel, index, part):
        for out_ref, (start, end) in zip(outs[rel], PIECES):
            if start <= index < end:
                out_ref[index - start] = part

    def place(index, grad):
        for group in range(4):
            part = grad[group * local : (group + 1) * local].astype(BF)
            for rel in range(4):

                @pl.when(t_ref[0] ^ rel == group)
                def _(rel=rel, part=part):
                    store(rel, index, part)

    copies[0].wait()
    copies[1].wait()
    place(0, tn(dqc[...], b[...]))
    for copy in copies[2:7]:
        copy.wait()
    for rel, o_ref in enumerate((o0, o1, o2, o3)):
        store(rel, 1, nn(o_ref[...], g1[...]).astype(BF))
    for copy in copies[7:10]:
        copy.wait()
    half = co_a.shape[0]
    place(4, tn(co_a[...], g2[:half, :]) + tn(co_b[...], g2[half:, :]))
    copies[10].wait()
    copies[11].wait()
    place(2, tn(dkv[:, :width], memory[...]))
    place(3, tn(dkv[:, width:], memory[...]))


def cross_weight(t, dqc, b, mixed, g1r, dkv, memory, co, g2r):
    width = b.shape[1]
    local = mixed[0].shape[0]
    args = (dqc, b, *mixed, g1r, *co, g2r, memory, dkv)
    outs = [shape_of((end - start, local, width), BF) for start, end in PIECES] * 4
    flat = call(
        cross_weight_body,
        "cross_weight",
        (1,),
        [anywhere()] * len(args),
        [whole(out) for out in outs],
        outs,
        (t, *args),
        scratch=[pltpu.VMEM(a.shape, a.dtype) for a in args] + [pltpu.SemaphoreType.DMA((len(args),))],
        prefetch=1,
    )
    return [tuple(flat[rel * len(PIECES) : (rel + 1) * len(PIECES)]) for rel in range(4)]


def input_grad_body(x_ref, da_ref, db_ref, dc_ref, g1_ref, gain_ref, out_ref):
    normed, inverse = standardize(x_ref[...].astype(F32))
    grad = da_ref[...].astype(F32) + db_ref[...].astype(F32) + dc_ref[...].astype(F32)
    out_ref[...] = g1_ref[...] + norm_pull(grad, normed, inverse, gain_ref[0:1, :])


def input_grad(x, parts, g1, gain):
    rows, width = x.shape
    tile = min(256, rows)
    row = rows_of(tile, width)
    return call(
        input_grad_body,
        "input_grad",
        (rows // tile,),
        [row] * 5 + [whole(gain)],
        row,
        shape_of((rows, width), F32),
        (x, *parts, g1, gain),
    )


def padded_tables(length):
    half = HEAD_DIM // 2
    frequency = np.float32(10000.0) ** (-np.arange(half, dtype=np.float32) / np.float32(half))
    angles = np.arange(length, dtype=np.float32)[:, None] * frequency[None, :]
    cosine = np.cos(angles.astype(np.float64)).astype(np.float32)
    sine = np.sin(angles.astype(np.float64)).astype(np.float32)
    zero = np.zeros_like(sine)
    return (
        jnp.asarray(np.concatenate([cosine, cosine, zero, zero], 1)),
        jnp.asarray(np.concatenate([-sine, zero, zero, zero], 1)),
        jnp.asarray(np.concatenate([zero, sine, zero, zero], 1)),
    )


def mask_lanes(segments):
    lane = lax.broadcasted_iota(jnp.int32, (segments.shape[0], LANES), 1)
    is_mask = (lane >= MASK_LANE) & (lane < MASK_LANE + DOCS)
    same = is_mask & (lane - MASK_LANE == segments[:, None])
    is_lse = (lane >= LSE_LANE) & (lane < LSE_LANE + 3)
    query_lanes = jnp.where(same, 1.0, 0.0).astype(BF)
    key_lanes = jnp.where(is_mask & ~same, NEGATIVE, jnp.where(is_lse, 1.0, 0.0)).astype(BF)
    return query_lanes, key_lanes


def pad_heads(values):
    lead = values.shape[:-1]
    heads = values.shape[-1] // HEAD_DIM
    values = values.reshape(lead + (heads, HEAD_DIM))
    values = jnp.pad(values, [(0, 0)] * (len(lead) + 1) + [(0, LANES - HEAD_DIM)])
    return values.reshape(lead[:-1] + (-1,))


def shards(
    layer_input,
    norm_gain,
    norm_bias,
    self_input_weight,
    self_input_bias,
    self_output_weight,
    out_bias,
    cross_query_weight,
    b_cross_q,
    w_cross_kv,
    b_cross_v,
    cross_output_weight,
    expand_weight_1,
    expand_bias_1,
    contract_weight_2,
    neighbours,
    segment_ids,
    span_map,
    cotangent,
):
    x = layer_input[0]
    rows, width = x.shape
    length = segment_ids.shape[1]
    local = self_input_weight.shape[2]
    heads = local // HEAD_DIM
    blocks, block_rows = neighbours.shape[1], neighbours.shape[2]
    grad_out = cotangent[0]
    index = lax.axis_index("tp")
    t = index.astype(jnp.int32).reshape(1)
    partners = [[(i, i ^ step) for i in range(4)] for step in (1, 2, 3)]

    tables = padded_tables(length)
    b_pad = pad_heads(self_input_bias)[None]
    piece = -(-(5 * local + 16) // (16 * lax.axis_size("dp"))) * 16
    w_pad, pack = prepare(
        self_input_weight.transpose(1, 2, 0),
        cross_query_weight.T,
        self_output_weight,
        w_cross_kv.transpose(1, 2, 0),
        cross_output_weight,
        b_cross_q[None],
        b_cross_v[None],
        piece * lax.axis_size("dp"),
    )
    qx, kx = mask_lanes(segment_ids[0])
    lane = lax.broadcasted_iota(jnp.int32, (1, LANES), 1)
    vx = jnp.where((lane >= HEAD_DIM) & (lane < HEAD_DIM + 3), 1.0, 0.0).astype(BF)
    core, chip, _ = partners

    half = blocks // 2

    across = lax.ppermute(x, "tp", chip)
    beside = lax.ppermute(x, "tp", core)
    a0, a1, c0, c1 = project_rows((0, 1), t, (x, beside), norm_gain, norm_bias, w_pad, b_pad, tables, heads)
    across, c0 = lax.optimization_barrier((across, c0))
    pack_piece, blocks_first, across = lax.optimization_barrier(
        (take_rows(pack, lax.axis_index("dp"), piece), neighbours[0][:half], across)
    )
    pack_piece = lax.ppermute(pack_piece, "tp", chip)
    blocks_first = lax.ppermute(blocks_first, "tp", chip)
    pack_across = lax.all_gather(pack_piece, "dp", axis=0, tiled=True)
    pack_beside = lax.ppermute(pack, "tp", core)
    xs = [x, beside, across, lax.ppermute(across, "tp", core)]
    blocks_beside = lax.ppermute(neighbours[0], "tp", core)
    a2, a3, c2, c3 = project_rows((2, 3), t, xs[2:], norm_gain, norm_bias, w_pad, b_pad, tables, heads)
    qe, ke, ve, ot, lse = attend(t, (c0, c1, c2, c3), qx, kx, vx)
    normed_first = [a0, a1, a2, a3]
    ot, blocks_first = follow(ot, blocks_first)
    mixed = exchange([ot[0], ot[1], ot[2], ot[3]], partners)
    blocks_second, mixed = follow(neighbours[0][half:], tuple(mixed))
    blocks_second = lax.ppermute(blocks_second, "tp", chip)
    packs = [pack, pack_beside, pack_across, lax.ppermute(pack_across, "tp", core)]

    block_ids = index * blocks + jnp.arange(blocks, dtype=jnp.int32)
    slot_ids = jnp.arange(span_map.shape[1], dtype=jnp.int32)
    slots = jnp.sum(jnp.where(span_map[0][None, :] == block_ids[:, None], slot_ids[None, :], 0), 1)
    chosen_ids = lax.dynamic_slice_in_dim(span_map[0], index * blocks, blocks, 0)

    x1, b, cq = after_attend(t, x, mixed, packs, out_bias, norm_gain, norm_bias)
    memories = [neighbours[0], blocks_beside, blocks_first, lax.ppermute(blocks_first, "tp", core)]
    pieces = [(0, 0, blocks), (1, 0, blocks), (2, 0, half), (3, 0, half)]
    memory_near = memory_rows("memory_near", t, chosen_ids, memories, pieces, packs, local)
    gathered, blocks_second, cq, memory_near = lax.optimization_barrier(
        (grad_out.astype(BF), blocks_second, cq, tuple(memory_near))
    )
    memories = [blocks_second, lax.ppermute(blocks_second, "tp", core)]
    pieces = [(2, half, half), (3, half, half)]
    grad_across = lax.ppermute(gathered, "tp", chip)
    grad_beside = lax.ppermute(gathered, "tp", core)
    kv, memory = memory_rows("memory_far", t, chosen_ids, memories, pieces, packs, local, memory_near)
    cross_args = (packs, local, out_bias, norm_gain, norm_bias)
    co_a, cross_lse_a, x2_a, m_a = cross(t, 0, cq, kv, x1, *cross_args)
    x1_late, m_a = lax.optimization_barrier((x1, m_a))
    co_b, cross_lse_b, x2_b, m_b = cross(t, 1, cq, kv, x1_late, *cross_args)

    feed_args = (expand_weight_1, contract_weight_2, expand_bias_1[None])
    m_a, grad_across = follow(m_a, grad_across)
    across_a = lax.ppermute(m_a, "tp", chip)
    beside_a = lax.ppermute(m_a, "tp", core)
    gs = [gathered, grad_beside, grad_across, lax.ppermute(grad_across, "tp", core)]
    near_a = feed("feed_near_0", 0, (m_a, beside_a), gs[:2], *feed_args)
    across_b = lax.ppermute(m_b, "tp", chip)
    beside_b = lax.ppermute(m_b, "tp", core)
    across_a, near_a[0] = lax.optimization_barrier((across_a, near_a[0]))
    diagonal_a = lax.ppermute(across_a, "tp", core)
    near_b = feed("feed_near_1", 1, (m_b, beside_b), gs[:2], *feed_args)
    diagonal_a, across_b, near_b[0] = lax.optimization_barrier((diagonal_a, across_b, near_b[0]))
    diagonal_b = lax.ppermute(across_b, "tp", core)
    far_a = feed("feed_far_0", 0, (across_a, diagonal_a), gs[2:], *feed_args)
    diagonal_b, far_a[0] = lax.optimization_barrier((diagonal_b, far_a[0]))
    far_b = feed("feed_far_1", 1, (across_b, diagonal_b), gs[2:], *feed_args)
    dm_far = [lax.ppermute(part[3], "tp", core) for part in (far_a, far_b)]
    sent = jnp.concatenate([rounded_sum(far_a[2], dm_far[0]), rounded_sum(far_b[2], dm_far[1])], 0)
    dm_across = lax.ppermute(sent, "tp", chip)
    dm_a, dm_b = [(part[2], lax.ppermute(part[3], "tp", core)) for part in (near_a, near_b)]
    ms = [m_a, m_b, beside_a, beside_b, across_a, across_b, diagonal_a, diagonal_b]
    ordered = [(near_a, 0), (near_b, 0), (near_a, 1), (near_b, 1), (far_a, 0), (far_b, 0), (far_a, 1), (far_b, 1)]
    grad_feed = feed_weight(ms, [f[6 + i] for f, i in ordered], [f[4 + i] for f, i in ordered], gs)

    out_far = [lax.ppermute(part[1], "tp", core) for part in (far_a, far_b, near_a, near_b)]
    out_sent = (rounded_sum(far_a[0], out_far[0]), rounded_sum(far_b[0], out_far[1]))
    dm_across, grad_feed = lax.optimization_barrier((dm_across, grad_feed))
    summed_feed = lax.psum(grad_feed, "dp")
    g2r, dkv, g1, g1r, dqc, *dos, small_middle = middle_back(
        t, (x2_a, x2_b), (dm_a, dm_b), dm_across, (cross_lse_a, cross_lse_b), grad_out, packs, local, norm_gain, cq, kv, x1
    )

    dos = exchange(dos, partners)
    dos[1], g1r = lax.optimization_barrier((dos[1], g1r))
    grad_cross = cross_weight(t, dqc, b, mixed, g1r, dkv, memory, (co_a, co_b), g2r)
    dos[2], dos[3], grad_cross, out_sent = lax.optimization_barrier((dos[2], dos[3], tuple(grad_cross), out_sent))
    out_across = tuple(lax.ppermute(part, "tp", chip) for part in out_sent)
    grad_far = [tuple(lax.ppermute(part, "tp", core) for part in grad_cross[r]) for r in (3, 1)]
    dp = attend_back(t, qe, ke, ve, dos, ot, lse, tables)
    dp, grad_far[0], out_across = lax.optimization_barrier((dp, grad_far[0], out_across))
    across = tuple(lax.ppermute(rounded_sum(a, b), "tp", chip) for a, b in zip(grad_cross[2], grad_far[0]))
    grad_qkv, grad_bqkv = qkv_weight(dp, normed_first)
    da3, da1, small_a = input_back((3, 1), (xs[3], xs[1]), dp, w_pad)
    da2, da0, small_b = input_back((2, 0), (xs[2], xs[0]), dp, w_pad)
    dkv, small_a, small_b = lax.optimization_barrier((dkv, small_a, small_b))
    grad_near = [block_grad(t, side, dkv, packs, local, blocks) for side in range(2)]
    small = small_rows(small_a, small_b, small_middle)
    sums = (near_a[8], near_b[8], far_a[8], far_b[8])
    last = last_rows(grad_cross[0], grad_far[1], across, grad_qkv, small, grad_bqkv, sums)
    da0, da1, da2, da3, last, grad_near, summed_feed = lax.optimization_barrier(
        (da0, da1, da2, da3, last, tuple(grad_near), summed_feed)
    )

    last = lax.psum(last, "dp")
    blocks_far = [lax.ppermute(value, "tp", chip) for value in grad_near]
    da, _ = collect([da0, da1, da2, da3], partners)
    returned = [*grad_near] + [lax.ppermute(value, "tp", core) for value in grad_near]
    returned += blocks_far + [lax.ppermute(value, "tp", core) for value in blocks_far]
    halves = [(rel, start, half) for rel in range(4) for start in (0, half)]
    grad_memory = return_blocks(t, slots, returned, halves)
    grad_input = input_grad(x, da, g1, norm_gain)
    kept = jnp.concatenate([rounded_sum(near_a[0], out_far[2]), rounded_sum(near_b[0], out_far[3])], 0)
    layer_output = jnp.concatenate([x2_a, x2_b], 0) + kept.astype(F32) + jnp.concatenate(out_across, 0).astype(F32) + out_bias[2]

    grad_w1, grad_w2 = widen_feed(summed_feed, width)
    last, grad_memory, grad_input, layer_output, grad_w1, grad_w2 = lax.optimization_barrier(
        (last, grad_memory, grad_input, layer_output, grad_w1, grad_w2)
    )
    small = last[8 * local : 8 * local + 16]
    small = small.astype(F32) + lax.ppermute(small, "tp", core).astype(F32)
    gains, shifts, biases, bq, bv = finish(t, small, lax.ppermute(small, "tp", chip), local)
    cq_t, grad_so, kv_t, grad_co, qkv_t, bqkv, b1 = widen(last, local)

    return (
        layer_output[None],
        grad_input[None],
        grad_memory[None],
        gains,
        shifts,
        qkv_t.transpose(2, 0, 1),
        bqkv,
        grad_so,
        biases,
        cq_t.T,
        bq[0],
        kv_t.transpose(2, 0, 1),
        bv[0],
        grad_co,
        grad_w1,
        b1[0],
        grad_w2,
    )


def solution(mesh):
    return jax.shard_map(
        shards,
        mesh=mesh,
        in_specs=(
            P("dp", "tp", None),
            P(),
            P(),
            P(None, None, "tp"),
            P(None, "tp"),
            P("tp", None),
            P(),
            P(None, "tp"),
            P("tp"),
            P(None, None, "tp"),
            P("tp"),
            P("tp", None),
            P(None, "tp"),
            P("tp"),
            P("tp", None),
            P("dp", "tp", None, None),
            P("dp", None),
            P("dp", None),
            P("dp", "tp", None),
        ),
        out_specs=(
            P("dp", "tp", None),
            P("dp", "tp", None),
            P("dp", "tp", None, None),
            P(),
            P(),
            P(None, None, "tp"),
            P(None, "tp"),
            P("tp", None),
            P(),
            P(None, "tp"),
            P("tp"),
            P(None, None, "tp"),
            P("tp"),
            P("tp", None),
            P(None, "tp"),
            P("tp"),
            P("tp", None),
        ),
        check_vma=False,
    )
```

```python
import functools
import math

import jax
import jax.numpy as jnp
import numpy as np
from jax import lax
from jax.experimental import pallas as pl
from jax.experimental.pallas import tpu as pltpu
from jax.sharding import PartitionSpec as P

HEAD_DIM = 64
SPAN = 64
LANES = 128
QUERY_ROWS = 256
NEGATIVE = -1e30
NORM_EPS = 1e-05
BF = jnp.bfloat16
F32 = jnp.float32
VMEM_BYTES = 56 * 1024 * 1024

PIECES = ((0, 2), (2, 4), (4, 5))

COST_US = {"widen": 30}

DOCS = 5
MASK_LANE = HEAD_DIM
LSE_LANE = HEAD_DIM + DOCS


def nn(a, b):
    return lax.dot_general(a, b, (((1,), (0,)), ((), ())), preferred_element_type=F32)


def nt(a, b):
    return lax.dot_general(a, b, (((1,), (1,)), ((), ())), preferred_element_type=F32)


def tn(a, b):
    return lax.dot_general(a, b, (((0,), (0,)), ((), ())), preferred_element_type=F32)


def call(body, name, grid, in_specs, out_specs, out_shape, args, scratch=(), prefetch=0, aliases=None):
    return pl.pallas_call(
        body,
        out_shape=out_shape,
        grid_spec=pltpu.PrefetchScalarGridSpec(
            num_scalar_prefetch=prefetch,
            grid=grid,
            in_specs=in_specs,
            out_specs=out_specs,
            scratch_shapes=list(scratch),
        ),
        compiler_params=pltpu.CompilerParams(
            vmem_limit_bytes=VMEM_BYTES, dimension_semantics=("arbitrary",) * len(grid)
        ),
        cost_estimate=pl.CostEstimate(flops=int(COST_US.get(name, 0.01) * 1e9), bytes_accessed=1, transcendentals=0),
        name=name,
        input_output_aliases=aliases or {},
    )(*args)


def whole(array):
    zeros = (0,) * len(array.shape)
    return pl.BlockSpec(array.shape, lambda *_: zeros)


def rows_of(tile, width):
    return pl.BlockSpec((tile, width), lambda i, *_: (i, 0))


def shape_of(shape, dtype):
    return jax.ShapeDtypeStruct(shape, dtype)


def standardize(values):
    centre = values - jnp.mean(values, -1, keepdims=True)
    inverse = lax.rsqrt(jnp.mean(centre * centre, -1, keepdims=True) + NORM_EPS)
    return centre * inverse, inverse


def norm_pull(grad, normed, inverse, gain):
    scaled = grad * gain
    return inverse * (
        scaled
        - jnp.mean(scaled, -1, keepdims=True)
        - normed * jnp.mean(scaled * normed, -1, keepdims=True)
    )


def column_sum(values):
    return jnp.sum(values, 0, keepdims=True)


def add_rows(out_ref, rows):
    @pl.when(pl.program_id(0) == 0)
    def _():
        out_ref[...] = jnp.zeros_like(out_ref)

    for index, row in enumerate(rows):
        out_ref[index : index + 1, :] += row


def follow(operand, earlier):
    return lax.optimization_barrier((operand, earlier))


def collect(parts, partners, earlier=None):
    core, chip, _ = partners
    far = lax.ppermute(parts[3], "tp", core)
    near = lax.ppermute(parts[1], "tp", core)
    sent = rounded_sum(parts[2], far)
    if earlier is not None:
        sent, earlier = follow(sent, earlier)
    return [parts[0], near, lax.ppermute(sent, "tp", chip)], earlier


def take_rows(values, part, rows):
    return lax.dynamic_slice_in_dim(values, part * rows, rows, 0)


def rounded_sum(*parts):
    return sum(part.astype(F32) for part in parts).astype(BF)


def small_rows_body(first_a, first_b, middle_ref, out_ref):
    out_ref[...] = jnp.zeros_like(out_ref)
    out_ref[0:2, :] = first_a[0:2, :] + first_b[0:2, :]
    out_ref[2:11, :] = middle_ref[0:9, :]


def small_rows(first_a, first_b, middle):
    args = (first_a, first_b, middle)
    return call(small_rows_body, "small_rows", (1,), [whole(a) for a in args], whole(middle), shape_of(middle.shape, F32), args)


def last_rows_body(*refs):
    parts = [refs[n * len(PIECES) : (n + 1) * len(PIECES)] for n in range(3)]
    qkv_ref, bias_ref, s0, s1, s2, s3, out_ref = refs[3 * len(PIECES) :]
    heads = bias_ref.shape[2] // LANES
    local, width = parts[0][0].shape[1:]
    start, rows, count = 0, qkv_ref.shape[0], 16
    for own_ref, near_ref, far_ref in zip(*parts):
        for j in range(own_ref.shape[0]):
            total = own_ref[j].astype(F32) + near_ref[j].astype(F32) + far_ref[j].astype(F32)
            out_ref[start : start + local, :] = total.astype(BF)
            start += local
    out_ref[start : start + rows, :] = qkv_ref[...]
    start += rows
    parts = [bias_ref[j][:, h * LANES : h * LANES + HEAD_DIM] for j in range(3) for h in range(heads)]
    bias = jnp.concatenate(parts + [jnp.zeros((1, width - rows), F32)], 1)
    other = sum(ref[0:1, :] for ref in (s0, s1, s2, s3))
    row = lax.broadcasted_iota(jnp.int32, (count, width), 0)
    out_ref[start:, :] = jnp.where(row == 0, bias, jnp.where(row == 1, other, 0.0)).astype(BF)


def last_rows(own, near, far, qkv, bias, sums):
    width = qkv.shape[1]
    total = sum(part.shape[0] * part.shape[1] for part in own)
    args = (*own, *near, *far, qkv, bias, *sums)
    out = shape_of((total + qkv.shape[0] + 16, width), BF)
    return call(last_rows_body, "last_rows", (1,), [whole(a) for a in args], whole(out), out, args)


def widen_body(x_ref, cq_ref, so_ref, kv_ref, co_ref, qkv_ref, bqkv_ref, b1_ref):
    local, width = cq_ref.shape
    start = 0

    def take(count):
        nonlocal start
        start += count
        return x_ref[start - count : start, :].astype(F32)

    cq_ref[...] = take(local)
    so_ref[...] = take(local)
    for target in (kv_ref.at[0], kv_ref.at[1], co_ref, qkv_ref.at[0], qkv_ref.at[1], qkv_ref.at[2]):
        target[...] = take(local)
    tail = take(16)
    bqkv_ref[...] = jnp.concatenate([tail[0:1, j * local : (j + 1) * local] for j in range(3)], 0)
    b1_ref[...] = tail[1:2]


def widen(rows, local):
    width = rows.shape[1]
    shapes = [(local, width), (local, width), (2, local, width), (local, width), (3, local, width)]
    shapes += [(3, local), (1, width)]
    outs = [shape_of(shape, F32) for shape in shapes]
    return call(widen_body, "widen", (1,), [whole(rows)], [whole(o) for o in outs], outs, (rows,))


def finish_body(t_ref, own_ref, other_ref, gain_ref, shift_ref, out_ref, bq_ref, bv_ref):
    small = own_ref[...] + other_ref[...]
    local = bq_ref.shape[1]

    def pick(rows):
        return jnp.concatenate([small[row : row + 1] for row in rows], 0)

    def mine(row):
        cuts = [row[:, group * local : (group + 1) * local] for group in range(4)]
        return sum(jnp.where(t_ref[0] == group, cut, 0.0) for group, cut in enumerate(cuts))

    gain_ref[...] = pick((0, 2, 4))
    shift_ref[...] = pick((1, 3, 5))
    out_ref[...] = pick((6, 7, 8))
    bq_ref[...] = mine(small[9:10])
    bv_ref[...] = mine(small[10:11])


def finish(t, own, other, local):
    width = own.shape[1]
    outs = [shape_of(shape, F32) for shape in [(3, width)] * 3 + [(1, local)] * 2]
    args = (own, other)
    return call(finish_body, "finish", (1,), [whole(a) for a in args], [whole(o) for o in outs], outs, (t, *args), prefetch=1)


def widen_feed_body(x_ref, first_ref, second_ref):
    rows = first_ref.shape[0]
    first_ref[...] = x_ref[:rows, :].astype(F32)
    second_ref[...] = x_ref[rows:, :].astype(F32)


def widen_feed(rows, width):
    outs = [shape_of((width, width), F32), shape_of((rows.shape[0] - width, width), F32)]
    return call(widen_feed_body, "widen_feed", (1,), [whole(rows)], [whole(o) for o in outs], outs, (rows,))


def exchange(parts, partners):
    return [parts[0]] + [lax.ppermute(parts[r], "tp", partners[r - 1]) for r in (1, 2, 3)]


def gather_rows(t_ref, refs, target, start=0):
    @pl.when(pl.program_id(0) == 0)
    def _():
        for rel, ref in enumerate(refs):
            count = ref.shape[0]
            target[pl.ds(pl.multiple_of((t_ref[0] ^ rel) * count + start, 16), count), :] = ref[...]


def gather_bias(t_ref, refs, start, local):
    rows = [ref[...].astype(F32)[0:1] for ref in refs]
    rows = [row[:, start : start + local] + row[:, start + local : start + 2 * local] for row in rows]
    groups = []
    for group in range(4):
        groups.append(sum(jnp.where(t_ref[0] ^ rel == group, row, 0.0) for rel, row in enumerate(rows)))
    return jnp.concatenate(groups, 1)


def pack_rows(local, width, part):
    return [pl.BlockSpec((local, width), lambda i, *_: (part, 0))] * 4


def prepare_body(qkv_ref, cq_ref, so_ref, kv_ref, co_ref, bq_ref, bv_ref, w_ref, pack_ref):
    local, width = so_ref.shape
    zeros = jnp.zeros((LANES - HEAD_DIM, width), BF)
    for j in range(3 * local // HEAD_DIM):
        part = qkv_ref[j * HEAD_DIM // local, j * HEAD_DIM % local : j * HEAD_DIM % local + HEAD_DIM, :]
        w_ref[j * LANES : j * LANES + HEAD_DIM, :] = part
        w_ref[j * LANES + HEAD_DIM : (j + 1) * LANES, :] = zeros
    for index, part in enumerate((cq_ref[...], so_ref[...], kv_ref[0], kv_ref[1], co_ref[...])):
        pack_ref[index * local : (index + 1) * local, :] = part
    parts = []
    for ref in (bq_ref, bv_ref):
        high = ref[...].astype(BF).astype(F32)
        parts += [high, ref[...] - high]
    row = jnp.concatenate(parts, 1)
    count = pack_ref.shape[0] - 5 * local
    first = lax.broadcasted_iota(jnp.int32, (count, width), 0) == 0
    pack_ref[5 * local :, :] = jnp.where(first, row, 0.0).astype(BF)


def prepare(qkv, cq, so, kv, co, bq, bv, pack_size):
    local, width = so.shape
    outs = [shape_of((3 * local // HEAD_DIM * LANES, width), BF), shape_of((pack_size, width), BF)]
    args = (qkv, cq, so, kv, co, bq, bv)
    return call(prepare_body, "prepare", (1,), [whole(a) for a in args], [whole(o) for o in outs], outs, args)


def qkv_body(t_ref, xa, xb, gain_ref, shift_ref, w_ref, b_ref, ca, sa, ta, cb, sb, tb, aa, ab, oa, ob):
    heads = oa.shape[1]
    for x_ref, cos_ref, left_ref, right_ref, a_ref, out_ref in ((xa, ca, sa, ta, aa, oa), (xb, cb, sb, tb, ab, ob)):
        normed, _ = standardize(x_ref[...].astype(F32))
        a = (normed * gain_ref[0:1, :] + shift_ref[0:1, :]).astype(BF)
        a_ref[...] = a
        proj = nt(a, w_ref[...]) + b_ref[...]
        cos, left, right = cos_ref[...], left_ref[...], right_ref[...]
        for j in range(3 * heads):
            part = proj[:, j * LANES : (j + 1) * LANES]
            if j < 2 * heads:
                part = part * cos + pltpu.roll(part, 96, 1) * left + pltpu.roll(part, 32, 1) * right
            if j < heads:
                part = part * (1.0 / math.sqrt(HEAD_DIM))
            out_ref[j // heads, j % heads] = part.astype(BF)


def project_rows(rels, t, xs, gain, shift, w, b, tables, heads):
    rows, width = xs[0].shape
    tile = min(256, rows)
    steps = rows // tile

    def table(rel):
        return pl.BlockSpec((tile, LANES), lambda i, t_ref: ((t_ref[0] ^ rel) * steps + i, 0))

    row = rows_of(tile, width)
    out = pl.BlockSpec((3, heads, tile, LANES), lambda i, t_ref: (0, 0, i, 0))
    return call(
        qkv_body,
        f"qkv_{rels[0]}{rels[1]}",
        (steps,),
        [row, row, whole(gain), whole(shift), whole(w), whole(b)] + [table(rels[0])] * 3 + [table(rels[1])] * 3,
        [row, row, out, out],
        [shape_of((rows, width), BF)] * 2 + [shape_of((3, heads, rows, LANES), BF)] * 2,
        (t, *xs, gain, shift, w, b, *tables, *tables),
        prefetch=1,
    )


def causal_corner(scores):
    keys = lax.broadcasted_iota(jnp.int32, scores.shape, 0)
    queries = lax.broadcasted_iota(jnp.int32, scores.shape, 1)
    return jnp.where(keys <= queries, scores, NEGATIVE)


def attend_body(t_ref, c0, c1, c2, c3, qx_ref, kx_ref, vx_ref, qe_ref, ke_ref, ve_ref, ot_ref, lse_ref, vt_ref):
    t = t_ref[0]
    rows = c0.shape[2]
    for rel, chunk in enumerate((c0, c1, c2, c3)):
        place = pl.ds(pl.multiple_of((t ^ rel) * rows, rows), rows)
        qe_ref[0, place, :] = chunk[0, 0] + qx_ref[place, :]
        ke_ref[0, place, :] = chunk[1, 0] + kx_ref[place, :]
        values = chunk[2, 0] + vx_ref[...]
        ve_ref[0, place, :] = values
        vt_ref[:, place] = values.astype(F32).T.astype(BF)
    step = QUERY_ROWS
    for low in range(0, qe_ref.shape[1], step):
        high = low + step
        query = qe_ref[0, low:high, :]
        corner = causal_corner(nt(ke_ref[0, low:high, :], query))
        top = jnp.max(corner, 0, keepdims=True)
        if low:
            earlier = nt(ke_ref[0, :low, :], query)
            top = jnp.maximum(top, jnp.max(earlier, 0, keepdims=True))
        mixed = nn(vt_ref[:, low:high], jnp.exp(corner - top).astype(BF))
        if low:
            mixed = mixed + nn(vt_ref[:, :low], jnp.exp(earlier - top).astype(BF))
        total = mixed[HEAD_DIM : HEAD_DIM + 1, :]
        lse_ref[0, :, low:high] = top + jnp.log(total)
        begin = low % rows
        ot_ref[t ^ (low // rows), :, begin : begin + step] = (mixed[:HEAD_DIM] / total).astype(BF)


def attend(t, chunks, qx, kx, vx):
    _, heads, rows, _ = chunks[0].shape
    length = qx.shape[0]
    chunk = pl.BlockSpec((3, 1, rows, LANES), lambda h, t_ref: (0, h, 0, 0))
    plane = pl.BlockSpec((1, length, LANES), lambda h, t_ref: (h, 0, 0))
    padded = shape_of((heads, length, LANES), BF)
    return call(
        attend_body,
        "attend",
        (heads,),
        [chunk] * 4 + [whole(qx), whole(kx), whole(vx)],
        [
            plane,
            plane,
            plane,
            pl.BlockSpec((4, HEAD_DIM, rows), lambda h, t_ref: (0, h, 0)),
            pl.BlockSpec((1, 1, length), lambda h, t_ref: (h, 0, 0)),
        ],
        [padded, padded, padded, shape_of((4, heads * HEAD_DIM, rows), BF), shape_of((heads, 1, length), F32)],
        (t, *chunks, qx, kx, vx),
        scratch=[pltpu.VMEM((LANES, length), BF)],
        prefetch=1,
    )


def three_parts(values):
    first = values.astype(BF).astype(F32)
    second = (values - first).astype(BF).astype(F32)
    return first, second, values - first - second


def attend_back_body(
    t_ref, qe_ref, ke_ref, ve_ref, d0, d1, d2, d3, ot_ref, lse_ref, cos_ref, sa_ref, sb_ref, out_ref,
    qt_ref, kt_ref, dt_ref, dk_ref, dv_ref,
):
    t = t_ref[0]
    rows = d0.shape[1]
    step = QUERY_ROWS
    length = qe_ref.shape[1]
    for rel, chunk in enumerate((d0, d1, d2, d3)):
        place = pl.ds(pl.multiple_of((t ^ rel) * rows, rows), rows)
        grad = chunk[...].astype(F32)
        delta = three_parts(jnp.sum(grad * ot_ref[rel].astype(F32), 0, keepdims=True))
        padded = jnp.concatenate([grad, jnp.zeros_like(grad)], 0)
        row = lax.broadcasted_iota(jnp.int32, padded.shape, 0)
        for index in range(3):
            padded = jnp.where(row == HEAD_DIM + index, -delta[index], padded)
        dt_ref[:, place] = padded.astype(BF)
    for low in range(0, length, rows):
        high = low + rows
        kt_ref[:, low:high] = ke_ref[0, low:high, :].astype(F32).T.astype(BF)
        turned = qe_ref[0, low:high, :].astype(F32).T
        row = lax.broadcasted_iota(jnp.int32, turned.shape, 0)
        pieces = three_parts(lse_ref[0, :, low:high])
        for index in range(3):
            turned = jnp.where(row == LSE_LANE + index, -pieces[index], turned)
        qt_ref[:, low:high] = turned.astype(BF)
    dk_ref[...] = jnp.zeros_like(dk_ref)
    dv_ref[...] = jnp.zeros_like(dv_ref)

    def unrotate(grad, place):
        return (
            grad * cos_ref[place, :]
            - pltpu.roll(grad, 96, 1) * sa_ref[place, :]
            - pltpu.roll(grad, 32, 1) * sb_ref[place, :]
        )

    for low in range(0, length, step):
        high = low + step
        query, query_t, grad_t = qe_ref[0, low:high, :], qt_ref[:, low:high], dt_ref[:, low:high]
        dq_t = None
        for begin, end in ((0, low), (low, high)):
            if begin == end:
                continue
            scores = nn(ke_ref[0, begin:end, :], query_t)
            if begin == low:
                scores = causal_corner(scores)
            prob = jnp.exp(scores)
            grad_scores = (prob * nn(ve_ref[0, begin:end, :], grad_t)).astype(BF)
            dv_ref[begin:end, :] += nt(prob.astype(BF), grad_t)
            dk_ref[begin:end, :] += nn(grad_scores, query)
            part = nn(kt_ref[:, begin:end], grad_scores)
            dq_t = part if dq_t is None else dq_t + part
        start = low % rows
        grad_query = unrotate(dq_t.T, slice(low, high)) * (1.0 / math.sqrt(HEAD_DIM))
        out_ref[t ^ (low // rows), 0, 0, start : start + step, :] = grad_query.astype(BF)
    for low in range(0, length, rows):
        place = slice(low, low + rows)
        rel = t ^ (low // rows)
        out_ref[rel, 1, 0] = unrotate(dk_ref[place, :], place).astype(BF)
        lane = lax.broadcasted_iota(jnp.int32, (rows, LANES), 1)
        out_ref[rel, 2, 0] = jnp.where(lane < HEAD_DIM, dv_ref[place, :], 0.0).astype(BF)


def attend_back(t, qe, ke, ve, grads, ot, lse, tables):
    heads, length, _ = qe.shape
    rows = grads[0].shape[1]
    plane = pl.BlockSpec((1, length, LANES), lambda h, t_ref: (h, 0, 0))
    grad = pl.BlockSpec((HEAD_DIM, rows), lambda h, t_ref: (h, 0))
    return call(
        attend_back_body,
        "attend_back",
        (heads,),
        [plane] * 3
        + [grad] * 4
        + [
            pl.BlockSpec((4, HEAD_DIM, rows), lambda h, t_ref: (0, h, 0)),
            pl.BlockSpec((1, 1, length), lambda h, t_ref: (h, 0, 0)),
        ]
        + [whole(table) for table in tables],
        pl.BlockSpec((4, 3, 1, rows, LANES), lambda h, t_ref: (0, 0, h, 0, 0)),
        shape_of((4, 3, heads, rows, LANES), BF),
        (t, qe, ke, ve, *grads, ot, lse, *tables),
        scratch=[pltpu.VMEM((LANES, length), BF)] * 3 + [pltpu.VMEM((length, LANES), F32)] * 2,
        prefetch=1,
    )


def input_back_body(xa, xb, da, db, w_ref, oa, ob, small_ref):
    heads = da.shape[2]
    totals = []
    for x_ref, dp_ref, out_ref in ((xa, da, oa), (xb, db, ob)):
        grads = jnp.concatenate([dp_ref[0, j // heads, j % heads] for j in range(3 * heads)], 1)
        grad = nn(grads, w_ref[...])
        normed, _ = standardize(x_ref[...].astype(F32))
        out_ref[...] = grad.astype(BF)
        totals.append((column_sum(grad * normed), column_sum(grad)))
    add_rows(small_ref, [totals[0][0] + totals[1][0], totals[0][1] + totals[1][1]])


def input_back(rels, xs, dp, w):
    rows, width = xs[0].shape
    heads = dp.shape[2]
    tile = min(256, rows)
    row = rows_of(tile, width)

    def part(rel):
        return pl.BlockSpec((1, 3, heads, tile, LANES), lambda i: (rel, 0, 0, i, 0))

    return call(
        input_back_body,
        f"input_back_{rels[0]}{rels[1]}",
        (rows // tile,),
        [row, row, part(rels[0]), part(rels[1]), whole(w)],
        [row, row, pl.BlockSpec((8, width), lambda i: (0, 0))],
        [shape_of((rows, width), BF)] * 2 + [shape_of((8, width), F32)],
        (*xs, dp, dp, w),
    )


def qkv_weight_body(dp_ref, a0, a1, a2, a3, out_ref, bias_ref):
    heads = dp_ref.shape[2]
    total, sums = None, None
    for rel, a_ref in enumerate((a0, a1, a2, a3)):
        grads = jnp.concatenate([dp_ref[rel, 0, h] for h in range(heads)], 1)
        part, part_sum = tn(grads, a_ref[...]), column_sum(grads.astype(F32))
        total = part if total is None else total + part
        sums = part_sum if sums is None else sums + part_sum
    for h in range(heads):
        out_ref[h * HEAD_DIM : (h + 1) * HEAD_DIM, :] = total[h * LANES : h * LANES + HEAD_DIM].astype(BF)
    bias_ref[0] = sums


def qkv_weight(dp, normed):
    _, _, heads, rows, _ = dp.shape
    width = normed[0].shape[1]
    local = heads * HEAD_DIM
    return call(
        qkv_weight_body,
        "qkv_weight",
        (3,),
        [pl.BlockSpec((4, 1, heads, rows, LANES), lambda j: (0, j, 0, 0, 0))] + [whole(a) for a in normed],
        [rows_of(local, width), pl.BlockSpec((1, 1, heads * LANES), lambda j: (j, 0, 0))],
        [shape_of((3 * local, width), BF), shape_of((3, 1, heads * LANES), F32)],
        (dp, *normed),
    )


def after_attend_body(
    t_ref, x_ref, o0, o1, o2, o3, w0, w1, w2, w3, q0, q1, q2, q3, b0, b1, b2, b3, bias_ref, gain_ref, shift_ref,
    x1_ref, b_ref, cq_ref, wq_ref,
):
    gather_rows(t_ref, (q0, q1, q2, q3), wq_ref)
    total = x_ref[...].astype(F32) + bias_ref[0:1, :]
    for o_ref, w_ref in ((o0, w0), (o1, w1), (o2, w2), (o3, w3)):
        total = total + tn(o_ref[...], w_ref[...])
    x1_ref[...] = total
    normed, _ = standardize(total)
    b = (normed * gain_ref[1:2, :] + shift_ref[1:2, :]).astype(BF)
    b_ref[...] = b
    bias = gather_bias(t_ref, (b0, b1, b2, b3), 0, w0.shape[0])
    cq_ref[...] = ((nt(b, wq_ref[...]) + bias) * (1.0 / math.sqrt(HEAD_DIM))).astype(BF)


def after_attend(t, x, mixed, packs, out_bias, gain, shift):
    rows, width = x.shape
    local = mixed[0].shape[0]
    tile = min(256, rows)
    return call(
        after_attend_body,
        "after_attend",
        (rows // tile,),
        [rows_of(tile, width)]
        + [pl.BlockSpec((local, tile), lambda i, *_: (0, i))] * 4
        + pack_rows(local, width, 1)
        + pack_rows(local, width, 0)
        + pack_rows(16, width, 5 * local // 16)
        + [whole(out_bias), whole(gain), whole(shift)],
        [rows_of(tile, width)] * 3,
        [shape_of((rows, width), F32), shape_of((rows, width), BF), shape_of((rows, width), BF)],
        (t, x, *mixed, *packs, *packs, *packs, out_bias, gain, shift),
        scratch=[pltpu.VMEM((width, width), BF)],
        prefetch=1,
    )


def split_pair(values):
    lane = lax.broadcasted_iota(jnp.int32, values.shape, 1)
    zero = jnp.zeros_like(values)
    return jnp.concatenate(
        [jnp.where(lane < HEAD_DIM, values, zero), jnp.where(lane >= HEAD_DIM, values, zero)], 0
    )


def join_pair(values):
    rows = values.shape[0] // 2
    lane = lax.broadcasted_iota(jnp.int32, (rows, values.shape[1]), 1)
    return jnp.where(lane < HEAD_DIM, values[:rows], values[rows:])


def lane_cuts(width):
    return [slice(start, start + LANES) for start in range(0, width, LANES)]


def cross_body(
    t_ref, cq_ref, kv_ref, x1_ref, w0, w1, w2, w3, bias_ref, gain_ref, shift_ref, co_ref, lse_ref, x2_ref, m_ref, w_ref
):
    gather_rows(t_ref, (w0, w1, w2, w3), w_ref)
    width = cq_ref.shape[1]
    spans, side, _ = lse_ref.shape
    keys = kv_ref.shape[0] // spans
    cuts = lane_cuts(width)
    for span in range(spans):
        place = slice(span * SPAN, (span + 1) * SPAN)
        query = cq_ref[place, :]
        key, value = kv_ref[span * keys : (span + 1) * keys, :width], kv_ref[span * keys : (span + 1) * keys, width:]
        scores = [nt(key[:, cut], split_pair(query[:, cut])) for cut in cuts]
        tops = [jnp.max(score, 0, keepdims=True) for score in scores]
        shifted = [jnp.exp(score - top) for score, top in zip(scores, tops)]
        totals = [jnp.sum(part, 0, keepdims=True) for part in shifted]
        probs = [(part * (1.0 / total)).astype(BF) for part, total in zip(shifted, totals)]
        mixed = [join_pair(tn(prob, value[:, cut])) for prob, cut in zip(probs, cuts)]
        co_ref[place, :] = jnp.concatenate(mixed, 1).astype(BF)
        rows = [top + jnp.log(total) for top, total in zip(tops, totals)]
        lse_ref[span] = jnp.concatenate(rows + [jnp.zeros((side - len(rows), LANES), F32)], 0)
    total = x1_ref[...] + nn(co_ref[...], w_ref[...]) + bias_ref[1:2, :]
    x2_ref[...] = total
    normed, _ = standardize(total)
    m_ref[...] = (normed * gain_ref[2:3, :] + shift_ref[2:3, :]).astype(BF)


def cross(t, half, cq, kv, x1, packs, local, out_bias, gain, shift):
    rows, width = x1.shape
    tile = rows // 2
    ratio = kv.shape[0] // rows
    side = -(-(width // LANES) // 8) * 8
    spans = tile // SPAN

    def rows_at(count, columns):
        return pl.BlockSpec((count, columns), lambda i, *_: (half, 0))

    row = rows_at(tile, width)
    outs = [
        shape_of((tile, width), BF),
        shape_of((spans, side, LANES), F32),
        shape_of((tile, width), F32),
        shape_of((tile, width), BF),
    ]
    return call(
        cross_body,
        f"cross_{half}",
        (1,),
        [row, rows_at(ratio * tile, 2 * width), row]
        + pack_rows(local, width, 4)
        + [whole(out_bias), whole(gain), whole(shift)],
        [whole(out) for out in outs],
        outs,
        (t, cq, kv, x1, *packs, out_bias, gain, shift),
        scratch=[pltpu.VMEM((width, width), BF)],
        prefetch=1,
    )


def middle_back_body(
    t_ref, x2a, x2b, da0, da1, db0, db1, lsea, lseb, across_ref, g_ref, gain_ref, cq_ref, kv_ref, x1_ref,
    c0, c1, c2, c3, q0, q1, q2, q3, w0, w1, w2, w3,
    g2r_ref, dkv_ref, g1_ref, g1r_ref, dqc_ref, d0, d1, d2, d3, small_ref,
    dco_ref, dq_ref, x2_ref, dm_ref, lse_ref, co_w_ref, wq_ref,
):
    gather_rows(t_ref, (c0, c1, c2, c3), co_w_ref)
    gather_rows(t_ref, (q0, q1, q2, q3), wq_ref)
    for side, (x2, parts, lse) in enumerate(((x2a, (da0, da1), lsea), (x2b, (db0, db1), lseb))):

        @pl.when(pl.program_id(0) == side)
        def _(x2=x2, parts=parts, lse=lse):
            x2_ref[...] = x2[...]
            dm_ref[...] = sum(part[...].astype(F32) for part in parts) + across_ref[...].astype(F32)
            lse_ref[...] = lse[...]

    width = cq_ref.shape[1]
    spans = lse_ref.shape[0]
    keys = kv_ref.shape[0] // spans
    cuts = lane_cuts(width)
    grad_m = dm_ref[...]
    normed_m, inverse = standardize(x2_ref[...])
    g = g_ref[...]
    g2 = g + norm_pull(grad_m, normed_m, inverse, gain_ref[2:3, :])
    g2r = g2.astype(BF)
    g2r_ref[...] = g2r
    dco_ref[...] = nt(g2r, co_w_ref[...]).astype(BF)
    for span in range(spans):
        place = slice(span * SPAN, (span + 1) * SPAN)
        block = slice(span * keys, (span + 1) * keys)
        query, grad = cq_ref[place, :], dco_ref[place, :]
        key, value = kv_ref[block, :width], kv_ref[block, width:]
        stats = lse_ref[span]
        queries = [split_pair(query[:, cut]) for cut in cuts]
        grads = [split_pair(grad[:, cut]) for cut in cuts]
        probs = [jnp.exp(nt(key[:, cut], q) - stats[j : j + 1]) for j, (cut, q) in enumerate(zip(cuts, queries))]
        pulls = [nt(value[:, cut], part) for cut, part in zip(cuts, grads)]
        deltas = [jnp.sum(prob * pull, 0, keepdims=True) for prob, pull in zip(probs, pulls)]
        scores = [(prob * (pull - delta)).astype(BF) for prob, pull, delta in zip(probs, pulls, deltas)]
        keys_back = [nn(score, q).astype(BF) for score, q in zip(scores, queries)]
        values_back = [nn(prob.astype(BF), part).astype(BF) for prob, part in zip(probs, grads)]
        dkv_ref[block, :] = jnp.concatenate(keys_back + values_back, 1)
        dq_ref[place, :] = jnp.concatenate([join_pair(tn(score, key[:, cut])) for score, cut in zip(scores, cuts)], 1)
    dqc = (dq_ref[...] * (1.0 / math.sqrt(HEAD_DIM))).astype(BF)
    dqc_ref[...] = dqc
    grad_b = nn(dqc, wq_ref[...])
    normed_b, inverse = standardize(x1_ref[...])
    g1 = g2 + norm_pull(grad_b, normed_b, inverse, gain_ref[1:2, :])
    g1_ref[...] = g1
    g1r = g1.astype(BF)
    g1r_ref[...] = g1r
    for w_ref, d_ref in ((w0, d0), (w1, d1), (w2, d2), (w3, d3)):
        d_ref[...] = nt(w_ref[...], g1r).astype(BF)
    add_rows(
        small_ref,
        [
            column_sum(grad_b * normed_b),
            column_sum(grad_b),
            column_sum(grad_m * normed_m),
            column_sum(grad_m),
            column_sum(g1),
            column_sum(g2),
            column_sum(g),
            column_sum(dqc.astype(F32)),
            column_sum(dkv_ref[:, width:].astype(F32)),
        ],
    )


def middle_back(t, x2, dm, across, lse, g, packs, local, gain, cq, kv, x1):
    rows, width = x1.shape
    tile = rows // 2
    ratio = kv.shape[0] // rows
    row = rows_of(tile, width)
    wide = rows_of(ratio * tile, 2 * width)
    turned = pl.BlockSpec((local, tile), lambda i, *_: (0, i))
    half = shape_of((rows, width), BF)
    halves = (*x2, *dm[0], *dm[1], *lse)
    return call(
        middle_back_body,
        "middle_back",
        (2,),
        [whole(value) for value in halves]
        + [row, row, whole(gain), row, wide, row]
        + pack_rows(local, width, 4)
        + pack_rows(local, width, 0)
        + pack_rows(local, width, 1),
        [row, wide, row, row, row] + [turned] * 4 + [pl.BlockSpec((16, width), lambda i, *_: (0, 0))],
        [half, shape_of(kv.shape, BF), shape_of((rows, width), F32), half, half]
        + [shape_of((local, rows), BF)] * 4
        + [shape_of((16, width), F32)],
        (t, *halves, across, g, gain, cq, kv, x1, *packs, *packs, *packs),
        scratch=[
            pltpu.VMEM((tile, width), BF),
            pltpu.VMEM((tile, width), F32),
            pltpu.VMEM((tile, width), F32),
            pltpu.VMEM((tile, width), F32),
            pltpu.VMEM(lse[0].shape, F32),
            pltpu.VMEM((width, width), BF),
            pltpu.VMEM((width, width), BF),
        ],
        prefetch=1,
    )


def block_place(block, blocks, t, piece):
    rel, start, count = piece
    inside = block % blocks - start
    held = ((block // blocks) ^ t == rel) & (inside >= 0) & (inside < count)
    return held, jnp.where(held, inside, 0)


def anywhere():
    return pl.BlockSpec(memory_space=pl.ANY)


def fetch_block(t_ref, block, blocks, refs, pieces, target, semaphore):
    found = False
    for ref, piece in zip(refs, pieces):
        held, index = block_place(block, blocks, t_ref[0], piece)

        @pl.when(held)
        def _(ref=ref, index=index):
            pltpu.make_async_copy(ref.at[index], target, semaphore).start()

        found = held | found
    return found


def gather_pair(t_ref, refs, target):
    width = target.shape[1]
    local = refs[0].shape[0] // 2
    gather_rows(t_ref, [ref.at[:local, :] for ref in refs], target)
    gather_rows(t_ref, [ref.at[local:, :] for ref in refs], target, width)


def memory_body(t_ref, id_ref, *refs, pieces, first):
    count = len(pieces)
    packs, biases = refs[count : count + 4], refs[count + 4 : count + 8]
    kv_ref, chosen_ref, w_ref, x_ref, out_ref, in_sem, kv_sem, out_sem = refs[count + 8 + (0 if first else 2) :]
    blocks, length, width = x_ref.shape
    held = [
        fetch_block(t_ref, id_ref[slot], blocks, refs, pieces, x_ref.at[slot], in_sem.at[slot])
        for slot in range(blocks)
    ]
    gather_pair(t_ref, packs, w_ref)
    local = packs[0].shape[0] // 2
    bias = gather_bias(t_ref, biases, 2 * local, local)

    def copies(slot):
        rows = pl.ds(slot * length, length)
        return (
            pltpu.make_async_copy(out_ref.at[slot], kv_ref.at[rows, :], kv_sem.at[slot]),
            pltpu.make_async_copy(x_ref.at[slot], chosen_ref.at[rows, :], out_sem.at[slot]),
        )

    for slot in range(blocks):

        @pl.when(held[slot])
        def _(slot=slot):
            pltpu.make_async_copy(refs[0].at[0], x_ref.at[slot], in_sem.at[slot]).wait()
            kv = nt(x_ref[slot], w_ref[...])
            out_ref[slot, :, :width] = kv[:, :width].astype(BF)
            out_ref[slot, :, width:] = (kv[:, width:] + bias).astype(BF)
            for copy in copies(slot):
                copy.start()

    for slot in range(blocks):

        @pl.when(held[slot])
        def _(slot=slot):
            for copy in copies(slot):
                copy.wait()


def memory_rows(name, t, ids, memories, pieces, packs, local, earlier=None):
    blocks = ids.shape[0]
    _, length, width = memories[0].shape
    outs = [shape_of((blocks * length, 2 * width), BF), shape_of((blocks * length, width), BF)]
    more = () if earlier is None else tuple(earlier)
    count = 2 + len(memories) + 8
    return call(
        functools.partial(memory_body, pieces=pieces, first=earlier is None),
        name,
        (1,),
        [anywhere()] * len(memories)
        + pack_rows(2 * local, width, 1)
        + pack_rows(16, width, 5 * local // 16)
        + [anywhere()] * len(more),
        [anywhere()] * 2,
        outs,
        (t, ids, *memories, *packs, *packs, *more),
        scratch=[
            pltpu.VMEM((2 * width, width), BF),
            pltpu.VMEM((blocks, length, width), BF),
            pltpu.VMEM((blocks, length, 2 * width), BF),
            pltpu.SemaphoreType.DMA((blocks,)),
            pltpu.SemaphoreType.DMA((blocks,)),
            pltpu.SemaphoreType.DMA((blocks,)),
        ],
        prefetch=2,
        aliases={count: 0, count + 1: 1} if more else {},
    )


def block_grad_body(t_ref, dkv_ref, w0, w1, w2, w3, out_ref, w_ref):
    gather_pair(t_ref, (w0, w1, w2, w3), w_ref)
    out_ref[...] = nn(dkv_ref[...], w_ref[...]).astype(BF).reshape(out_ref.shape)


def block_grad(t, half, dkv, packs, local, blocks):
    rows, width = dkv.shape[0], dkv.shape[1] // 2
    length = rows // blocks
    steps = blocks // 4
    return call(
        block_grad_body,
        f"block_grad_{half}",
        (steps,),
        [pl.BlockSpec((2 * length, 2 * width), lambda i, *_: (half * steps + i, 0))] + pack_rows(2 * local, width, 1),
        pl.BlockSpec((2, length, width), lambda i, *_: (i, 0, 0)),
        shape_of((blocks // 2, length, width), BF),
        (t, dkv, *packs),
        scratch=[pltpu.VMEM((2 * width, width), BF)],
        prefetch=1,
    )


def return_body(t_ref, id_ref, *refs, pieces):
    out_ref, x_ref, semaphores = refs[len(pieces) :]
    blocks = id_ref.shape[0]
    step, steps = pl.program_id(0), pl.num_programs(0)
    sides = x_ref.shape[1]

    def fetch(at):
        for side in range(sides):
            slot = at % 2
            block = id_ref[at * sides + side]
            fetch_block(t_ref, block, blocks, refs, pieces, x_ref.at[slot, side], semaphores.at[slot, side])

    @pl.when(step == 0)
    def _():
        fetch(0)

    @pl.when(step + 1 < steps)
    def _():
        fetch(step + 1)

    now = step % 2
    for side in range(sides):
        pltpu.make_async_copy(refs[0].at[0], x_ref.at[now, side], semaphores.at[now, side]).wait()
        out_ref[side] = x_ref[now, side].astype(out_ref.dtype)


def return_blocks(t, slots, grads, pieces):
    blocks = slots.shape[0]
    sides = 4
    _, length, width = grads[0].shape
    return call(
        functools.partial(return_body, pieces=pieces),
        "return_blocks",
        (blocks // sides,),
        [anywhere()] * len(grads),
        pl.BlockSpec((sides, length, width), lambda i, *_: (i, 0, 0)),
        shape_of((blocks, length, width), F32),
        (t, slots, *grads),
        scratch=[pltpu.VMEM((2, sides, length, width), BF), pltpu.SemaphoreType.DMA((2, sides))],
        prefetch=2,
    )


def feed_body(ma, mb, ga, gb, w1_ref, w2_ref, b1_ref, oa, ob, da, db, ha, hb, ua, ub, sum_ref):
    curve = math.sqrt(2.0 / math.pi)
    total = None
    for m_ref, g_ref, out_ref, dm_ref, h_ref, du_ref in ((ma, ga, oa, da, ha, ua), (mb, gb, ob, db, hb, ub)):
        u = nn(m_ref[...], w1_ref[...]) + b1_ref[...]
        square = u * u
        bent = jnp.tanh(curve * (u + 0.044715 * u * square))
        half = 0.5 * (1.0 + bent)
        h = (u * half).astype(BF)
        h_ref[...] = h
        slope = half + 0.5 * u * (1.0 - bent * bent) * (curve * (1.0 + 3.0 * 0.044715 * square))
        du = (nt(g_ref[...], w2_ref[...]) * slope).astype(BF)
        du_ref[...] = du
        dm_ref[...] = nt(du, w1_ref[...]).astype(BF)
        out_ref[...] = nn(h, w2_ref[...]).astype(BF)
        part = column_sum(du.astype(F32))
        total = part if total is None else total + part
    add_rows(sum_ref, [total])


def feed(name, half, ms, gs, w1, w2, b1):
    rows, width = ms[0].shape
    hidden = w1.shape[1]
    row, wide = shape_of((rows, width), BF), shape_of((rows, hidden), BF)
    outs = [row] * 4 + [wide] * 4 + [shape_of((8, hidden), F32)]
    return list(call(
        feed_body,
        name,
        (1,),
        [whole(row)] * 2 + [pl.BlockSpec((rows, width), lambda i: (half, 0))] * 2 + [whole(w1), whole(w2), whole(b1)],
        [whole(out) for out in outs],
        outs,
        (*ms, *gs, w1, w2, b1),
    ))


def feed_weight_body(*refs):
    out_ref = refs[-1]
    count = (len(refs) - 1) // 7
    ms, dus, hs, gs = refs[: 2 * count], refs[2 * count : 4 * count], refs[4 * count : 6 * count], refs[6 * count : -1]
    rows = dus[0].shape[0]
    half = pl.num_programs(0) // 2

    @pl.when(pl.program_id(0) < half)
    def _():
        out_ref[...] = sum(tn(m[...], du[...]) for m, du in zip(ms, dus)).astype(BF)

    @pl.when(pl.program_id(0) >= half)
    def _():
        total = 0.0
        for index, h in enumerate(hs):
            side = index % 2
            total = total + tn(h[...], gs[index // 2][side * rows : (side + 1) * rows, :])
        out_ref[...] = total.astype(BF)


def feed_weight(ms, dus, hs, gs):
    rows, width = ms[0].shape
    hidden = hs[0].shape[1]
    tile = 256
    first, second = width // tile, hidden // tile
    return call(
        feed_weight_body,
        "feed_weight",
        (first + second,),
        [pl.BlockSpec((rows, tile), lambda i: (0, jnp.minimum(i, first - 1)))] * len(ms)
        + [whole(r) for r in dus]
        + [pl.BlockSpec((rows, tile), lambda i: (0, jnp.maximum(i - first, 0)))] * len(hs)
        + [whole(r) for r in gs],
        rows_of(tile, width),
        shape_of((width + hidden, width), BF),
        (*ms, *dus, *hs, *gs),
    )


def cross_weight_body(t_ref, *refs):
    pieces = len(PIECES)
    count = (len(refs) - 1 - 4 * pieces) // 2
    sources, buffers, semaphores = refs[:count], refs[count + 4 * pieces : -1], refs[-1]
    outs = [refs[count + rel * pieces : count + (rel + 1) * pieces] for rel in range(4)]
    local, width = outs[0][0].shape[1:]
    copies = [
        pltpu.make_async_copy(source, buffer, semaphores.at[index])
        for index, (source, buffer) in enumerate(zip(sources, buffers))
    ]
    for copy in copies:
        copy.start()
    dqc, b, o0, o1, o2, o3, g1, co_a, co_b, g2, memory, dkv = buffers

    def store(rel, index, part):
        for out_ref, (start, end) in zip(outs[rel], PIECES):
            if start <= index < end:
                out_ref[index - start] = part

    def place(index, grad):
        for group in range(4):
            part = grad[group * local : (group + 1) * local].astype(BF)
            for rel in range(4):

                @pl.when(t_ref[0] ^ rel == group)
                def _(rel=rel, part=part):
                    store(rel, index, part)

    copies[0].wait()
    copies[1].wait()
    place(0, tn(dqc[...], b[...]))
    for copy in copies[2:7]:
        copy.wait()
    for rel, o_ref in enumerate((o0, o1, o2, o3)):
        store(rel, 1, nn(o_ref[...], g1[...]).astype(BF))
    for copy in copies[7:10]:
        copy.wait()
    half = co_a.shape[0]
    place(4, tn(co_a[...], g2[:half, :]) + tn(co_b[...], g2[half:, :]))
    copies[10].wait()
    copies[11].wait()
    place(2, tn(dkv[:, :width], memory[...]))
    place(3, tn(dkv[:, width:], memory[...]))


def cross_weight(t, dqc, b, mixed, g1r, dkv, memory, co, g2r):
    width = b.shape[1]
    local = mixed[0].shape[0]
    args = (dqc, b, *mixed, g1r, *co, g2r, memory, dkv)
    outs = [shape_of((end - start, local, width), BF) for start, end in PIECES] * 4
    flat = call(
        cross_weight_body,
        "cross_weight",
        (1,),
        [anywhere()] * len(args),
        [whole(out) for out in outs],
        outs,
        (t, *args),
        scratch=[pltpu.VMEM(a.shape, a.dtype) for a in args] + [pltpu.SemaphoreType.DMA((len(args),))],
        prefetch=1,
    )
    return [tuple(flat[rel * len(PIECES) : (rel + 1) * len(PIECES)]) for rel in range(4)]


def input_grad_body(x_ref, da_ref, db_ref, dc_ref, g1_ref, gain_ref, out_ref):
    normed, inverse = standardize(x_ref[...].astype(F32))
    grad = da_ref[...].astype(F32) + db_ref[...].astype(F32) + dc_ref[...].astype(F32)
    out_ref[...] = g1_ref[...] + norm_pull(grad, normed, inverse, gain_ref[0:1, :])


def input_grad(x, parts, g1, gain):
    rows, width = x.shape
    tile = min(256, rows)
    row = rows_of(tile, width)
    return call(
        input_grad_body,
        "input_grad",
        (rows // tile,),
        [row] * 5 + [whole(gain)],
        row,
        shape_of((rows, width), F32),
        (x, *parts, g1, gain),
    )


def padded_tables(length):
    half = HEAD_DIM // 2
    frequency = np.float32(10000.0) ** (-np.arange(half, dtype=np.float32) / np.float32(half))
    angles = np.arange(length, dtype=np.float32)[:, None] * frequency[None, :]
    cosine = np.cos(angles.astype(np.float64)).astype(np.float32)
    sine = np.sin(angles.astype(np.float64)).astype(np.float32)
    zero = np.zeros_like(sine)
    return (
        jnp.asarray(np.concatenate([cosine, cosine, zero, zero], 1)),
        jnp.asarray(np.concatenate([-sine, zero, zero, zero], 1)),
        jnp.asarray(np.concatenate([zero, sine, zero, zero], 1)),
    )


def mask_lanes(segments):
    lane = lax.broadcasted_iota(jnp.int32, (segments.shape[0], LANES), 1)
    is_mask = (lane >= MASK_LANE) & (lane < MASK_LANE + DOCS)
    same = is_mask & (lane - MASK_LANE == segments[:, None])
    is_lse = (lane >= LSE_LANE) & (lane < LSE_LANE + 3)
    query_lanes = jnp.where(same, 1.0, 0.0).astype(BF)
    key_lanes = jnp.where(is_mask & ~same, NEGATIVE, jnp.where(is_lse, 1.0, 0.0)).astype(BF)
    return query_lanes, key_lanes


def pad_heads(values):
    lead = values.shape[:-1]
    heads = values.shape[-1] // HEAD_DIM
    values = values.reshape(lead + (heads, HEAD_DIM))
    values = jnp.pad(values, [(0, 0)] * (len(lead) + 1) + [(0, LANES - HEAD_DIM)])
    return values.reshape(lead[:-1] + (-1,))


def shards(
    layer_input,
    norm_gain,
    norm_bias,
    self_input_weight,
    self_input_bias,
    self_output_weight,
    out_bias,
    cross_query_weight,
    b_cross_q,
    w_cross_kv,
    b_cross_v,
    cross_output_weight,
    expand_weight_1,
    expand_bias_1,
    contract_weight_2,
    neighbours,
    segment_ids,
    span_map,
    cotangent,
):
    x = layer_input[0]
    rows, width = x.shape
    length = segment_ids.shape[1]
    local = self_input_weight.shape[2]
    heads = local // HEAD_DIM
    blocks, block_rows = neighbours.shape[1], neighbours.shape[2]
    grad_out = cotangent[0]
    index = lax.axis_index("tp")
    t = index.astype(jnp.int32).reshape(1)
    partners = [[(i, i ^ step) for i in range(4)] for step in (1, 2, 3)]

    tables = padded_tables(length)
    b_pad = pad_heads(self_input_bias)[None]
    piece = -(-(5 * local + 16) // (16 * lax.axis_size("dp"))) * 16
    w_pad, pack = prepare(
        self_input_weight.transpose(1, 2, 0),
        cross_query_weight.T,
        self_output_weight,
        w_cross_kv.transpose(1, 2, 0),
        cross_output_weight,
        b_cross_q[None],
        b_cross_v[None],
        piece * lax.axis_size("dp"),
    )
    qx, kx = mask_lanes(segment_ids[0])
    lane = lax.broadcasted_iota(jnp.int32, (1, LANES), 1)
    vx = jnp.where((lane >= HEAD_DIM) & (lane < HEAD_DIM + 3), 1.0, 0.0).astype(BF)
    core, chip, _ = partners

    half = blocks // 2

    across = lax.ppermute(x, "tp", chip)
    beside = lax.ppermute(x, "tp", core)
    a0, a1, c0, c1 = project_rows((0, 1), t, (x, beside), norm_gain, norm_bias, w_pad, b_pad, tables, heads)
    across, c0 = lax.optimization_barrier((across, c0))
    pack_piece, blocks_first, across = lax.optimization_barrier(
        (take_rows(pack, lax.axis_index("dp"), piece), neighbours[0][:half], across)
    )
    pack_piece = lax.ppermute(pack_piece, "tp", chip)
    blocks_first = lax.ppermute(blocks_first, "tp", chip)
    pack_across = lax.all_gather(pack_piece, "dp", axis=0, tiled=True)
    pack_beside = lax.ppermute(pack, "tp", core)
    xs = [x, beside, across, lax.ppermute(across, "tp", core)]
    blocks_beside = lax.ppermute(neighbours[0], "tp", core)
    a2, a3, c2, c3 = project_rows((2, 3), t, xs[2:], norm_gain, norm_bias, w_pad, b_pad, tables, heads)
    qe, ke, ve, ot, lse = attend(t, (c0, c1, c2, c3), qx, kx, vx)
    normed_first = [a0, a1, a2, a3]
    ot, blocks_first = follow(ot, blocks_first)
    mixed = exchange([ot[0], ot[1], ot[2], ot[3]], partners)
    blocks_second, mixed = follow(neighbours[0][half:], tuple(mixed))
    blocks_second = lax.ppermute(blocks_second, "tp", chip)
    packs = [pack, pack_beside, pack_across, lax.ppermute(pack_across, "tp", core)]

    block_ids = index * blocks + jnp.arange(blocks, dtype=jnp.int32)
    slot_ids = jnp.arange(span_map.shape[1], dtype=jnp.int32)
    slots = jnp.sum(jnp.where(span_map[0][None, :] == block_ids[:, None], slot_ids[None, :], 0), 1)
    chosen_ids = lax.dynamic_slice_in_dim(span_map[0], index * blocks, blocks, 0)

    x1, b, cq = after_attend(t, x, mixed, packs, out_bias, norm_gain, norm_bias)
    memories = [neighbours[0], blocks_beside, blocks_first, lax.ppermute(blocks_first, "tp", core)]
    pieces = [(0, 0, blocks), (1, 0, blocks), (2, 0, half), (3, 0, half)]
    memory_near = memory_rows("memory_near", t, chosen_ids, memories, pieces, packs, local)
    gathered, blocks_second, cq, memory_near = lax.optimization_barrier(
        (grad_out.astype(BF), blocks_second, cq, tuple(memory_near))
    )
    memories = [blocks_second, lax.ppermute(blocks_second, "tp", core)]
    pieces = [(2, half, half), (3, half, half)]
    grad_across = lax.ppermute(gathered, "tp", chip)
    grad_beside = lax.ppermute(gathered, "tp", core)
    kv, memory = memory_rows("memory_far", t, chosen_ids, memories, pieces, packs, local, memory_near)
    cross_args = (packs, local, out_bias, norm_gain, norm_bias)
    co_a, cross_lse_a, x2_a, m_a = cross(t, 0, cq, kv, x1, *cross_args)
    x1_late, m_a = lax.optimization_barrier((x1, m_a))
    co_b, cross_lse_b, x2_b, m_b = cross(t, 1, cq, kv, x1_late, *cross_args)

    feed_args = (expand_weight_1, contract_weight_2, expand_bias_1[None])
    m_a, grad_across = follow(m_a, grad_across)
    across_a = lax.ppermute(m_a, "tp", chip)
    beside_a = lax.ppermute(m_a, "tp", core)
    gs = [gathered, grad_beside, grad_across, lax.ppermute(grad_across, "tp", core)]
    near_a = feed("feed_near_0", 0, (m_a, beside_a), gs[:2], *feed_args)
    across_b = lax.ppermute(m_b, "tp", chip)
    beside_b = lax.ppermute(m_b, "tp", core)
    across_a, near_a[0] = lax.optimization_barrier((across_a, near_a[0]))
    diagonal_a = lax.ppermute(across_a, "tp", core)
    near_b = feed("feed_near_1", 1, (m_b, beside_b), gs[:2], *feed_args)
    diagonal_a, across_b, near_b[0] = lax.optimization_barrier((diagonal_a, across_b, near_b[0]))
    diagonal_b = lax.ppermute(across_b, "tp", core)
    far_a = feed("feed_far_0", 0, (across_a, diagonal_a), gs[2:], *feed_args)
    diagonal_b, far_a[0] = lax.optimization_barrier((diagonal_b, far_a[0]))
    far_b = feed("feed_far_1", 1, (across_b, diagonal_b), gs[2:], *feed_args)
    dm_far = [lax.ppermute(part[3], "tp", core) for part in (far_a, far_b)]
    sent = jnp.concatenate([rounded_sum(far_a[2], dm_far[0]), rounded_sum(far_b[2], dm_far[1])], 0)
    dm_across = lax.ppermute(sent, "tp", chip)
    dm_a, dm_b = [(part[2], lax.ppermute(part[3], "tp", core)) for part in (near_a, near_b)]
    ms = [m_a, m_b, beside_a, beside_b, across_a, across_b, diagonal_a, diagonal_b]
    ordered = [(near_a, 0), (near_b, 0), (near_a, 1), (near_b, 1), (far_a, 0), (far_b, 0), (far_a, 1), (far_b, 1)]
    grad_feed = feed_weight(ms, [f[6 + i] for f, i in ordered], [f[4 + i] for f, i in ordered], gs)

    out_far = [lax.ppermute(part[1], "tp", core) for part in (far_a, far_b, near_a, near_b)]
    out_sent = (rounded_sum(far_a[0], out_far[0]), rounded_sum(far_b[0], out_far[1]))
    dm_across, grad_feed = lax.optimization_barrier((dm_across, grad_feed))
    summed_feed = lax.psum(grad_feed, "dp")
    g2r, dkv, g1, g1r, dqc, *dos, small_middle = middle_back(
        t, (x2_a, x2_b), (dm_a, dm_b), dm_across, (cross_lse_a, cross_lse_b), grad_out, packs, local, norm_gain, cq, kv, x1
    )

    dos = exchange(dos, partners)
    dos[1], g1r = lax.optimization_barrier((dos[1], g1r))
    grad_cross = cross_weight(t, dqc, b, mixed, g1r, dkv, memory, (co_a, co_b), g2r)
    dos[2], dos[3], grad_cross, out_sent = lax.optimization_barrier((dos[2], dos[3], tuple(grad_cross), out_sent))
    out_across = tuple(lax.ppermute(part, "tp", chip) for part in out_sent)
    grad_far = [tuple(lax.ppermute(part, "tp", core) for part in grad_cross[r]) for r in (3, 1)]
    dp = attend_back(t, qe, ke, ve, dos, ot, lse, tables)
    dp, grad_far[0], out_across = lax.optimization_barrier((dp, grad_far[0], out_across))
    across = tuple(lax.ppermute(rounded_sum(a, b), "tp", chip) for a, b in zip(grad_cross[2], grad_far[0]))
    grad_qkv, grad_bqkv = qkv_weight(dp, normed_first)
    da3, da1, small_a = input_back((3, 1), (xs[3], xs[1]), dp, w_pad)
    da2, da0, small_b = input_back((2, 0), (xs[2], xs[0]), dp, w_pad)
    dkv, small_a, small_b = lax.optimization_barrier((dkv, small_a, small_b))
    grad_near = [block_grad(t, side, dkv, packs, local, blocks) for side in range(2)]
    sums = (near_a[8], near_b[8], far_a[8], far_b[8])
    last = last_rows(grad_cross[0], grad_far[1], across, grad_qkv, grad_bqkv, sums)
    da0, da1, da2, da3, last, grad_near, small_a, small_b, summed_feed = lax.optimization_barrier(
        (da0, da1, da2, da3, last, tuple(grad_near), small_a, small_b, summed_feed)
    )

    last = lax.psum(last, "dp")
    blocks_far = [lax.ppermute(value, "tp", chip) for value in grad_near]
    da, _ = collect([da0, da1, da2, da3], partners)
    small = small_rows(small_a, small_b, small_middle)
    small = small + lax.ppermute(small, "tp", core)
    small = small + lax.ppermute(small, "tp", chip)
    step, replicas = 1, lax.axis_size("dp")
    while 2 * step < replicas:
        small = small + lax.ppermute(small, "dp", [(i, i ^ step) for i in range(replicas)])
        step *= 2
    other = lax.ppermute(small, "dp", [(i, i ^ step) for i in range(replicas)]) if replicas > 1 else jnp.zeros_like(small)
    gains, shifts, biases, bq, bv = finish(t, small, other, local)
    returned = [*grad_near] + [lax.ppermute(value, "tp", core) for value in grad_near]
    returned += blocks_far + [lax.ppermute(value, "tp", core) for value in blocks_far]
    halves = [(rel, start, half) for rel in range(4) for start in (0, half)]
    grad_memory = return_blocks(t, slots, returned, halves)
    grad_input = input_grad(x, da, g1, norm_gain)
    kept = jnp.concatenate([rounded_sum(near_a[0], out_far[2]), rounded_sum(near_b[0], out_far[3])], 0)
    layer_output = jnp.concatenate([x2_a, x2_b], 0) + kept.astype(F32) + jnp.concatenate(out_across, 0).astype(F32) + out_bias[2]

    grad_w1, grad_w2 = widen_feed(summed_feed, width)
    last, grad_memory, grad_input, layer_output, grad_w1, grad_w2, gains = lax.optimization_barrier(
        (last, grad_memory, grad_input, layer_output, grad_w1, grad_w2, gains)
    )
    cq_t, grad_so, kv_t, grad_co, qkv_t, bqkv, b1 = widen(last, local)

    return (
        layer_output[None],
        grad_input[None],
        grad_memory[None],
        gains,
        shifts,
        qkv_t.transpose(2, 0, 1),
        bqkv,
        grad_so,
        biases,
        cq_t.T,
        bq[0],
        kv_t.transpose(2, 0, 1),
        bv[0],
        grad_co,
        grad_w1,
        b1[0],
        grad_w2,
    )


def solution(mesh):
    return jax.shard_map(
        shards,
        mesh=mesh,
        in_specs=(
            P("dp", "tp", None),
            P(),
            P(),
            P(None, None, "tp"),
            P(None, "tp"),
            P("tp", None),
            P(),
            P(None, "tp"),
            P("tp"),
            P(None, None, "tp"),
            P("tp"),
            P("tp", None),
            P(None, "tp"),
            P("tp"),
            P("tp", None),
            P("dp", "tp", None, None),
            P("dp", None),
            P("dp", None),
            P("dp", "tp", None),
        ),
        out_specs=(
            P("dp", "tp", None),
            P("dp", "tp", None),
            P("dp", "tp", None, None),
            P(),
            P(),
            P(None, None, "tp"),
            P(None, "tp"),
            P("tp", None),
            P(),
            P(None, "tp"),
            P("tp"),
            P(None, None, "tp"),
            P("tp"),
            P("tp", None),
            P(None, "tp"),
            P("tp"),
            P("tp", None),
        ),
        check_vma=False,
    )
```
